256 devices in a mesh: gx: 32 (over y, z), gz: 8 (over x, core).
Axes of the slice: x: 4, y: 4, z: 8, core: 2. Of those that a mesh axis runs over, the one named last changes fastest.
Arguments:
- charge: float32 [64, 1024, 1024], P('gz', 'gx'), may hold values from -24 to 24
- cell_permittivity: float32 [64], replicated, may hold values from 1 to 4
- face_permittivity: float32 [64], replicated, may hold values from 1 to 4
- screening: float32 [64], replicated, may hold values from 0.001 to 0.01
Outputs:
- potential: float32 [64, 1024, 1024], P('gz', 'gx')
The draws below stay inside these ranges and needn't reach their ends.
All inputs are finite; a program needn't handle non-finite values.
Results may differ from the reference program's by a relative error of at most 0.0003.
Values sent between devices are 32-bit elements; how exact they have to be, the bound alone decides.
No kernel may reach another device: no remote copies, remote signals or barrier semaphores. Data moves between devices by JAX's collectives and lax.ppermute only.
A program may use at most 128 MiB of HBM per device.

```python
import math
import jax
import jax.numpy as jnp
from jax import lax

NX = 1024
NY = 1024
NZ = 64


def block_scale(rng, shape, cuts, smallest, top_value):
    def one(dim, parts):
        steps = jax.random.uniform(jax.random.fold_in(jax.random.fold_in(rng, 6), dim), (parts,), jnp.float32, smallest / len(cuts), top_value / len(cuts))
        return jnp.repeat(jnp.exp(steps), shape[dim] // parts).reshape((-1,) + (1,) * (len(shape) - dim - 1))

    loudness = one(*cuts[0])
    for cut in cuts[1:]:
        loudness = loudness * one(*cut)
    return loudness


def normal_values(stream_key, shape, deviation, reach, split=(), held_as=jnp.bfloat16):
    array = jax.random.normal(stream_key, shape, jnp.float32) * deviation
    if len(split) > 0:
        array = block_scale(stream_key, shape, split, -0.22, 0.18) * array
    return jnp.clip(array, min=-reach, max=reach).astype(held_as)


def setup_inputs(seed: int = 0) -> dict:
    streams_of = jax.random.split(jax.random.key(seed), 5)
    return {
        "charge": normal_values(streams_of[0], (NZ, NX, NY), 4.0, 24.0, ((0, 8), (1, 32)), jnp.float32),
        "cell_permittivity": jnp.clip(jnp.exp(jax.random.uniform(streams_of[1], (NZ,), jnp.float32, math.log(1.0), math.log(4.0))), 1.0, 4.0),
        "face_permittivity": jnp.clip(jnp.exp(jax.random.uniform(streams_of[2], (NZ,), jnp.float32, math.log(1.0), math.log(4.0))), 1.0, 4.0),
        "screening": jnp.clip(jnp.exp(jax.random.uniform(streams_of[3], (NZ,), jnp.float32, math.log(0.001), math.log(0.01))), 0.001, 0.01),
    }


def mode_shift(count, length):
    frequency = jnp.arange(count, dtype=jnp.int32)
    angles = frequency.astype(jnp.float32) * (2.0 * math.pi / length)
    return 2.0 - 2.0 * jnp.cos(angles)


def reference(charge, cell_permittivity, face_permittivity, screening):
    layers = charge.shape[0]
    spectrum = jnp.fft.rfft2(charge, axes=(1, 2))
    half_width = NY // 2 + 1
    shifts = mode_shift(NX, NX)[:, None] + mode_shift(half_width, NY)[None, :]
    stacked = jnp.stack([jnp.real(spectrum), jnp.imag(spectrum)], axis=1).astype(jnp.float32)
    face_below = jnp.roll(face_permittivity, 1)
    layer_index = jnp.arange(layers, dtype=jnp.int32)
    sub_coef = jnp.where(layer_index > 0, -face_below, 0.0)
    sup_coef = jnp.where(layer_index < layers - 1, -face_permittivity, 0.0)

    def forward(carry, item):
        ratio_prev, part_prev = carry
        sub_one, sup_one, low_one, up_one, cell_one, scr_one, plane = item
        pivot = low_one + up_one + cell_one * shifts + scr_one - sub_one * ratio_prev
        ratio_next = sup_one / pivot
        part_next = (plane - sub_one * part_prev) / pivot[None]
        return (ratio_next, part_next), (ratio_next, part_next)

    start_carry = (jnp.zeros(shifts.shape, jnp.float32), jnp.zeros(stacked.shape[1:], jnp.float32))
    _, (ratios, partial_values) = lax.scan(forward, start_carry, (sub_coef, sup_coef, face_below, face_permittivity, cell_permittivity, screening, stacked))

    def backward(later, item):
        ratio_one, part_one = item
        value = part_one - ratio_one[None] * later
        return value, value

    _, solved = lax.scan(backward, jnp.zeros(stacked.shape[1:], jnp.float32), (ratios, partial_values), reverse=True)
    complex_field = lax.complex(solved[:, 0], solved[:, 1])
    potential = jnp.fft.irfft2(complex_field, s=(NX, NY), axes=(1, 2))
    return potential.astype(jnp.float32)
```

```python
import functools
import math

import jax
import jax.numpy as jnp
import ml_dtypes
import numpy as np
from jax import lax
from jax.experimental import pallas as pl
from jax.experimental.pallas import tpu as pltpu
from jax.sharding import PartitionSpec as P

NX, NY, NZ = 1024, 1024, 64
SLABS, PLANES = 32, 32
HALF = NY // 2
CHIPS = 4
LAYERS = NZ // CHIPS
LANES = 128
highest = lax.Precision.HIGHEST
VMEM_LIMIT = 48 * 1024 * 1024


def split_pair(table):
    high = table.astype(np.float32).astype(ml_dtypes.bfloat16)
    low = (table - high.astype(np.float64)).astype(np.float32).astype(ml_dtypes.bfloat16)
    return high, low


def y_frequencies():
    index = np.arange(HALF)
    even = np.where(index <= HALF // 2, 2 * index, 2 * (index - HALF // 2))
    odd = np.where(index < HALF // 2, 2 * index + 1, 2 * (index - HALF // 2) + 1)
    even_is_cos = index <= HALF // 2
    odd_is_cos = index < HALF // 2
    return np.stack([even, odd]), np.stack([even_is_cos, odd_is_cos])


def y_tables():
    freq, is_cos = y_frequencies()
    point = np.arange(HALF)
    angle = 2.0 * np.pi * (point[None, :, None] * freq[:, None, :] % NY) / NY
    forward = np.where(is_cos[:, None, :], np.cos(angle), np.sin(angle))
    weight = np.where((freq == 0) | (freq == NY // 2), 1.0 / NY, 2.0 / NY)
    backward = np.swapaxes(forward * weight[:, None, :], 1, 2)
    return forward, backward


def y_shifts():
    freq, _ = y_frequencies()
    shift = 4.0 * np.sin(np.pi * freq / NY) ** 2
    return shift.reshape(2, CHIPS, LANES).transpose(1, 0, 2).reshape(2 * CHIPS, LANES)


def slab_basis():
    index = np.arange(PLANES)
    basis = math.sqrt(2.0 / PLANES) * np.sin(np.pi * np.outer(index, index) / PLANES)
    basis[0, :] = 0.0
    basis[:, 0] = 0.0
    basis[0, 0] = 1.0
    return basis


def interface_tables():
    mode = np.arange(SLABS)
    freq = np.where(mode <= SLABS // 2, mode, mode - SLABS // 2)
    is_cos = mode <= SLABS // 2
    weight = np.where((freq == 0) | (freq == SLABS // 2), 1.0, 2.0) / SLABS / SLABS

    def basis(offset):
        angle = 2.0 * np.pi * ((np.arange(SLABS)[:, None] + offset) * freq[None, :] % SLABS) / SLABS
        return np.where(is_cos[None, :], np.cos(angle), np.sin(angle))

    forward = np.zeros((2, 4, SLABS, LANES), np.float32)
    backward = np.zeros((2, 4, SLABS, LANES), np.float32)
    for which in range(2):
        for part in range(4):
            forward[which, part, :, part * SLABS : (part + 1) * SLABS] = basis(which)
            backward[which, part, :, part * SLABS : (part + 1) * SLABS] = basis(which) * weight[None, :]
    alias = freq[None, :] + SLABS * np.arange(SLABS)[:, None]
    alias_shift = 4.0 * np.sin(np.pi * alias / NX) ** 2
    return forward, backward, np.tile(alias_shift, (1, 4)).astype(np.float32)


def fold_tables():
    own = np.zeros((NZ, 8, 2 * NZ), np.float32)
    far = np.zeros((NZ, 8, 2 * NZ), np.float32)
    for layer in range(NZ):
        own[layer, :, layer] = 1.0
        far[layer, :, NZ + layer] = np.where(np.arange(8) % 2 == 1, 1.0, -1.0)
    return own.reshape(8 * NZ, 2 * NZ), far.reshape(8 * NZ, 2 * NZ)


def near_weights():
    weight = slab_basis()[1].copy()
    weight[0] = 0.0
    return np.broadcast_to(weight[:, None], (PLANES, LANES)).astype(np.float32)


def split_values(values):
    high = values.astype(jnp.bfloat16)
    low = (values - high.astype(jnp.float32)).astype(jnp.bfloat16)
    return high, low


def dot_split(left, right):
    left_high, left_low = left
    right_high, right_low = right
    dot = functools.partial(jnp.dot, preferred_element_type=jnp.float32)
    return dot(left_high, right_high) + (dot(left_high, right_low) + dot(left_low, right_high))


def dot_full(left, right, contract):
    return lax.dot_general(
        left, right, (contract, ((), ())), precision=highest, preferred_element_type=jnp.float32
    )


def forward_kernel(place, own, other, table_high, table_low, slab_high, slab_low, out0, out1, out2, out3, modes):
    core, chip = place[0], place[1]
    rows = 8 * PLANES
    own_rows = own[...].reshape(rows, HALF)
    other_rows = other[...].reshape(rows, HALF)
    slab = (slab_high[...], slab_low[...])
    table = (table_high[0], table_low[0])
    for half in range(2):
        values = jnp.where(core == half, own_rows, other_rows)
        spectrum = dot_split(split_values(values), table)
        modes[half * rows : (half + 1) * rows, :] = dot_split(slab, split_values(spectrum))
    for step, out in enumerate((out0, out1, out2, out3)):
        block = lax.rem(chip + step, CHIPS)
        start = pl.multiple_of(block * LANES, LANES)
        out[...] = modes[:, pl.ds(start, LANES)].reshape(LAYERS, PLANES, LANES)


def pivot_kernel(shift, cell, face, screening, out):
    shifts = shift[...]
    previous = None
    for layer in range(NZ):
        below = face[layer - 1] if layer > 0 else face[NZ - 1]
        pivot = (below + face[layer] + screening[layer]) + cell[layer] * shifts
        if previous is not None:
            pivot = pivot - (below * below) * previous
        previous = 1.0 / pivot
        out[layer] = previous


def first_solve_kernel(place, in0, in1, in2, in3, inverse, weights, fold_own, fold_far, cell, face, field, ends, part, folded, folded_own):
    chip = place[1]
    for step, source in enumerate((in0, in1, in2, in3)):
        block = lax.rem(chip + CHIPS - step, CHIPS)
        field[pl.ds(block * LAYERS, LAYERS)] = source[...]
    value = None
    for layer in range(NZ):
        inv = inverse[layer]
        scaled = field[layer] * inv
        value = scaled if value is None else scaled + (face[layer - 1] * inv) * value
        part[layer] = value
    weight = weights[...]
    keep = lax.broadcasted_iota(jnp.int32, (8, LANES), 0) == 0
    value = None
    for layer in reversed(range(NZ)):
        value = part[layer] if value is None else part[layer] + (face[layer] * inverse[layer]) * value
        weighted = weight * value
        total = (weighted[0:8] + weighted[8:16]) + (weighted[16:24] + weighted[24:32])
        total = total * cell[layer]
        folded[layer] = total
        folded_own[layer] = total + jnp.where(keep, field[layer, 0:8], 0.0)
    near = folded_own[...].reshape(8 * NZ, LANES)
    far = folded[...].reshape(8 * NZ, LANES)
    ends[...] = dot_full(near, fold_own[...], ((0,), (0,))) + dot_full(far, fold_far[...], ((0,), (0,)))


def interface_kernel(ends, inverse, forward, backward, fold_own, face, out, source, part, folded):
    total = jnp.zeros((NZ, LANES), jnp.float32)
    for slot in range(4):
        block = ends[pl.ds(slot, SLABS, stride=4), :]
        turned = block.T
        total = total + dot_full(turned[:NZ], forward[0, slot], ((1,), (0,)))
        total = total + dot_full(turned[NZ:], forward[1, slot], ((1,), (0,)))
    source[...] = total
    value = None
    for layer in range(NZ):
        inv = inverse[layer]
        row = jnp.broadcast_to(source[layer : layer + 1, :], (SLABS, LANES))
        scaled = row * inv
        value = scaled if value is None else scaled + (face[layer - 1] * inv) * value
        part[layer] = value
    value = None
    for layer in reversed(range(NZ)):
        value = part[layer] if value is None else part[layer] + (face[layer] * inverse[layer]) * value
        folded[layer] = (value[0:8] + value[8:16]) + (value[16:24] + value[24:32])
    solved = dot_full(fold_own[...], folded[...].reshape(8 * NZ, LANES), ((0,), (0,)))
    lower = solved
    upper = jnp.concatenate([solved[NZ:], solved[:NZ]], axis=0)
    for slot in range(4):
        block = dot_full(backward[0, slot], lower, ((1,), (1,))) + dot_full(backward[1, slot], upper, ((1,), (1,)))
        out[pl.ds(slot, SLABS, stride=4), :] = block


def second_solve_kernel(place, field, ends, inverse, weights, cell, face, out0, out1, out2, out3, part, edges):
    chip = place[1]
    edges[...] = ends[...].T
    weight = weights[...]
    sublane = lax.broadcasted_iota(jnp.int32, (8, LANES), 0)
    sign = jnp.where(lax.rem(sublane, 2) == 1, 1.0, -1.0)
    keep = lax.broadcasted_iota(jnp.int32, (PLANES, LANES), 0) == 0
    value = None
    for layer in range(NZ):
        inv = inverse[layer]
        near = edges[layer : layer + 1, :]
        far = edges[NZ + layer : NZ + layer + 1, :]
        edge = (near + sign * far) * cell[layer]
        edge = jnp.concatenate([edge] * 4, axis=0)
        scaled = (field[layer] + weight * edge) * inv
        value = scaled if value is None else scaled + (face[layer - 1] * inv) * value
        part[layer] = value
    value = None
    for layer in reversed(range(NZ)):
        value = part[layer] if value is None else part[layer] + (face[layer] * inverse[layer]) * value
        part[layer] = jnp.where(keep, edges[layer : layer + 1, :], value)
    for step, out in enumerate((out0, out1, out2, out3)):
        block = lax.rem(chip + step, CHIPS)
        out[...] = part[pl.ds(block * LAYERS, LAYERS)]


def backward_kernel(place, in0, in1, in2, in3, table_high, table_low, slab_high, slab_low, out, modes):
    chip = place[1]
    rows = 8 * PLANES
    for step, source in enumerate((in0, in1, in2, in3)):
        block = lax.rem(chip + CHIPS - step, CHIPS)
        start = pl.multiple_of(block * LANES, LANES)
        modes[:, pl.ds(start, LANES)] = source[...].reshape(rows, LANES)
    slab = (slab_high[...], slab_low[...])
    table = (table_high[0], table_low[0])
    planes = dot_split(slab, split_values(modes[...]))
    out[...] = dot_split(split_values(planes), table).reshape(8, PLANES, HALF)


def whole(*shape):
    return pl.BlockSpec(shape, lambda step, place: (0,) * len(shape))


scalars = pl.BlockSpec(memory_space=pltpu.SMEM)


def call(kernel, place, inputs, in_specs, outs, scratch, flops=10_000_000, bytes_accessed=4_000_000):
    grid_spec = pltpu.PrefetchScalarGridSpec(
        num_scalar_prefetch=1,
        grid=(1,),
        in_specs=in_specs,
        out_specs=[whole(*shape) for shape in outs],
        scratch_shapes=[pltpu.VMEM(shape, jnp.float32) for shape in scratch],
    )
    return pl.pallas_call(
        kernel,
        grid_spec=grid_spec,
        out_shape=[jax.ShapeDtypeStruct(shape, jnp.float32) for shape in outs],
        compiler_params=pltpu.CompilerParams(vmem_limit_bytes=VMEM_LIMIT),
        cost_estimate=pl.CostEstimate(flops=flops, bytes_accessed=bytes_accessed, transcendentals=0),
    )(place, *inputs)


def body(charge, cell, face, screening):
    gx, gz = lax.axis_index("gx"), lax.axis_index("gz")
    core, chip = lax.rem(gz, 2), lax.div(gz, 2)
    place = jnp.stack([core, chip, 1 - core]).astype(jnp.int32)
    forward_y, backward_y = y_tables()
    fy_high, fy_low = split_pair(forward_y)
    by_high, by_low = split_pair(backward_y)
    basis = slab_basis()
    slab_high, slab_low = split_pair(np.kron(np.eye(8), basis))
    slab_forward, slab_backward, alias_shift = interface_tables()
    fold_own, fold_far = fold_tables()
    weights = near_weights()
    shift_y = y_shifts().astype(np.float32)
    slab_shift = (4.0 * np.sin(np.pi * np.arange(PLANES) / (2 * PLANES)) ** 2).astype(np.float32)

    mode_row = lax.dynamic_slice_in_dim(jnp.asarray(shift_y), gz, 1, 0)
    mode_shift = mode_row + jnp.asarray(slab_shift)[:, None]
    spread = np.repeat(shift_y.reshape(2 * CHIPS * SLABS, 4), SLABS, axis=1)
    alias_total = jnp.asarray(alias_shift) + lax.dynamic_slice_in_dim(jnp.asarray(spread), gz * SLABS + gx, 1, 0)

    cube = (LAYERS, PLANES, LANES)
    tall = (NZ, PLANES, LANES)
    square = (LANES, LANES)

    def pivots(shift):
        def kernel(place, *refs):
            pivot_kernel(*refs)

        return call(kernel, place, (shift, cell, face, screening), [whole(PLANES, LANES), scalars, scalars, scalars], [tall], [])[0]

    pair = [(s, s ^ 1) for s in range(2 * CHIPS)]

    def chip_shift(step):
        return [(s, (s + 2 * step) % (2 * CHIPS)) for s in range(2 * CHIPS)]

    sign = jnp.where(core == 0, 1.0, -1.0)
    lower, upper = charge[:, :, :HALF], charge[:, :, HALF:]
    kept = lower + sign * upper
    sent = lower - sign * upper
    other = lax.ppermute(sent, "gz", pair)
    table_spec = pl.BlockSpec((1, HALF, HALF), lambda step, place: (place[0], 0, 0))
    slab_spec = whole(8 * PLANES, 8 * PLANES)
    half_block = whole(8, PLANES, HALF)
    blocks = call(
        forward_kernel,
        place,
        (kept, other, fy_high, fy_low, slab_high, slab_low),
        [half_block, half_block, table_spec, table_spec, slab_spec, slab_spec],
        [cube] * 4,
        [(LAYERS * PLANES, HALF)],
    )
    arrived = [blocks[0]] + [lax.ppermute(blocks[step], "gz", chip_shift(step)) for step in (1, 2, 3)]
    inverse = pivots(mode_shift)
    alias_inverse = pivots(alias_total)
    field, ends = call(
        first_solve_kernel,
        place,
        (*arrived, inverse, weights, fold_own, fold_far, cell, face),
        [whole(*cube)] * 4 + [whole(*tall), whole(PLANES, LANES), whole(*fold_own.shape), whole(*fold_own.shape), scalars, scalars],
        [tall, square],
        [tall, (NZ, 8, LANES), (NZ, 8, LANES)],
    )
    ends = lax.all_to_all(ends.reshape(SLABS, 4, LANES), "gx", 0, 0, tiled=True).reshape(square)

    def interface(place, *refs):
        interface_kernel(*refs)

    ends = call(
        interface,
        place,
        (ends, alias_inverse, slab_forward, slab_backward, fold_own, face),
        [whole(*square), whole(*tall), whole(*slab_forward.shape), whole(*slab_forward.shape), whole(*fold_own.shape), scalars],
        [square],
        [(NZ, LANES), tall, (NZ, 8, LANES)],
    )[0]
    ends = lax.all_to_all(ends.reshape(SLABS, 4, LANES), "gx", 0, 0, tiled=True).reshape(square)
    solved = call(
        second_solve_kernel,
        place,
        (field, ends, inverse, weights, cell, face),
        [whole(*tall), whole(*square), whole(*tall), whole(PLANES, LANES), scalars, scalars],
        [cube] * 4,
        [tall, square],
    )
    arrived = [solved[0]] + [lax.ppermute(solved[step], "gz", chip_shift(step)) for step in (1, 2, 3)]

    def back(which):
        part_spec = pl.BlockSpec((8, PLANES, LANES), lambda step, place: (place[which], 0, 0))
        return call(
            backward_kernel,
            place,
            (*arrived, by_high, by_low, slab_high, slab_low),
            [part_spec] * 4 + [table_spec, table_spec, slab_spec, slab_spec],
            [(8, PLANES, HALF)],
            [(8 * PLANES, HALF)],
        )[0]

    sent = back(2)
    other = lax.ppermute(sent, "gz", pair)
    kept = back(0)
    return jnp.concatenate([kept + other, sign * (kept - other)], axis=2)


def solution(mesh):
    in_specs = (P("gz", "gx", None), P(), P(), P())
    out_specs = P("gz", "gx", None)
    return jax.shard_map(body, mesh=mesh, in_specs=in_specs, out_specs=out_specs, check_vma=False)
```

```python
import functools
import math

import jax
import jax.numpy as jnp
import ml_dtypes
import numpy as np
from jax import lax
from jax.experimental import pallas as pl
from jax.experimental.pallas import tpu as pltpu
from jax.sharding import PartitionSpec as P

NX, NY, NZ = 1024, 1024, 64
SLABS, PLANES = 32, 32
HALF = NY // 2
CHIPS = 4
LAYERS = NZ // CHIPS
PEERS = SLABS * CHIPS
PARTS = 4
LANES = 128
highest = lax.Precision.HIGHEST
VMEM_LIMIT = 48 * 1024 * 1024


def split_pair(table):
    high = table.astype(np.float32).astype(ml_dtypes.bfloat16)
    low = (table - high.astype(np.float64)).astype(np.float32).astype(ml_dtypes.bfloat16)
    return high, low


def y_frequencies():
    index = np.arange(HALF)
    even = np.where(index <= HALF // 2, 2 * index, 2 * (index - HALF // 2))
    odd = np.where(index < HALF // 2, 2 * index + 1, 2 * (index - HALF // 2) + 1)
    even_is_cos = index <= HALF // 2
    odd_is_cos = index < HALF // 2
    return np.stack([even, odd]), np.stack([even_is_cos, odd_is_cos])


def y_tables():
    freq, is_cos = y_frequencies()
    point = np.arange(HALF)
    angle = 2.0 * np.pi * (point[None, :, None] * freq[:, None, :] % NY) / NY
    forward = np.where(is_cos[:, None, :], np.cos(angle), np.sin(angle))
    weight = np.where((freq == 0) | (freq == NY // 2), 1.0 / NY, 2.0 / NY)
    backward = np.swapaxes(forward * weight[:, None, :], 1, 2)
    return forward, backward


def y_shifts():
    freq, _ = y_frequencies()
    return (4.0 * np.sin(np.pi * freq / NY) ** 2).astype(np.float32)


def slab_basis():
    index = np.arange(PLANES)
    basis = math.sqrt(2.0 / PLANES) * np.sin(np.pi * np.outer(index, index) / PLANES)
    basis[0, :] = 0.0
    basis[:, 0] = 0.0
    basis[0, 0] = 1.0
    return basis


def slab_shifts():
    return (4.0 * np.sin(np.pi * np.arange(PLANES) / (2 * PLANES)) ** 2).astype(np.float32)


def near_weights():
    weight = slab_basis()[1].copy()
    weight[0] = 0.0
    return weight.astype(np.float32)


def far_signs():
    return np.where(np.arange(PLANES) % 2 == 1, 1.0, -1.0).astype(np.float32)


def interface_tables():
    mode = np.arange(SLABS)
    freq = np.where(mode <= SLABS // 2, mode, mode - SLABS // 2)
    is_cos = mode <= SLABS // 2
    weight = np.where((freq == 0) | (freq == SLABS // 2), 1.0, 2.0) / SLABS / SLABS

    def basis(offset):
        angle = 2.0 * np.pi * ((np.arange(SLABS)[:, None] + offset) * freq[None, :] % SLABS) / SLABS
        return np.where(is_cos[None, :], np.cos(angle), np.sin(angle))

    forward = np.concatenate([np.tile(basis(0), (1, 4)), np.tile(basis(1), (1, 4))], axis=1)
    high, low = split_pair(forward)
    backward = np.concatenate([np.tile(basis(0) * weight, (1, 4)), np.tile(basis(1) * weight, (1, 4))], axis=0)
    alias = freq[None, None, :] + SLABS * (np.arange(8)[:, None, None] + 8 * np.arange(4)[None, :, None])
    alias_shift = 4.0 * np.sin(np.pi * alias / NX) ** 2
    return (
        np.concatenate([high, low, high], axis=0),
        backward.astype(np.float32),
        alias_shift.reshape(8, LANES).astype(np.float32),
    )


def fold_table():
    fold = np.zeros((2, LAYERS, LAYERS, 8), np.float32)
    for layer in range(LAYERS):
        fold[0, layer, layer, :] = 1.0
        fold[1, layer, layer, :] = far_signs()[:8]
    return fold.reshape(2 * LAYERS, 8 * LAYERS).astype(ml_dtypes.bfloat16)


def spread_tables():
    spread = np.zeros((CHIPS, LAYERS, CHIPS, 2, PARTS, LAYERS), np.float32)
    for chip in range(CHIPS):
        for layer in range(LAYERS):
            spread[chip, layer, chip, :, :, layer] = 1.0
    mask = np.zeros((PARTS, PLANES, 2, PARTS, LAYERS), np.float32)
    for part in range(PARTS):
        mask[part, :, 0, part, :] = near_weights()[:, None]
        mask[part, :, 1, part, :] = (near_weights() * far_signs())[:, None]
    return spread.reshape(NZ, CHIPS * LANES), mask.reshape(LANES, LANES)


def split_values(values):
    high = values.astype(jnp.bfloat16)
    low = (values - high.astype(jnp.float32)).astype(jnp.bfloat16)
    return high, low


def dot_split(left, right, contract=((1,), (0,))):
    left_high, left_low = left
    right_high, right_low = right

    def dot(one, two):
        return lax.dot_general(one, two, (contract, ((), ())), preferred_element_type=jnp.float32)

    return dot(left_high, right_high) + (dot(left_high, right_low) + dot(left_low, right_high))


def dot_full(left, right, contract):
    return lax.dot_general(
        left, right, (contract, ((), ())), precision=highest, preferred_element_type=jnp.float32
    )


def pivot_kernel(place, shift_row, shift_col, cell, face, screening, out):
    base = place[1] * LAYERS
    shifts = shift_col[...] + shift_row[0]
    previous = None
    for layer in range(1, LAYERS):
        below, above = face[base + layer - 1], face[base + layer]
        pivot = (below + above + screening[base + layer]) + cell[base + layer] * shifts
        if previous is not None:
            pivot = pivot - (below * below) * previous
        previous = 1.0 / pivot
        out[layer] = previous


def stack_parts(values):
    return jnp.concatenate([values[:, part * LANES : (part + 1) * LANES] for part in range(PARTS)], axis=0).T


def unstack_parts(values):
    turned = values.T
    return jnp.concatenate([turned[part * PLANES : (part + 1) * PLANES] for part in range(PARTS)], axis=1)


def forward_kernel(place, own, other, table_high, table_low, slab_high, slab_low, inverse, weights, fold, cell, face, modes, out, part, folded):
    core, base = place[0], place[1] * LAYERS
    rows = 8 * PLANES
    own_rows = own[...].reshape(rows, HALF)
    other_rows = other[...].reshape(rows, HALF)
    slab = (slab_high[...], slab_low[...])
    table = (table_high[0], table_low[0])
    for half in range(2):
        values = jnp.where(core == half, own_rows, other_rows)
        spectrum = dot_split(split_values(values), table)
        modes[half * 8 : (half + 1) * 8] = dot_split(slab, split_values(spectrum)).reshape(8, PLANES, HALF)
    value = None
    for layer in range(1, LAYERS):
        inv = inverse[layer]
        scaled = modes[layer] * inv
        value = scaled if value is None else scaled + (face[base + layer - 1] * inv) * value
        part[layer] = value
    weight = weights[...]
    value = None
    folded[0:8] = jnp.zeros((8, HALF), jnp.float32)
    for layer in reversed(range(1, LAYERS)):
        value = part[layer] if value is None else part[layer] + (face[base + layer] * inverse[layer]) * value
        if layer == LAYERS - 1:
            out[pl.ds(1, PEERS, stride=4), :] = stack_parts(face[base + layer] * value)
        weighted = weight * value
        total = (weighted[0:8] + weighted[8:16]) + (weighted[16:24] + weighted[24:32])
        folded[layer * 8 : (layer + 1) * 8] = total * cell[base + layer]
    out[pl.ds(0, PEERS, stride=4), :] = stack_parts(modes[0] + face[base] * value)
    high, low = split_values(folded[...])
    sums = jnp.dot(fold[...], high, preferred_element_type=jnp.float32) + jnp.dot(fold[...], low, preferred_element_type=jnp.float32)
    planes = jnp.concatenate([modes[layer, 0:1] for layer in range(LAYERS)], axis=0)
    near = sums[:LAYERS] + planes
    far = sums[LAYERS:]
    blocks = [half[:, step * LANES : (step + 1) * LANES] for half in (near, far) for step in range(PARTS)]
    out[pl.ds(2, PEERS, stride=4), :] = jnp.concatenate(blocks, axis=0).T
    out[pl.ds(3, PEERS, stride=4), :] = jnp.zeros((PEERS, LANES), jnp.float32)


def prepare_kernel(place, shift_y, alias_shift, mode_shift, spread, mask, cell, face, screening, alias_inverse, response_high, response_low, corners, inverses, columns, scaled):
    start = place[0] * HALF + place[3]
    values = [shift_y[start + part * PEERS] for part in range(PARTS)]
    alias = jnp.concatenate([alias_shift[...] + value for value in values], axis=0)
    lane = lax.broadcasted_iota(jnp.int32, (8, LANES), 1)
    mode = jnp.broadcast_to(mode_shift[...], (8, LANES))
    for part in range(PARTS):
        mode = mode + jnp.where(lax.div(lane, PLANES) == part, values[part], 0.0)
    shifts = jnp.concatenate([alias, mode], axis=0)
    row = lax.broadcasted_iota(jnp.int32, (8, LANES), 0)
    previous = None
    value = None
    for layer in range(NZ):
        below = face[layer - 1] if layer > 0 else face[NZ - 1]
        pivot = (below + face[layer] + screening[layer]) + cell[layer] * shifts
        if previous is not None:
            pivot = pivot - (below * below) * previous
        previous = 1.0 / pivot
        alias_inverse[layer] = previous[: 8 * PARTS]
        inv = previous[8 * PARTS :]
        inverses[layer] = inv
        fresh = jnp.where(row == layer // LAYERS, inv, 0.0) if layer % LAYERS == 0 else None
        if value is None:
            value = fresh
        else:
            value = (face[layer - 1] * inv) * value
            if fresh is not None:
                value = value + fresh
        columns[layer] = value
    value = None
    for layer in reversed(range(NZ)):
        value = columns[layer] if value is None else columns[layer] + (face[layer] * inverses[layer]) * value
        scaled[layer * 8 : (layer + 1) * 8] = cell[layer] * value
        if layer % LAYERS == 0:
            corners[layer // LAYERS] = value
    weight = jnp.concatenate([mask[...]] * CHIPS, axis=1)
    for chip in range(CHIPS):
        column = scaled[pl.ds(chip, NZ, stride=8), :]
        response = dot_full(column, spread[...], ((0,), (0,))) * weight
        high, low = split_values(response)
        response_high[chip * LANES : (chip + 1) * LANES, :] = high
        response_low[chip * LANES : (chip + 1) * LANES, :] = low


def interface_kernel(place, arrived, response_high, response_low, corners, alias_inverse, forward, backward, face, out, source, part, solved):
    def rows(chip, slot):
        return pl.ds(4 * chip + slot, SLABS, stride=4 * CHIPS)

    sides = []
    for chip in range(CHIPS):
        side = arrived[rows(chip, 0), :]
        sides.append(side + arrived[rows(chip - 1, 1), :] if chip > 0 else side)
    response = (response_high[...], response_low[...])
    sums = dot_split(split_values(jnp.concatenate(sides, axis=1)), response)
    sums = sums + jnp.concatenate([arrived[rows(chip, 2), :] for chip in range(CHIPS)], axis=1)
    high, low = split_values(sums)
    stacked = jnp.concatenate([high, high, low], axis=0)
    turned = lax.dot_general(stacked, forward[...], (((0,), (0,)), ((), ())), preferred_element_type=jnp.float32)
    half = PARTS * LAYERS
    for chip in range(CHIPS):
        at = chip * LANES
        source[chip * half : (chip + 1) * half, :] = turned[at : at + half, :LANES] + turned[at + half : at + LANES, LANES:]
    value = None
    for layer in range(NZ):
        inv = alias_inverse[layer]
        first = (layer // LAYERS) * half + layer % LAYERS
        row = jnp.concatenate(
            [jnp.broadcast_to(source[first + step * LAYERS : first + step * LAYERS + 1, :], (8, LANES)) for step in range(PARTS)], axis=0
        )
        scaled = row * inv
        value = scaled if value is None else scaled + (face[layer - 1] * inv) * value
        part[layer] = value
    value = None
    for layer in reversed(range(NZ)):
        value = part[layer] if value is None else part[layer] + (face[layer] * alias_inverse[layer]) * value
        first = (layer // LAYERS) * half + layer % LAYERS
        solved[pl.ds(first, PARTS, stride=LAYERS), :] = jnp.sum(value.reshape(PARTS, 8, LANES), axis=1)
    planes = dot_full(backward[...], solved[...], ((1,), (1,)))
    own = []
    for chip in range(CHIPS):
        at = chip * half
        own.append(jnp.concatenate([planes[:SLABS, at : at + half], planes[SLABS:, at : at + half]], axis=1))
    change = dot_split(split_values(jnp.concatenate(own, axis=1)), response, ((1,), (1,)))
    ends = []
    for chip in range(CHIPS):
        end = change[:, chip * LANES : (chip + 1) * LANES]
        for other in range(CHIPS):
            end = end + corners[chip, other : other + 1, :] * sides[other]
        ends.append(end)
    nothing = jnp.zeros((SLABS, LANES), jnp.float32)
    ends.append(nothing)
    for chip in range(CHIPS):
        out[rows(chip, 0), :] = ends[chip]
        out[rows(chip, 1), :] = ends[chip + 1]
        out[rows(chip, 2), :] = own[chip]
        out[rows(chip, 3), :] = nothing


def second_solve_kernel(place, modes, arrived, inverse, weights, signs, table_high, table_low, slab_high, slab_low, cell, face, kept, sent, part, near, edge):
    core, base = place[0], place[1] * LAYERS
    below = unstack_parts(arrived[pl.ds(0, PEERS, stride=4), :])
    above = unstack_parts(arrived[pl.ds(1, PEERS, stride=4), :])
    turned = arrived[pl.ds(2, PEERS, stride=4), :].T
    for which, target in enumerate((near, edge)):
        for step in range(PARTS):
            at = (which * PARTS + step) * LAYERS
            target[:, step * LANES : (step + 1) * LANES] = turned[at : at + LAYERS]
    weight = weights[...]
    signed = signs[...]
    keep = lax.broadcasted_iota(jnp.int32, (PLANES, HALF), 0) == 0
    value = None
    for layer in range(1, LAYERS):
        inv = inverse[layer]
        both = (near[layer : layer + 1, :] * weight + edge[layer : layer + 1, :] * signed) * cell[base + layer]
        right = modes[layer] + both
        if layer == 1:
            right = right + face[base] * below
        if layer == LAYERS - 1:
            right = right + face[base + layer] * above
        scaled = right * inv
        value = scaled if value is None else scaled + (face[base + layer - 1] * inv) * value
        part[layer] = value
    value = None
    for layer in reversed(range(1, LAYERS)):
        value = part[layer] if value is None else part[layer] + (face[base + layer] * inverse[layer]) * value
        part[layer] = jnp.where(keep, near[layer : layer + 1, :], value)
    part[0] = jnp.where(keep, near[0:1, :], below)
    rows = 8 * PLANES
    kept[...] = part[pl.ds(core * 8, 8)]
    other = part[pl.ds((1 - core) * 8, 8)].reshape(rows, HALF)
    planes = dot_split((slab_high[...], slab_low[...]), split_values(other))
    sent[...] = dot_split(split_values(planes), (table_high[0], table_low[0])).reshape(8, PLANES, HALF)


def backward_kernel(place, modes, table_high, table_low, slab_high, slab_low, out):
    rows = 8 * PLANES
    planes = dot_split((slab_high[...], slab_low[...]), split_values(modes[...].reshape(rows, HALF)))
    out[...] = dot_split(split_values(planes), (table_high[0], table_low[0])).reshape(8, PLANES, HALF)


def whole(*shape):
    return pl.BlockSpec(shape, lambda step, place: (0,) * len(shape))


scalars = pl.BlockSpec(memory_space=pltpu.SMEM)


def call(kernel, place, inputs, in_specs, outs, scratch, cost=10_000_000):
    outs = [out if isinstance(out, jax.ShapeDtypeStruct) else jax.ShapeDtypeStruct(out, jnp.float32) for out in outs]
    grid_spec = pltpu.PrefetchScalarGridSpec(
        num_scalar_prefetch=1,
        grid=(1,),
        in_specs=in_specs,
        out_specs=[whole(*out.shape) for out in outs],
        scratch_shapes=[pltpu.VMEM(shape, jnp.float32) for shape in scratch],
    )
    return pl.pallas_call(
        kernel,
        grid_spec=grid_spec,
        out_shape=outs,
        compiler_params=pltpu.CompilerParams(vmem_limit_bytes=VMEM_LIMIT),
        cost_estimate=pl.CostEstimate(flops=cost, bytes_accessed=4_000_000, transcendentals=0),
    )(place, *inputs)


def body(charge, cell, face, screening):
    gx, gz = lax.axis_index("gx"), lax.axis_index("gz")
    core, chip = lax.rem(gz, 2), lax.div(gz, 2)
    place = jnp.stack([core, chip, 1 - core, gx * CHIPS + chip]).astype(jnp.int32)
    forward_y, backward_y = y_tables()
    fy_high, fy_low = split_pair(forward_y)
    by_high, by_low = split_pair(backward_y)
    slab_high, slab_low = split_pair(np.kron(np.eye(8), slab_basis()))
    forward_slab, backward_slab, alias_shift = interface_tables()
    spread, mask = spread_tables()
    weights = np.broadcast_to(near_weights()[:, None], (PLANES, HALF)).copy()
    signs = weights * far_signs()[:, None]
    shift_y = y_shifts()
    mode_shift = np.tile(slab_shifts(), PARTS)[None, :]

    cube = (8, PLANES, HALF)
    field = (LAYERS, PLANES, HALF)
    message = (4 * PEERS, LANES)
    square = (CHIPS * LANES, CHIPS * LANES)
    groups = [[x * 2 * CHIPS + 2 * c + r for x in range(SLABS) for c in range(CHIPS)] for r in range(2)]

    def exchange(values):
        blocks = values.reshape(PEERS, 4, LANES)
        return lax.all_to_all(blocks, ("gx", "gz"), 0, 0, axis_index_groups=groups, tiled=True).reshape(message)

    pair = [(s, s ^ 1) for s in range(2 * CHIPS)]
    sign = jnp.where(core == 0, 1.0, -1.0)
    lower, upper = charge[:, :, :HALF], charge[:, :, HALF:]
    own = lower + sign * upper
    other = lax.ppermute(lower - sign * upper, "gz", pair)
    row_spec = pl.BlockSpec((1, 1, HALF), lambda step, place: (place[0], 0, 0))
    table_spec = pl.BlockSpec((1, HALF, HALF), lambda step, place: (place[0], 0, 0))
    slab_spec = whole(8 * PLANES, 8 * PLANES)
    inverse = call(
        pivot_kernel,
        place,
        (shift_y[:, None, :], np.broadcast_to(slab_shifts()[:, None], (PLANES, HALF)).copy(), cell, face, screening),
        [row_spec, whole(PLANES, HALF), scalars, scalars, scalars],
        [field],
        [],
    )[0]
    modes, ends = call(
        forward_kernel,
        place,
        (own, other, fy_high, fy_low, slab_high, slab_low, inverse, weights, fold_table(), cell, face),
        [whole(*cube)] * 2 + [table_spec] * 2 + [slab_spec] * 2
        + [whole(*field), whole(PLANES, HALF), whole(2 * LAYERS, 8 * LAYERS), scalars, scalars],
        [field, message],
        [field, (8 * LAYERS, HALF)],
    )
    alias_inverse, response_high, response_low, corners = call(
        prepare_kernel,
        place,
        (shift_y.reshape(-1), alias_shift, mode_shift, spread, mask, cell, face, screening),
        [scalars, whole(8, LANES), whole(1, LANES), whole(*spread.shape), whole(*mask.shape), scalars, scalars, scalars],
        [(NZ, 8 * PARTS, LANES), jax.ShapeDtypeStruct(square, jnp.bfloat16), jax.ShapeDtypeStruct(square, jnp.bfloat16), (CHIPS, 8, LANES)],
        [(NZ, 8, LANES), (NZ, 8, LANES), (8 * NZ, LANES)],
    )
    ends = exchange(ends)
    ends = call(
        interface_kernel,
        place,
        (ends, response_high, response_low, corners, alias_inverse, forward_slab, backward_slab, face),
        [whole(*message), whole(*square), whole(*square), whole(CHIPS, 8, LANES), whole(NZ, 8 * PARTS, LANES)]
        + [whole(*forward_slab.shape), whole(*backward_slab.shape), scalars],
        [message],
        [(CHIPS * PARTS * LAYERS, LANES), (NZ, 8 * PARTS, LANES), (CHIPS * PARTS * LAYERS, LANES)],
    )[0]
    ends = exchange(ends)
    kept, sent = call(
        second_solve_kernel,
        place,
        (modes, ends, inverse, weights, signs, by_high, by_low, slab_high, slab_low, cell, face),
        [whole(*field), whole(*message), whole(*field), whole(PLANES, HALF), whole(PLANES, HALF)]
        + [table_spec] * 2 + [slab_spec] * 2 + [scalars] * 2,
        [cube, cube],
        [field, (LAYERS, HALF), (LAYERS, HALF)],
    )
    other = lax.ppermute(sent, "gz", pair)
    kept = call(
        backward_kernel,
        place,
        (kept, by_high, by_low, slab_high, slab_low),
        [whole(*cube)] + [table_spec] * 2 + [slab_spec] * 2,
        [cube],
        [],
    )[0]
    return jnp.concatenate([kept + other, sign * (kept - other)], axis=2)


def solution(mesh):
    in_specs = (P("gz", "gx", None), P(), P(), P())
    out_specs = P("gz", "gx", None)
    return jax.shard_map(body, mesh=mesh, in_specs=in_specs, out_specs=out_specs, check_vma=False)
```

```python
import functools
import math

import jax
import jax.numpy as jnp
import ml_dtypes
import numpy as np
from jax import lax
from jax.experimental import pallas as pl
from jax.experimental.pallas import tpu as pltpu
from jax.sharding import PartitionSpec as P

NX, NY, NZ = 1024, 1024, 64
SLABS, PLANES = 32, 32
HALF = NY // 2
CHIPS = 4
LAYERS = NZ // CHIPS
PEERS = SLABS * CHIPS
PARTS = 4
ROWS = 4
LANES = 128
highest = lax.Precision.HIGHEST
VMEM_LIMIT = 48 * 1024 * 1024


def split_pair(table):
    high = table.astype(np.float32).astype(ml_dtypes.bfloat16)
    low = (table - high.astype(np.float64)).astype(np.float32).astype(ml_dtypes.bfloat16)
    return high, low


def y_frequencies():
    index = np.arange(HALF)
    even = np.where(index <= HALF // 2, 2 * index, 2 * (index - HALF // 2))
    odd = np.where(index < HALF // 2, 2 * index + 1, 2 * (index - HALF // 2) + 1)
    even_is_cos = index <= HALF // 2
    odd_is_cos = index < HALF // 2
    return np.stack([even, odd]), np.stack([even_is_cos, odd_is_cos])


def y_tables():
    freq, is_cos = y_frequencies()
    point = np.arange(HALF)
    angle = 2.0 * np.pi * (point[None, :, None] * freq[:, None, :] % NY) / NY
    forward = np.where(is_cos[:, None, :], np.cos(angle), np.sin(angle))
    weight = np.where((freq == 0) | (freq == NY // 2), 1.0 / NY, 2.0 / NY)
    backward = np.swapaxes(forward * weight[:, None, :], 1, 2)
    return forward, backward


def y_shifts():
    freq, _ = y_frequencies()
    return (4.0 * np.sin(np.pi * freq / NY) ** 2).astype(np.float32)


def slab_basis():
    index = np.arange(PLANES)
    basis = math.sqrt(2.0 / PLANES) * np.sin(np.pi * np.outer(index, index) / PLANES)
    basis[0, :] = 0.0
    basis[:, 0] = 0.0
    basis[0, 0] = 1.0
    return basis


def slab_shifts():
    return (4.0 * np.sin(np.pi * np.arange(PLANES) / (2 * PLANES)) ** 2).astype(np.float32)


def near_weights():
    weight = slab_basis()[1].copy()
    weight[0] = 0.0
    return weight.astype(np.float32)


def far_signs():
    return np.where(np.arange(PLANES) % 2 == 1, 1.0, -1.0).astype(np.float32)


def interface_tables():
    mode = np.arange(SLABS)
    freq = np.where(mode <= SLABS // 2, mode, mode - SLABS // 2)
    is_cos = mode <= SLABS // 2
    weight = np.where((freq == 0) | (freq == SLABS // 2), 1.0, 2.0) / SLABS / SLABS

    def basis(offset):
        angle = 2.0 * np.pi * ((np.arange(SLABS)[:, None] + offset) * freq[None, :] % SLABS) / SLABS
        return np.where(is_cos[None, :], np.cos(angle), np.sin(angle))

    forward = np.concatenate([np.tile(basis(0), (1, 4)), np.tile(basis(1), (1, 4))], axis=1)
    high, low = split_pair(forward)
    backward = np.concatenate([np.tile(basis(0) * weight, (1, 4)), np.tile(basis(1) * weight, (1, 4))], axis=0)
    alias = freq[None, None, :] + SLABS * (np.arange(8)[:, None, None] + 8 * np.arange(4)[None, :, None])
    alias = np.repeat(alias, PARTS, axis=0)
    alias_shift = 4.0 * np.sin(np.pi * alias / NX) ** 2
    return (
        np.concatenate([high, low, high], axis=0),
        backward.astype(np.float32),
        alias_shift.reshape(8 * PARTS, LANES).astype(np.float32),
    )


def fold_table():
    fold = np.zeros((2, LAYERS, LAYERS, 8), np.float32)
    for layer in range(LAYERS):
        fold[0, layer, layer, :] = 1.0
        fold[1, layer, layer, :] = far_signs()[:8]
    return fold.reshape(2 * LAYERS, 8 * LAYERS).astype(ml_dtypes.bfloat16)


def spread_tables():
    spread = np.zeros((CHIPS, LAYERS, CHIPS, 2, PARTS, LAYERS), np.float32)
    for chip in range(CHIPS):
        for layer in range(LAYERS):
            spread[chip, layer, chip, :, :, layer] = 1.0
    mask = np.zeros((PARTS, PLANES, 2, PARTS, LAYERS), np.float32)
    for part in range(PARTS):
        mask[part, :, 0, part, :] = near_weights()[:, None]
        mask[part, :, 1, part, :] = (near_weights() * far_signs())[:, None]
    return spread.reshape(NZ, CHIPS * LANES), mask.reshape(LANES, LANES)


def split_values(values):
    high = values.astype(jnp.bfloat16)
    low = (values - high.astype(jnp.float32)).astype(jnp.bfloat16)
    return high, low


def dot_split(left, right, contract=((1,), (0,))):
    left_high, left_low = left
    right_high, right_low = right

    def dot(one, two):
        return lax.dot_general(one, two, (contract, ((), ())), preferred_element_type=jnp.float32)

    return dot(left_high, right_high) + (dot(left_high, right_low) + dot(left_low, right_high))


def dot_full(left, right, contract):
    return lax.dot_general(
        left, right, (contract, ((), ())), precision=highest, preferred_element_type=jnp.float32
    )


def split_kernel(place, charge, own, sent, held_charge, sems):
    copies = [pltpu.make_async_copy(charge.at[step], held_charge.at[step], sems.at[step]) for step in range(8)]
    for copy in copies:
        copy.start()
    sign = jnp.where(place[0] == 0, 1.0, -1.0)
    for step, copy in enumerate(copies):
        copy.wait()
        lower, upper = held_charge[step, :, :HALF], sign * held_charge[step, :, HALF:]
        own[step] = lower + upper
        sent[step] = lower - upper


def early_kernel(place, own, tables_high, tables_low, slab_high, slab_low, shift_y, shift_col, cell, face, screening, inverse, table_high, table_low, modes, sems):
    core, base = place[0], place[1] * LAYERS
    copies = [
        pltpu.make_async_copy(tables_high.at[core], table_high, sems.at[0]),
        pltpu.make_async_copy(tables_low.at[core], table_low, sems.at[1]),
    ]
    for copy in copies:
        copy.start()
    shifts = shift_col[...] + shift_y[core]
    previous = None
    for layer in range(1, LAYERS):
        below, above = face[base + layer - 1], face[base + layer]
        pivot = (below + above + screening[base + layer]) + cell[base + layer] * shifts
        if previous is not None:
            pivot = pivot - (below * below) * previous
        previous = 1.0 / pivot
        inverse[layer] = previous
    for copy in copies:
        copy.wait()
    modes[...] = to_modes(own, table_high, table_low, slab_high, slab_low)


def to_modes(planes, table_high, table_low, slab_high, slab_low):
    values = planes[...].reshape(8 * PLANES, HALF)
    spectrum = dot_split(split_values(values), (table_high[...], table_low[...]))
    return dot_split((slab_high[...], slab_low[...]), split_values(spectrum)).reshape(8, PLANES, HALF)


def to_planes(modes, table_high, table_low, slab_high, slab_low):
    values = dot_split((slab_high[...], slab_low[...]), split_values(modes.reshape(8 * PLANES, HALF)))
    return dot_split(split_values(values), (table_high[...], table_low[...])).reshape(8, PLANES, HALF)


def stack_parts(values):
    return jnp.concatenate([values[:, part * LANES : (part + 1) * LANES] for part in range(PARTS)], axis=0).T


def unstack_parts(values):
    turned = values.T
    return jnp.concatenate([turned[part * PLANES : (part + 1) * PLANES] for part in range(PARTS)], axis=1)


def forward_kernel(place, own_modes, other, table_high, table_low, slab_high, slab_low, inverse, weights, fold, cell, face, kept, kept_inverse, out, modes, part, folded, sems):
    core, base = place[0], place[1] * LAYERS
    copies = [pltpu.make_async_copy(inverse, kept_inverse, sems.at[0])]
    copies[0].start()
    modes[pl.ds(core * 8, 8)] = own_modes[...]
    modes[pl.ds((1 - core) * 8, 8)] = to_modes(other, table_high, table_low, slab_high, slab_low)
    copies.append(pltpu.make_async_copy(modes, kept, sems.at[1]))
    copies[1].start()
    value = None
    for layer in range(1, LAYERS):
        inv = inverse[layer]
        scaled = modes[layer] * inv
        value = scaled if value is None else scaled + (face[base + layer - 1] * inv) * value
        part[layer] = value
    weight = weights[...]
    value = None
    folded[0:8] = jnp.zeros((8, HALF), jnp.float32)
    for layer in reversed(range(1, LAYERS)):
        value = part[layer] if value is None else part[layer] + (face[base + layer] * inverse[layer]) * value
        if layer == LAYERS - 1:
            out[pl.ds(1, PEERS, stride=ROWS), :] = stack_parts(face[base + layer] * value)
        weighted = weight * value
        total = (weighted[0:8] + weighted[8:16]) + (weighted[16:24] + weighted[24:32])
        folded[layer * 8 : (layer + 1) * 8] = total * cell[base + layer]
    out[pl.ds(0, PEERS, stride=ROWS), :] = stack_parts(modes[0] + face[base] * value)
    high, low = split_values(folded[...])
    sums = jnp.dot(fold[...], high, preferred_element_type=jnp.float32) + jnp.dot(fold[...], low, preferred_element_type=jnp.float32)
    planes = jnp.concatenate([modes[layer, 0:1] for layer in range(LAYERS)], axis=0)
    near = sums[:LAYERS] + planes
    far = sums[LAYERS:]
    blocks = [half[:, step * LANES : (step + 1) * LANES] for half in (near, far) for step in range(PARTS)]
    out[pl.ds(2, PEERS, stride=ROWS), :] = jnp.concatenate(blocks, axis=0).T
    out[pl.ds(3, PEERS, stride=ROWS), :] = jnp.zeros((PEERS, LANES), jnp.float32)
    for copy in copies:
        copy.wait()


def prepare_kernel(place, shift_y, alias_shift, mode_shift, spread, mask, cell, face, screening, alias_inverse, response_high, response_low, corners, inverses, columns, scaled):
    start = place[0] * HALF + place[3]
    values = [shift_y[start + part * PEERS] for part in range(PARTS)]
    sublane = lax.rem(lax.broadcasted_iota(jnp.int32, (8 * PARTS, LANES), 0), PARTS)
    alias = alias_shift[...]
    for part in range(PARTS):
        alias = alias + jnp.where(sublane == part, values[part], 0.0)
    lane = lax.broadcasted_iota(jnp.int32, (8, LANES), 1)
    mode = jnp.broadcast_to(mode_shift[...], (8, LANES))
    for part in range(PARTS):
        mode = mode + jnp.where(lax.div(lane, PLANES) == part, values[part], 0.0)
    shifts = jnp.concatenate([alias, mode], axis=0)
    row = lax.broadcasted_iota(jnp.int32, (8, LANES), 0)
    previous = None
    value = None
    for layer in range(NZ):
        below = face[layer - 1] if layer > 0 else face[NZ - 1]
        pivot = (below + face[layer] + screening[layer]) + cell[layer] * shifts
        if previous is not None:
            pivot = pivot - (below * below) * previous
        previous = 1.0 / pivot
        alias_inverse[layer] = previous[: 8 * PARTS]
        inv = previous[8 * PARTS :]
        inverses[layer] = inv
        fresh = jnp.where(row == layer // LAYERS, inv, 0.0) if layer % LAYERS == 0 else None
        if value is None:
            value = fresh
        else:
            value = (face[layer - 1] * inv) * value
            if fresh is not None:
                value = value + fresh
        columns[layer] = value
    value = None
    for layer in reversed(range(NZ)):
        value = columns[layer] if value is None else columns[layer] + (face[layer] * inverses[layer]) * value
        scaled[layer * 8 : (layer + 1) * 8] = cell[layer] * value
        if layer % LAYERS == 0:
            corners[layer // LAYERS] = value
    weight = jnp.concatenate([mask[...]] * CHIPS, axis=1)
    for chip in range(CHIPS):
        column = scaled[pl.ds(chip, NZ, stride=8), :]
        response = dot_full(column, spread[...], ((0,), (0,))) * weight
        high, low = split_values(response)
        response_high[chip * LANES : (chip + 1) * LANES, :] = high
        response_low[chip * LANES : (chip + 1) * LANES, :] = low


def interface_kernel(place, arrived, response_high, response_low, corners, alias_inverse, forward, backward, face, out, source, part, solved):
    def rows(chip, slot):
        return pl.ds(ROWS * chip + slot, SLABS, stride=ROWS * CHIPS)

    sides = []
    for chip in range(CHIPS):
        side = arrived[rows(chip, 0), :]
        sides.append(side + arrived[rows(chip - 1, 1), :] if chip > 0 else side)
    response = (response_high[...], response_low[...])
    sums = dot_split(split_values(jnp.concatenate(sides, axis=1)), response)
    sums = sums + jnp.concatenate([arrived[rows(chip, 2), :] for chip in range(CHIPS)], axis=1)
    high, low = split_values(sums)
    stacked = jnp.concatenate([high, high, low], axis=0)
    turned = lax.dot_general(stacked, forward[...], (((0,), (0,)), ((), ())), preferred_element_type=jnp.float32)
    half = PARTS * LAYERS
    for chip in range(CHIPS):
        at = chip * LANES
        source[chip * half : (chip + 1) * half, :] = turned[at : at + half, :LANES] + turned[at + half : at + LANES, LANES:]
    value = None
    for layer in range(NZ):
        inv = alias_inverse[layer]
        first = (layer // LAYERS) * half + layer % LAYERS
        row = source[pl.ds(first, PARTS, stride=LAYERS), :]
        row = jnp.concatenate([row] * 8, axis=0)
        scaled = row * inv
        value = scaled if value is None else scaled + (face[layer - 1] * inv) * value
        part[layer] = value
    value = None
    for layer in reversed(range(NZ)):
        value = part[layer] if value is None else part[layer] + (face[layer] * alias_inverse[layer]) * value
        first = (layer // LAYERS) * half + layer % LAYERS
        total = (value[0:8] + value[8:16]) + (value[16:24] + value[24:32])
        solved[pl.ds(first, PARTS, stride=LAYERS), :] = total[:PARTS] + total[PARTS:]
    planes = dot_full(backward[...], solved[...], ((1,), (1,)))
    own = []
    for chip in range(CHIPS):
        at = chip * half
        own.append(jnp.concatenate([planes[:SLABS, at : at + half], planes[SLABS:, at : at + half]], axis=1))
    change = dot_split(split_values(jnp.concatenate(own, axis=1)), response, ((1,), (1,)))
    ends = []
    for chip in range(CHIPS):
        end = change[:, chip * LANES : (chip + 1) * LANES]
        for other in range(CHIPS):
            end = end + corners[chip, other : other + 1, :] * sides[other]
        ends.append(end)
    nothing = jnp.zeros((SLABS, LANES), jnp.float32)
    ends.append(nothing)
    for chip in range(CHIPS):
        out[rows(chip, 0), :] = ends[chip]
        out[rows(chip, 1), :] = ends[chip + 1]
        out[rows(chip, 2), :] = own[chip]
        out[rows(chip, 3), :] = nothing


def second_solve_kernel(place, modes, arrived, inverse, weights, signs, tables_high, tables_low, slab_high, slab_low, cell, face, kept, sent, table_high, table_low, part, near, edge, sems):
    core, base = place[0], place[1] * LAYERS
    copies = [
        pltpu.make_async_copy(tables_high.at[core], table_high, sems.at[0]),
        pltpu.make_async_copy(tables_low.at[core], table_low, sems.at[1]),
    ]
    for copy in copies:
        copy.start()
    below = unstack_parts(arrived[pl.ds(0, PEERS, stride=ROWS), :])
    above = unstack_parts(arrived[pl.ds(1, PEERS, stride=ROWS), :])
    turned = arrived[pl.ds(2, PEERS, stride=ROWS), :].T
    for which, target in enumerate((near, edge)):
        for step in range(PARTS):
            at = (which * PARTS + step) * LAYERS
            target[:, step * LANES : (step + 1) * LANES] = turned[at : at + LAYERS]
    weight = weights[...]
    signed = signs[...]
    keep = lax.broadcasted_iota(jnp.int32, (PLANES, HALF), 0) == 0
    value = None
    for layer in range(1, LAYERS):
        inv = inverse[layer]
        both = (near[layer : layer + 1, :] * weight + edge[layer : layer + 1, :] * signed) * cell[base + layer]
        right = modes[layer] + both
        if layer == 1:
            right = right + face[base] * below
        if layer == LAYERS - 1:
            right = right + face[base + layer] * above
        scaled = right * inv
        value = scaled if value is None else scaled + (face[base + layer - 1] * inv) * value
        part[layer] = value
    value = None
    for layer in reversed(range(1, LAYERS)):
        value = part[layer] if value is None else part[layer] + (face[base + layer] * inverse[layer]) * value
        part[layer] = jnp.where(keep, near[layer : layer + 1, :], value)
    part[0] = jnp.where(keep, near[0:1, :], below)
    kept[...] = part[pl.ds(core * 8, 8)]
    for copy in copies:
        copy.wait()
    sent[...] = to_planes(part[pl.ds((1 - core) * 8, 8)], table_high, table_low, slab_high, slab_low)


def backward_kernel(place, modes, table_high, table_low, slab_high, slab_low, out):
    out[...] = to_planes(modes[...], table_high, table_low, slab_high, slab_low)


def join_kernel(place, kept, other, out, joined, sems):
    sign = jnp.where(place[0] == 0, 1.0, -1.0)
    copies = []
    for step in range(8):
        one, two = kept[step], other[step]
        joined[step, :, :HALF] = one + two
        joined[step, :, HALF:] = sign * (one - two)
        copies.append(pltpu.make_async_copy(joined.at[step], out.at[step], sems.at[step]))
        copies[-1].start()
    for copy in copies:
        copy.wait()


held = pl.BlockSpec(memory_space=pltpu.VMEM)
far = pl.BlockSpec(memory_space=pl.ANY)
scalars = pl.BlockSpec(memory_space=pltpu.SMEM)
in_hbm = functools.partial(pltpu.with_memory_space_constraint, memory_space=pltpu.HBM)


def call(kernel, place, inputs, in_specs, outs, out_specs, scratch=(), grid=(), cost=10_000_000):
    return pl.pallas_call(
        kernel,
        grid=grid,
        in_specs=[scalars, *in_specs],
        out_specs=out_specs,
        out_shape=outs,
        scratch_shapes=scratch,
        compiler_params=pltpu.CompilerParams(vmem_limit_bytes=VMEM_LIMIT),
        cost_estimate=pl.CostEstimate(flops=cost, bytes_accessed=4_000_000, transcendentals=0),
    )(place, *inputs)


def body(charge, cell, face, screening):
    gx, gz = lax.axis_index("gx"), lax.axis_index("gz")
    core, chip = lax.rem(gz, 2), lax.div(gz, 2)
    place = jnp.stack([core, chip, 1 - core, gx * CHIPS + chip]).astype(jnp.int32)
    forward_y, backward_y = y_tables()
    fy_high, fy_low = split_pair(forward_y)
    by_high, by_low = split_pair(backward_y)
    slab_high, slab_low = split_pair(np.kron(np.eye(8), slab_basis()))
    forward_slab, backward_slab, alias_shift = interface_tables()
    spread, mask = spread_tables()
    weights = np.broadcast_to(near_weights()[:, None], (PLANES, HALF)).copy()
    signs = weights * far_signs()[:, None]
    shift_y = y_shifts()
    mode_shift = np.tile(slab_shifts(), PARTS)[None, :]

    cube = (8, PLANES, HALF)
    field = (LAYERS, PLANES, HALF)
    message = (ROWS * PEERS, LANES)
    square = (CHIPS * LANES, CHIPS * LANES)
    table = pltpu.VMEM((HALF, HALF), jnp.bfloat16)
    groups = [[x * 2 * CHIPS + 2 * c + r for x in range(SLABS) for c in range(CHIPS)] for r in range(2)]

    def vmem(*shape):
        return pltpu.VMEM(shape, jnp.float32)

    def exchange(values):
        blocks = values.reshape(PEERS, ROWS, LANES)
        return lax.all_to_all(blocks, ("gx", "gz"), 0, 0, axis_index_groups=groups, tiled=True).reshape(message)

    pair = [(s, s ^ 1) for s in range(2 * CHIPS)]
    lines = vmem(8, PLANES, NY)
    own, sent = call(
        split_kernel, place, (in_hbm(charge),), [far], [vmem(*cube), vmem(*cube)], [held] * 2, [lines, pltpu.SemaphoreType.DMA((8,))]
    )
    other = lax.ppermute(sent, "gz", pair)
    inverse, table_high, table_low, own_modes = call(
        early_kernel,
        place,
        (own, in_hbm(fy_high), in_hbm(fy_low), slab_high, slab_low, shift_y[:, None, :], np.broadcast_to(slab_shifts()[:, None], (PLANES, HALF)).copy(), cell, face, screening),
        [held, far, far] + [held] * 4 + [scalars] * 3,
        [vmem(*field), table, table, vmem(*cube)],
        [held] * 4,
        [pltpu.SemaphoreType.DMA((2,))],
    )
    modes, inverse, ends = call(
        forward_kernel,
        place,
        (own_modes, other, table_high, table_low, slab_high, slab_low, inverse, weights, fold_table(), cell, face),
        [held] * 9 + [scalars] * 2,
        [pltpu.HBM(field, jnp.float32), pltpu.HBM(field, jnp.float32), pltpu.HBM(message, jnp.float32)],
        [far, far, held],
        [vmem(*field), vmem(*field), vmem(8 * LAYERS, HALF), pltpu.SemaphoreType.DMA((2,))],
    )
    alias_inverse, response_high, response_low, corners = call(
        prepare_kernel,
        place,
        (shift_y.reshape(-1), alias_shift, mode_shift, spread, mask, cell, face, screening),
        [scalars] + [held] * 4 + [scalars] * 3,
        [vmem(NZ, 8 * PARTS, LANES), pltpu.VMEM(square, jnp.bfloat16), pltpu.VMEM(square, jnp.bfloat16), vmem(CHIPS, 8, LANES)],
        [held] * 4,
        [vmem(NZ, 8, LANES), vmem(NZ, 8, LANES), vmem(8 * NZ, LANES)],
    )
    ends = exchange(ends)
    ends = call(
        interface_kernel,
        place,
        (ends, response_high, response_low, corners, alias_inverse, forward_slab, backward_slab, face),
        [held] * 7 + [scalars],
        vmem(*message),
        held,
        [vmem(CHIPS * PARTS * LAYERS, LANES), vmem(NZ, 8 * PARTS, LANES), vmem(CHIPS * PARTS * LAYERS, LANES)],
    )
    ends = exchange(ends)
    kept, sent, table_high, table_low = call(
        second_solve_kernel,
        place,
        (modes, ends, inverse, weights, signs, in_hbm(by_high), in_hbm(by_low), slab_high, slab_low, cell, face),
        [held] * 5 + [far] * 2 + [held] * 2 + [scalars] * 2,
        [vmem(*cube), vmem(*cube), table, table],
        [held] * 4,
        [vmem(*field), vmem(LAYERS, HALF), vmem(LAYERS, HALF), pltpu.SemaphoreType.DMA((2,))],
    )
    other = lax.ppermute(sent, "gz", pair)
    kept = call(backward_kernel, place, (kept, table_high, table_low, slab_high, slab_low), [held] * 5, vmem(*cube), held)
    return call(
        join_kernel, place, (kept, other), [held] * 2, pltpu.HBM((8, PLANES, NY), jnp.float32), far, [lines, pltpu.SemaphoreType.DMA((8,))]
    )


def solution(mesh):
    in_specs = (P("gz", "gx", None), P(), P(), P())
    out_specs = P("gz", "gx", None)
    return jax.shard_map(body, mesh=mesh, in_specs=in_specs, out_specs=out_specs, check_vma=False)
```

```python
import functools
import math

import jax
import jax.numpy as jnp
import ml_dtypes
import numpy as np
from jax import lax
from jax.experimental import pallas as pl
from jax.experimental.pallas import tpu as pltpu
from jax.sharding import PartitionSpec as P

NX, NY, NZ = 1024, 1024, 64
SLABS, PLANES = 32, 32
HALF = NY // 2
CHIPS = 4
LAYERS = NZ // CHIPS
PEERS = SLABS * CHIPS
PARTS = 4
ROWS = 4
LANES = 128
highest = lax.Precision.HIGHEST
VMEM_LIMIT = 48 * 1024 * 1024


def split_pair(table):
    high = table.astype(np.float32).astype(ml_dtypes.bfloat16)
    low = (table - high.astype(np.float64)).astype(np.float32).astype(ml_dtypes.bfloat16)
    return high, low


def y_frequencies():
    index = np.arange(HALF)
    even = np.where(index <= HALF // 2, 2 * index, 2 * (index - HALF // 2))
    odd = np.where(index < HALF // 2, 2 * index + 1, 2 * (index - HALF // 2) + 1)
    even_is_cos = index <= HALF // 2
    odd_is_cos = index < HALF // 2
    return np.stack([even, odd]), np.stack([even_is_cos, odd_is_cos])


def y_tables():
    freq, is_cos = y_frequencies()
    point = np.arange(HALF)
    angle = 2.0 * np.pi * (point[None, :, None] * freq[:, None, :] % NY) / NY
    forward = np.where(is_cos[:, None, :], np.cos(angle), np.sin(angle))
    weight = np.where((freq == 0) | (freq == NY // 2), 1.0 / NY, 2.0 / NY)
    backward = np.swapaxes(forward * weight[:, None, :], 1, 2)
    return forward, backward


def y_shifts():
    freq, _ = y_frequencies()
    return (4.0 * np.sin(np.pi * freq / NY) ** 2).astype(np.float32)


def slab_basis():
    index = np.arange(PLANES)
    basis = math.sqrt(2.0 / PLANES) * np.sin(np.pi * np.outer(index, index) / PLANES)
    basis[0, :] = 0.0
    basis[:, 0] = 0.0
    basis[0, 0] = 1.0
    return basis


def slab_shifts():
    return (4.0 * np.sin(np.pi * np.arange(PLANES) / (2 * PLANES)) ** 2).astype(np.float32)


def near_weights():
    weight = slab_basis()[1].copy()
    weight[0] = 0.0
    return weight.astype(np.float32)


def far_signs():
    return np.where(np.arange(PLANES) % 2 == 1, 1.0, -1.0).astype(np.float32)


def interface_tables():
    mode = np.arange(SLABS)
    freq = np.where(mode <= SLABS // 2, mode, mode - SLABS // 2)
    is_cos = mode <= SLABS // 2
    weight = np.where((freq == 0) | (freq == SLABS // 2), 1.0, 2.0) / SLABS / SLABS

    def basis(offset):
        angle = 2.0 * np.pi * ((np.arange(SLABS)[:, None] + offset) * freq[None, :] % SLABS) / SLABS
        return np.where(is_cos[None, :], np.cos(angle), np.sin(angle))

    forward = np.concatenate([np.tile(basis(0), (1, 4)), np.tile(basis(1), (1, 4))], axis=1)
    high, low = split_pair(forward)
    backward = np.concatenate([np.tile(basis(0) * weight, (1, 4)), np.tile(basis(1) * weight, (1, 4))], axis=0)
    alias = freq[None, None, :] + SLABS * (np.arange(8)[:, None, None] + 8 * np.arange(4)[None, :, None])
    alias = np.repeat(alias, PARTS, axis=0)
    alias_shift = 4.0 * np.sin(np.pi * alias / NX) ** 2
    return (
        np.concatenate([high, low, high], axis=0),
        backward.astype(np.float32),
        alias_shift.reshape(8 * PARTS, LANES).astype(np.float32),
    )


def fold_table():
    fold = np.zeros((2, LAYERS, LAYERS, 8), np.float32)
    for layer in range(LAYERS):
        fold[0, layer, layer, :] = 1.0
        fold[1, layer, layer, :] = far_signs()[:8]
    return fold.reshape(2 * LAYERS, 8 * LAYERS).astype(ml_dtypes.bfloat16)


def spread_tables():
    spread = np.zeros((CHIPS, LAYERS, CHIPS, 2, PARTS, LAYERS), np.float32)
    for chip in range(CHIPS):
        for layer in range(LAYERS):
            spread[chip, layer, chip, :, :, layer] = 1.0
    mask = np.zeros((PARTS, PLANES, 2, PARTS, LAYERS), np.float32)
    for part in range(PARTS):
        mask[part, :, 0, part, :] = near_weights()[:, None]
        mask[part, :, 1, part, :] = (near_weights() * far_signs())[:, None]
    return spread.reshape(NZ, CHIPS * LANES), mask.reshape(LANES, LANES)


class Column:
    def __init__(self, ref, which):
        self.ref, self.start = ref, which * NZ

    def __getitem__(self, layer):
        return self.ref[self.start + layer]


def columns_of(ref):
    return [Column(ref, which) for which in range(3)]


def split_values(values):
    high = values.astype(jnp.bfloat16)
    low = (values - high.astype(jnp.float32)).astype(jnp.bfloat16)
    return high, low


def dot_split(left, right, contract=((1,), (0,))):
    left_high, left_low = left
    right_high, right_low = right

    def dot(one, two):
        return lax.dot_general(one, two, (contract, ((), ())), preferred_element_type=jnp.float32)

    return dot(left_high, right_high) + (dot(left_high, right_low) + dot(left_low, right_high))


def dot_full(left, right, contract):
    return lax.dot_general(
        left, right, (contract, ((), ())), precision=highest, preferred_element_type=jnp.float32
    )


def split_kernel(place, charge, tables_high, tables_low, own, sent, table_high, table_low, held_charge, sems):
    copies = [pltpu.make_async_copy(charge.at[step], held_charge.at[step], sems.at[step]) for step in range(8)]
    copies.append(pltpu.make_async_copy(tables_high.at[place[0]], table_high, sems.at[8]))
    copies.append(pltpu.make_async_copy(tables_low.at[place[0]], table_low, sems.at[9]))
    for copy in copies:
        copy.start()
    sign = jnp.where(place[0] == 0, 1.0, -1.0)
    for step, copy in enumerate(copies[:8]):
        copy.wait()
        lower, upper = held_charge[step, :, :HALF], sign * held_charge[step, :, HALF:]
        own[step] = lower + upper
        sent[step] = lower - upper
    for copy in copies[8:]:
        copy.wait()


def chip_pivots(place, shift_y, shift_col, coefficients, inverse):
    cell, face, screening = columns_of(coefficients)
    base = place[1] * LAYERS
    shifts = shift_col[...] + shift_y[place[0]]
    previous = None
    for layer in range(1, LAYERS):
        below, above = face[base + layer - 1], face[base + layer]
        pivot = (below + above + screening[base + layer]) + cell[base + layer] * shifts
        if previous is not None:
            pivot = pivot - (below * below) * previous
        previous = 1.0 / pivot
        inverse[layer] = previous


def early_kernel(place, own, table_high, table_low, slab_high, slab_low, shift_y, shift_col, coefficients, inverse, modes):
    chip_pivots(place, shift_y, shift_col, coefficients, inverse)
    modes[...] = to_modes(own, table_high, table_low, slab_high, slab_low)


def to_modes(planes, table_high, table_low, slab_high, slab_low):
    values = planes[...].reshape(8 * PLANES, HALF)
    spectrum = dot_split(split_values(values), (table_high[...], table_low[...]))
    return dot_split((slab_high[...], slab_low[...]), split_values(spectrum)).reshape(8, PLANES, HALF)


def to_planes(modes, table_high, table_low, slab_high, slab_low):
    values = dot_split((slab_high[...], slab_low[...]), split_values(modes.reshape(8 * PLANES, HALF)))
    return dot_split(split_values(values), (table_high[...], table_low[...])).reshape(8, PLANES, HALF)


def stack_parts(values):
    return jnp.concatenate([values[:, part * LANES : (part + 1) * LANES] for part in range(PARTS)], axis=0).T


def unstack_parts(values):
    turned = values.T
    return jnp.concatenate([turned[part * PLANES : (part + 1) * PLANES] for part in range(PARTS)], axis=1)


def forward_kernel(place, own_modes, other, table_high, table_low, slab_high, slab_low, inverse, weights, fold, coefficients, kept, out, modes, part, folded, sem):
    core, base = place[0], place[1] * LAYERS
    cell, face, _ = columns_of(coefficients)
    modes[pl.ds(core * 8, 8)] = own_modes[...]
    modes[pl.ds((1 - core) * 8, 8)] = to_modes(other, table_high, table_low, slab_high, slab_low)
    copy = pltpu.make_async_copy(modes, kept, sem)
    copy.start()
    value = None
    for layer in range(1, LAYERS):
        inv = inverse[layer]
        scaled = modes[layer] * inv
        value = scaled if value is None else scaled + (face[base + layer - 1] * inv) * value
        part[layer] = value
    weight = weights[...]
    value = None
    folded[0:8] = jnp.zeros((8, HALF), jnp.float32)
    for layer in reversed(range(1, LAYERS)):
        value = part[layer] if value is None else part[layer] + (face[base + layer] * inverse[layer]) * value
        if layer == LAYERS - 1:
            out[pl.ds(1, PEERS, stride=ROWS), :] = stack_parts(face[base + layer] * value)
        weighted = weight * value
        total = (weighted[0:8] + weighted[8:16]) + (weighted[16:24] + weighted[24:32])
        folded[layer * 8 : (layer + 1) * 8] = total * cell[base + layer]
    out[pl.ds(0, PEERS, stride=ROWS), :] = stack_parts(modes[0] + face[base] * value)
    high, low = split_values(folded[...])
    sums = jnp.dot(fold[...], high, preferred_element_type=jnp.float32) + jnp.dot(fold[...], low, preferred_element_type=jnp.float32)
    planes = jnp.concatenate([modes[layer, 0:1] for layer in range(LAYERS)], axis=0)
    near = sums[:LAYERS] + planes
    far = sums[LAYERS:]
    blocks = [half[:, step * LANES : (step + 1) * LANES] for half in (near, far) for step in range(PARTS)]
    out[pl.ds(2, PEERS, stride=ROWS), :] = jnp.concatenate(blocks, axis=0).T
    out[pl.ds(3, PEERS, stride=ROWS), :] = jnp.zeros((PEERS, LANES), jnp.float32)
    copy.wait()


def prepare_kernel(place, shift_y, alias_shift, mode_shift, spread, mask, tables_high, tables_low, coefficients, alias_inverse, response_high, response_low, corners, table_high, table_low, inverses, columns, scaled, sems):
    copies = [
        pltpu.make_async_copy(tables_high.at[place[0]], table_high, sems.at[0]),
        pltpu.make_async_copy(tables_low.at[place[0]], table_low, sems.at[1]),
    ]
    for copy in copies:
        copy.start()
    cell, face, screening = columns_of(coefficients)
    start = place[0] * HALF + place[3]
    values = [shift_y[start + part * PEERS] for part in range(PARTS)]
    sublane = lax.rem(lax.broadcasted_iota(jnp.int32, (8 * PARTS, LANES), 0), PARTS)
    alias = alias_shift[...]
    for part in range(PARTS):
        alias = alias + jnp.where(sublane == part, values[part], 0.0)
    lane = lax.broadcasted_iota(jnp.int32, (8, LANES), 1)
    mode = jnp.broadcast_to(mode_shift[...], (8, LANES))
    for part in range(PARTS):
        mode = mode + jnp.where(lax.div(lane, PLANES) == part, values[part], 0.0)
    shifts = jnp.concatenate([alias, mode], axis=0)
    row = lax.broadcasted_iota(jnp.int32, (8, LANES), 0)
    previous = None
    value = None
    for layer in range(NZ):
        below = face[layer - 1] if layer > 0 else face[NZ - 1]
        pivot = (below + face[layer] + screening[layer]) + cell[layer] * shifts
        if previous is not None:
            pivot = pivot - (below * below) * previous
        previous = 1.0 / pivot
        alias_inverse[layer] = previous[: 8 * PARTS]
        inv = previous[8 * PARTS :]
        inverses[layer] = inv
        fresh = jnp.where(row == layer // LAYERS, inv, 0.0) if layer % LAYERS == 0 else None
        if value is None:
            value = fresh
        else:
            value = (face[layer - 1] * inv) * value
            if fresh is not None:
                value = value + fresh
        columns[layer] = value
    value = None
    for layer in reversed(range(NZ)):
        value = columns[layer] if value is None else columns[layer] + (face[layer] * inverses[layer]) * value
        scaled[layer * 8 : (layer + 1) * 8] = cell[layer] * value
        if layer % LAYERS == 0:
            corners[layer // LAYERS] = value
    weight = jnp.concatenate([mask[...]] * CHIPS, axis=1)
    for chip in range(CHIPS):
        column = scaled[pl.ds(chip, NZ, stride=8), :]
        response = dot_full(column, spread[...], ((0,), (0,))) * weight
        high, low = split_values(response)
        response_high[chip * LANES : (chip + 1) * LANES, :] = high
        response_low[chip * LANES : (chip + 1) * LANES, :] = low
    for copy in copies:
        copy.wait()


def interface_kernel(place, arrived, response_high, response_low, alias_inverse, forward_far, backward_far, corners_far, coefficients, out, source, part, solved, forward, backward, corners, sems):
    pairs = ((forward_far, forward), (backward_far, backward), (corners_far, corners))
    copies = [pltpu.make_async_copy(*pair, sems.at[step]) for step, pair in enumerate(pairs)]
    for copy in copies:
        copy.start()
    face = columns_of(coefficients)[1]

    def rows(chip, slot):
        return pl.ds(ROWS * chip + slot, SLABS, stride=ROWS * CHIPS)

    sides = []
    for chip in range(CHIPS):
        side = arrived[rows(chip, 0), :]
        sides.append(side + arrived[rows(chip - 1, 1), :] if chip > 0 else side)
    response = (response_high[...], response_low[...])
    sums = dot_split(split_values(jnp.concatenate(sides, axis=1)), response)
    sums = sums + jnp.concatenate([arrived[rows(chip, 2), :] for chip in range(CHIPS)], axis=1)
    high, low = split_values(sums)
    stacked = jnp.concatenate([high, high, low], axis=0)
    for copy in copies:
        copy.wait()
    turned = lax.dot_general(stacked, forward[...], (((0,), (0,)), ((), ())), preferred_element_type=jnp.float32)
    half = PARTS * LAYERS
    for chip in range(CHIPS):
        at = chip * LANES
        source[chip * half : (chip + 1) * half, :] = turned[at : at + half, :LANES] + turned[at + half : at + LANES, LANES:]
    value = None
    for layer in range(NZ):
        inv = alias_inverse[layer]
        first = (layer // LAYERS) * half + layer % LAYERS
        row = source[pl.ds(first, PARTS, stride=LAYERS), :]
        row = jnp.concatenate([row] * 8, axis=0)
        scaled = row * inv
        value = scaled if value is None else scaled + (face[layer - 1] * inv) * value
        part[layer] = value
    value = None
    for layer in reversed(range(NZ)):
        value = part[layer] if value is None else part[layer] + (face[layer] * alias_inverse[layer]) * value
        first = (layer // LAYERS) * half + layer % LAYERS
        total = (value[0:8] + value[8:16]) + (value[16:24] + value[24:32])
        solved[pl.ds(first, PARTS, stride=LAYERS), :] = total[:PARTS] + total[PARTS:]
    planes = dot_full(backward[...], solved[...], ((1,), (1,)))
    own = []
    for chip in range(CHIPS):
        at = chip * half
        own.append(jnp.concatenate([planes[:SLABS, at : at + half], planes[SLABS:, at : at + half]], axis=1))
    change = dot_split(split_values(jnp.concatenate(own, axis=1)), response, ((1,), (1,)))
    ends = []
    for chip in range(CHIPS):
        end = change[:, chip * LANES : (chip + 1) * LANES]
        for other in range(CHIPS):
            end = end + corners[chip, other : other + 1, :] * sides[other]
        ends.append(end)
    nothing = jnp.zeros((SLABS, LANES), jnp.float32)
    ends.append(nothing)
    for chip in range(CHIPS):
        out[rows(chip, 0), :] = ends[chip]
        out[rows(chip, 1), :] = ends[chip + 1]
        out[rows(chip, 2), :] = own[chip]
        out[rows(chip, 3), :] = nothing


def second_solve_kernel(place, modes, arrived, shift_y, shift_col, weights, signs, table_high, table_low, slab_high, slab_low, coefficients, kept, sent, part, near, edge, inverse):
    core, base = place[0], place[1] * LAYERS
    cell, face, _ = columns_of(coefficients)
    chip_pivots(place, shift_y, shift_col, coefficients, inverse)
    below = unstack_parts(arrived[pl.ds(0, PEERS, stride=ROWS), :])
    above = unstack_parts(arrived[pl.ds(1, PEERS, stride=ROWS), :])
    turned = arrived[pl.ds(2, PEERS, stride=ROWS), :].T
    for which, target in enumerate((near, edge)):
        for step in range(PARTS):
            at = (which * PARTS + step) * LAYERS
            target[:, step * LANES : (step + 1) * LANES] = turned[at : at + LAYERS]
    weight = weights[...]
    signed = signs[...]
    keep = lax.broadcasted_iota(jnp.int32, (PLANES, HALF), 0) == 0
    value = None
    for layer in range(1, LAYERS):
        inv = inverse[layer]
        both = (near[layer : layer + 1, :] * weight + edge[layer : layer + 1, :] * signed) * cell[base + layer]
        right = modes[layer] + both
        if layer == 1:
            right = right + face[base] * below
        if layer == LAYERS - 1:
            right = right + face[base + layer] * above
        scaled = right * inv
        value = scaled if value is None else scaled + (face[base + layer - 1] * inv) * value
        part[layer] = value
    value = None
    for layer in reversed(range(1, LAYERS)):
        value = part[layer] if value is None else part[layer] + (face[base + layer] * inverse[layer]) * value
        part[layer] = jnp.where(keep, near[layer : layer + 1, :], value)
    part[0] = jnp.where(keep, near[0:1, :], below)
    kept[...] = part[pl.ds(core * 8, 8)]
    sent[...] = to_planes(part[pl.ds((1 - core) * 8, 8)], table_high, table_low, slab_high, slab_low)


def backward_kernel(place, modes, table_high, table_low, slab_high, slab_low, out):
    out[...] = to_planes(modes[...], table_high, table_low, slab_high, slab_low)


held = pl.BlockSpec(memory_space=pltpu.VMEM)
far = pl.BlockSpec(memory_space=pl.ANY)
scalars = pl.BlockSpec(memory_space=pltpu.SMEM)
in_hbm = functools.partial(pltpu.with_memory_space_constraint, memory_space=pltpu.HBM)


def call(kernel, place, inputs, in_specs, outs, out_specs, scratch=(), grid=(), cost=10_000_000):
    return pl.pallas_call(
        kernel,
        grid=grid,
        in_specs=[scalars, *in_specs],
        out_specs=out_specs,
        out_shape=outs,
        scratch_shapes=scratch,
        compiler_params=pltpu.CompilerParams(vmem_limit_bytes=VMEM_LIMIT),
        cost_estimate=pl.CostEstimate(flops=cost, bytes_accessed=4_000_000, transcendentals=0),
    )(place, *inputs)


def body(charge, cell, face, screening):
    gx, gz = lax.axis_index("gx"), lax.axis_index("gz")
    core, chip = lax.rem(gz, 2), lax.div(gz, 2)
    place = jnp.stack([core, chip, 1 - core, gx * CHIPS + chip]).astype(jnp.int32)
    forward_y, backward_y = y_tables()
    fy_high, fy_low = split_pair(forward_y)
    by_high, by_low = split_pair(backward_y)
    slab_high, slab_low = split_pair(np.kron(np.eye(8), slab_basis()))
    forward_slab, backward_slab, alias_shift = interface_tables()
    spread, mask = spread_tables()
    weights = np.broadcast_to(near_weights()[:, None], (PLANES, HALF)).copy()
    signs = weights * far_signs()[:, None]
    shift_y = y_shifts()
    mode_shift = np.tile(slab_shifts(), PARTS)[None, :]

    cube = (8, PLANES, HALF)
    field = (LAYERS, PLANES, HALF)
    message = (ROWS * PEERS, LANES)
    square = (CHIPS * LANES, CHIPS * LANES)
    table = pltpu.VMEM((HALF, HALF), jnp.bfloat16)
    far_table = pltpu.HBM((HALF, HALF), jnp.bfloat16)
    groups = [[x * 2 * CHIPS + 2 * c + r for x in range(SLABS) for c in range(CHIPS)] for r in range(2)]

    def vmem(*shape):
        return pltpu.VMEM(shape, jnp.float32)

    def exchange(values):
        blocks = values.reshape(PEERS, ROWS, LANES)
        return lax.all_to_all(blocks, ("gx", "gz"), 0, 0, axis_index_groups=groups, tiled=True).reshape(message)

    pair = [(s, s ^ 1) for s in range(2 * CHIPS)]
    lines = vmem(8, PLANES, NY)
    own, sent, table_high, table_low = call(
        split_kernel,
        place,
        (in_hbm(charge), in_hbm(fy_high), in_hbm(fy_low)),
        [far] * 3,
        [vmem(*cube), vmem(*cube), table, table],
        [held] * 4,
        [lines, pltpu.SemaphoreType.DMA((10,))],
    )
    other = lax.ppermute(sent, "gz", pair)
    shifts = (shift_y[:, None, :], np.broadcast_to(slab_shifts()[:, None], (PLANES, HALF)).copy())
    coefficients = jnp.concatenate([cell, face, screening])
    inverse, own_modes = call(
        early_kernel,
        place,
        (own, table_high, table_low, slab_high, slab_low, *shifts, coefficients),
        [held] * 7 + [scalars],
        [vmem(*field), vmem(*cube)],
        [held] * 2,
    )
    modes, ends = call(
        forward_kernel,
        place,
        (own_modes, other, table_high, table_low, slab_high, slab_low, inverse, weights, fold_table(), coefficients),
        [held] * 9 + [scalars],
        [pltpu.HBM(field, jnp.float32), pltpu.HBM(message, jnp.float32)],
        [far, held],
        [vmem(*field), vmem(*field), vmem(8 * LAYERS, HALF), pltpu.SemaphoreType.DMA],
    )
    alias_inverse, response_high, response_low, corners, table_high, table_low = call(
        prepare_kernel,
        place,
        (shift_y.reshape(-1), alias_shift, mode_shift, spread, mask, in_hbm(by_high), in_hbm(by_low), coefficients),
        [scalars] + [held] * 4 + [far] * 2 + [scalars],
        [vmem(NZ, 8 * PARTS, LANES), pltpu.VMEM(square, jnp.bfloat16), pltpu.VMEM(square, jnp.bfloat16), pltpu.HBM((CHIPS, 8, LANES), jnp.float32), far_table, far_table],
        [held] * 4 + [far] * 2,
        [vmem(NZ, 8, LANES), vmem(NZ, 8, LANES), vmem(8 * NZ, LANES), pltpu.SemaphoreType.DMA((2,))],
    )
    ends = exchange(ends)
    ends = call(
        interface_kernel,
        place,
        (ends, response_high, response_low, alias_inverse, in_hbm(forward_slab), in_hbm(backward_slab), in_hbm(corners), coefficients),
        [held] * 4 + [far] * 3 + [scalars],
        vmem(*message),
        held,
        [vmem(CHIPS * PARTS * LAYERS, LANES), vmem(NZ, 8 * PARTS, LANES), vmem(CHIPS * PARTS * LAYERS, LANES)]
        + [pltpu.VMEM(forward_slab.shape, jnp.bfloat16), vmem(*backward_slab.shape), vmem(CHIPS, 8, LANES), pltpu.SemaphoreType.DMA((3,))],
    )
    ends = exchange(ends)
    kept, sent = call(
        second_solve_kernel,
        place,
        (modes, ends, *shifts, weights, signs, table_high, table_low, slab_high, slab_low, coefficients),
        [held] * 10 + [scalars],
        [vmem(*cube), vmem(*cube)],
        [held] * 2,
        [vmem(*field), vmem(LAYERS, HALF), vmem(LAYERS, HALF), vmem(*field)],
    )
    other = lax.ppermute(sent, "gz", pair)
    kept = call(backward_kernel, place, (kept, table_high, table_low, slab_high, slab_low), [held] * 5, vmem(*cube), held)
    sign = jnp.where(core == 0, 1.0, -1.0)
    return jnp.concatenate([kept + other, sign * (kept - other)], axis=2)


def solution(mesh):
    in_specs = (P("gz", "gx", None), P(), P(), P())
    out_specs = P("gz", "gx", None)
    return jax.shard_map(body, mesh=mesh, in_specs=in_specs, out_specs=out_specs, check_vma=False)
```

```python
import functools
import math

import jax
import jax.numpy as jnp
import ml_dtypes
import numpy as np
from jax import lax
from jax.experimental import pallas as pl
from jax.experimental.pallas import tpu as pltpu
from jax.sharding import PartitionSpec as P

NX, NY, NZ = 1024, 1024, 64
SLABS, PLANES = 32, 32
HALF = NY // 2
CHIPS = 4
LAYERS = NZ // CHIPS
PEERS = SLABS * CHIPS
PARTS = 4
ROWS = 4
LANES = 128
highest = lax.Precision.HIGHEST
VMEM_LIMIT = 48 * 1024 * 1024


def split_pair(table):
    high = table.astype(np.float32).astype(ml_dtypes.bfloat16)
    low = (table - high.astype(np.float64)).astype(np.float32).astype(ml_dtypes.bfloat16)
    return high, low


def y_frequencies():
    index = np.arange(HALF)
    even = np.where(index <= HALF // 2, 2 * index, 2 * (index - HALF // 2))
    odd = np.where(index < HALF // 2, 2 * index + 1, 2 * (index - HALF // 2) + 1)
    even_is_cos = index <= HALF // 2
    odd_is_cos = index < HALF // 2
    return np.stack([even, odd]), np.stack([even_is_cos, odd_is_cos])


def y_tables():
    freq, is_cos = y_frequencies()
    point = np.arange(HALF)
    angle = 2.0 * np.pi * (point[None, :, None] * freq[:, None, :] % NY) / NY
    forward = np.where(is_cos[:, None, :], np.cos(angle), np.sin(angle))
    weight = np.where((freq == 0) | (freq == NY // 2), 1.0 / NY, 2.0 / NY)
    backward = np.swapaxes(forward * weight[:, None, :], 1, 2)
    return forward, backward


def y_shifts():
    freq, _ = y_frequencies()
    return (4.0 * np.sin(np.pi * freq / NY) ** 2).astype(np.float32)


def slab_basis():
    index = np.arange(PLANES)
    basis = math.sqrt(2.0 / PLANES) * np.sin(np.pi * np.outer(index, index) / PLANES)
    basis[0, :] = 0.0
    basis[:, 0] = 0.0
    basis[0, 0] = 1.0
    return basis


def slab_shifts():
    return (4.0 * np.sin(np.pi * np.arange(PLANES) / (2 * PLANES)) ** 2).astype(np.float32)


def near_weights():
    weight = slab_basis()[1].copy()
    weight[0] = 0.0
    return weight.astype(np.float32)


def far_signs():
    return np.where(np.arange(PLANES) % 2 == 1, 1.0, -1.0).astype(np.float32)


def interface_tables():
    mode = np.arange(SLABS)
    freq = np.where(mode <= SLABS // 2, mode, mode - SLABS // 2)
    is_cos = mode <= SLABS // 2
    weight = np.where((freq == 0) | (freq == SLABS // 2), 1.0, 2.0) / SLABS / SLABS

    def basis(offset):
        angle = 2.0 * np.pi * ((np.arange(SLABS)[:, None] + offset) * freq[None, :] % SLABS) / SLABS
        return np.where(is_cos[None, :], np.cos(angle), np.sin(angle))

    forward = np.concatenate([np.tile(basis(0), (1, 4)), np.tile(basis(1), (1, 4))], axis=1)
    high, low = split_pair(forward)
    backward = np.concatenate([np.tile(basis(0) * weight, (1, 4)), np.tile(basis(1) * weight, (1, 4))], axis=0)
    alias = freq[None, None, :] + SLABS * (np.arange(8)[:, None, None] + 8 * np.arange(4)[None, :, None])
    alias = np.repeat(alias, PARTS, axis=0)
    alias_shift = 4.0 * np.sin(np.pi * alias / NX) ** 2
    return (
        np.concatenate([high, low, high], axis=0),
        backward.astype(np.float32),
        alias_shift.reshape(8 * PARTS, LANES).astype(np.float32),
    )


def fold_table():
    fold = np.zeros((2, LAYERS, LAYERS, 8), np.float32)
    for layer in range(LAYERS):
        fold[0, layer, layer, :] = 1.0
        fold[1, layer, layer, :] = far_signs()[:8]
    return fold.reshape(2 * LAYERS, 8 * LAYERS).astype(ml_dtypes.bfloat16)


def spread_tables():
    spread = np.zeros((CHIPS, LAYERS, CHIPS, 2, PARTS, LAYERS), np.float32)
    for chip in range(CHIPS):
        for layer in range(LAYERS):
            spread[chip, layer, chip, :, :, layer] = 1.0
    mask = np.zeros((PARTS, PLANES, 2, PARTS, LAYERS), np.float32)
    for part in range(PARTS):
        mask[part, :, 0, part, :] = near_weights()[:, None]
        mask[part, :, 1, part, :] = (near_weights() * far_signs())[:, None]
    return spread.reshape(NZ, CHIPS * LANES), mask.reshape(LANES, LANES)


class Column:
    def __init__(self, ref, which):
        self.ref, self.start = ref, which * NZ

    def __getitem__(self, layer):
        return self.ref[self.start + layer]


def columns_of(ref):
    return [Column(ref, which) for which in range(3)]


def split_values(values):
    high = values.astype(jnp.bfloat16)
    low = (values - high.astype(jnp.float32)).astype(jnp.bfloat16)
    return high, low


def dot_split(left, right, contract=((1,), (0,))):
    left_high, left_low = left
    right_high, right_low = right

    def dot(one, two):
        return lax.dot_general(one, two, (contract, ((), ())), preferred_element_type=jnp.float32)

    return dot(left_high, right_high) + (dot(left_high, right_low) + dot(left_low, right_high))


def dot_full(left, right, contract):
    return lax.dot_general(
        left, right, (contract, ((), ())), precision=highest, preferred_element_type=jnp.float32
    )


def split_kernel(place, charge, tables_high, tables_low, own, sent, table_high, table_low, held_charge, sems):
    copies = [pltpu.make_async_copy(charge.at[step], held_charge.at[step], sems.at[step]) for step in range(8)]
    copies.append(pltpu.make_async_copy(tables_high.at[place[0]], table_high, sems.at[8]))
    copies.append(pltpu.make_async_copy(tables_low.at[place[0]], table_low, sems.at[9]))
    for copy in copies:
        copy.start()
    sign = jnp.where(place[0] == 0, 1.0, -1.0)
    for step, copy in enumerate(copies[:8]):
        copy.wait()
        lower, upper = held_charge[step, :, :HALF], sign * held_charge[step, :, HALF:]
        own[step] = lower + upper
        sent[step] = lower - upper
    for copy in copies[8:]:
        copy.wait()


def widen(table):
    return jnp.concatenate([table[...]] * PARTS, axis=1)


def chip_pivots(place, shift_y, shift_col, coefficients, inverse):
    cell, face, screening = columns_of(coefficients)
    base = place[1] * LAYERS
    shifts = widen(shift_col) + shift_y[place[0]]
    previous = None
    for layer in range(1, LAYERS):
        below, above = face[base + layer - 1], face[base + layer]
        pivot = (below + above + screening[base + layer]) + cell[base + layer] * shifts
        if previous is not None:
            pivot = pivot - (below * below) * previous
        previous = 1.0 / pivot
        inverse[layer] = previous


def early_kernel(place, own, table_high, table_low, slab_high, slab_low, shift_y, shift_col, coefficients, inverse, modes):
    chip_pivots(place, shift_y, shift_col, coefficients, inverse)
    modes[...] = to_modes(own, table_high, table_low, slab_high, slab_low)


def to_modes(planes, table_high, table_low, slab_high, slab_low):
    values = planes[...].reshape(8 * PLANES, HALF)
    spectrum = dot_split(split_values(values), (table_high[...], table_low[...]))
    return dot_split((slab_high[...], slab_low[...]), split_values(spectrum)).reshape(8, PLANES, HALF)


def to_planes(modes, table_high, table_low, slab_high, slab_low):
    values = dot_split((slab_high[...], slab_low[...]), split_values(modes.reshape(8 * PLANES, HALF)))
    return dot_split(split_values(values), (table_high[...], table_low[...])).reshape(8, PLANES, HALF)


def stack_parts(values):
    return jnp.concatenate([values[:, part * LANES : (part + 1) * LANES] for part in range(PARTS)], axis=0).T


def unstack_parts(values):
    turned = values.T
    return jnp.concatenate([turned[part * PLANES : (part + 1) * PLANES] for part in range(PARTS)], axis=1)


def forward_kernel(place, own_modes, other, table_high, table_low, slab_high, slab_low, inverse, weights, fold, coefficients, kept, out, modes, part, folded, sems):
    core, base = place[0], place[1] * LAYERS
    cell, face, _ = columns_of(coefficients)
    copies = [pltpu.make_async_copy(own_modes, kept.at[pl.ds(core * 8, 8)], sems.at[0])]
    copies[0].start()
    modes[pl.ds(core * 8, 8)] = own_modes[...]
    modes[pl.ds((1 - core) * 8, 8)] = to_modes(other, table_high, table_low, slab_high, slab_low)
    far_half = pl.ds((1 - core) * 8, 8)
    copies.append(pltpu.make_async_copy(modes.at[far_half], kept.at[far_half], sems.at[1]))
    copies[1].start()
    value = None
    for layer in range(1, LAYERS):
        inv = inverse[layer]
        scaled = modes[layer] * inv
        value = scaled if value is None else scaled + (face[base + layer - 1] * inv) * value
        part[layer] = value
    weight = widen(weights)
    value = None
    folded[0:8] = jnp.zeros((8, HALF), jnp.float32)
    for layer in reversed(range(1, LAYERS)):
        value = part[layer] if value is None else part[layer] + (face[base + layer] * inverse[layer]) * value
        if layer == LAYERS - 1:
            out[pl.ds(1, PEERS, stride=ROWS), :] = stack_parts(face[base + layer] * value)
        weighted = weight * value
        total = (weighted[0:8] + weighted[8:16]) + (weighted[16:24] + weighted[24:32])
        folded[layer * 8 : (layer + 1) * 8] = total * cell[base + layer]
    out[pl.ds(0, PEERS, stride=ROWS), :] = stack_parts(modes[0] + face[base] * value)
    high, low = split_values(folded[...])
    sums = jnp.dot(fold[...], high, preferred_element_type=jnp.float32) + jnp.dot(fold[...], low, preferred_element_type=jnp.float32)
    planes = jnp.concatenate([modes[layer, 0:1] for layer in range(LAYERS)], axis=0)
    near = sums[:LAYERS] + planes
    far = sums[LAYERS:]
    blocks = [half[:, step * LANES : (step + 1) * LANES] for half in (near, far) for step in range(PARTS)]
    out[pl.ds(2, PEERS, stride=ROWS), :] = jnp.concatenate(blocks, axis=0).T
    out[pl.ds(3, PEERS, stride=ROWS), :] = jnp.zeros((PEERS, LANES), jnp.float32)
    for copy in copies:
        copy.wait()


def prepare_kernel(place, shift_y, alias_shift, mode_shift, spread, mask, tables_high, tables_low, coefficients, alias_inverse, response_high, response_low, corners, table_high, table_low, inverses, columns, scaled, held_high, held_low, sems):
    copies = [
        pltpu.make_async_copy(tables_high.at[place[0]], held_high, sems.at[0]),
        pltpu.make_async_copy(tables_low.at[place[0]], held_low, sems.at[1]),
    ]
    for copy in copies:
        copy.start()
    cell, face, screening = columns_of(coefficients)
    start = place[0] * HALF + place[3]
    values = [shift_y[start + part * PEERS] for part in range(PARTS)]
    sublane = lax.rem(lax.broadcasted_iota(jnp.int32, (8 * PARTS, LANES), 0), PARTS)
    alias = alias_shift[...]
    for part in range(PARTS):
        alias = alias + jnp.where(sublane == part, values[part], 0.0)
    lane = lax.broadcasted_iota(jnp.int32, (8, LANES), 1)
    mode = jnp.broadcast_to(mode_shift[...], (8, LANES))
    for part in range(PARTS):
        mode = mode + jnp.where(lax.div(lane, PLANES) == part, values[part], 0.0)
    shifts = jnp.concatenate([alias, mode], axis=0)
    row = lax.broadcasted_iota(jnp.int32, (8, LANES), 0)
    previous = None
    value = None
    for layer in range(NZ):
        below = face[layer - 1] if layer > 0 else face[NZ - 1]
        pivot = (below + face[layer] + screening[layer]) + cell[layer] * shifts
        if previous is not None:
            pivot = pivot - (below * below) * previous
        previous = 1.0 / pivot
        alias_inverse[layer] = previous[: 8 * PARTS]
        inv = previous[8 * PARTS :]
        inverses[layer] = inv
        fresh = jnp.where(row == layer // LAYERS, inv, 0.0) if layer % LAYERS == 0 else None
        if value is None:
            value = fresh
        else:
            value = (face[layer - 1] * inv) * value
            if fresh is not None:
                value = value + fresh
        columns[layer] = value
    value = None
    for layer in reversed(range(NZ)):
        value = columns[layer] if value is None else columns[layer] + (face[layer] * inverses[layer]) * value
        scaled[layer * 8 : (layer + 1) * 8] = cell[layer] * value
        if layer % LAYERS == 0:
            corners[layer // LAYERS] = value
    for copy in copies:
        copy.wait()
    copies = [pltpu.make_async_copy(held_high, table_high, sems.at[2]), pltpu.make_async_copy(held_low, table_low, sems.at[3])]
    for copy in copies:
        copy.start()
    weight = jnp.concatenate([mask[...]] * CHIPS, axis=1)
    for chip in range(CHIPS):
        column = scaled[pl.ds(chip, NZ, stride=8), :]
        response = dot_full(column, spread[...], ((0,), (0,))) * weight
        high, low = split_values(response)
        response_high[chip * LANES : (chip + 1) * LANES, :] = high
        response_low[chip * LANES : (chip + 1) * LANES, :] = low
    for copy in copies:
        copy.wait()


def interface_kernel(place, arrived, response_high, response_low, corners, alias_inverse, forward, backward, coefficients, out, source, part, solved):
    face = columns_of(coefficients)[1]

    def rows(chip, slot):
        return pl.ds(ROWS * chip + slot, SLABS, stride=ROWS * CHIPS)

    sides = []
    for chip in range(CHIPS):
        side = arrived[rows(chip, 0), :]
        sides.append(side + arrived[rows(chip - 1, 1), :] if chip > 0 else side)
    response = (response_high[...], response_low[...])
    sums = dot_split(split_values(jnp.concatenate(sides, axis=1)), response)
    sums = sums + jnp.concatenate([arrived[rows(chip, 2), :] for chip in range(CHIPS)], axis=1)
    high, low = split_values(sums)
    stacked = jnp.concatenate([high, high, low], axis=0)
    turned = lax.dot_general(stacked, forward[...], (((0,), (0,)), ((), ())), preferred_element_type=jnp.float32)
    half = PARTS * LAYERS
    for chip in range(CHIPS):
        at = chip * LANES
        source[chip * half : (chip + 1) * half, :] = turned[at : at + half, :LANES] + turned[at + half : at + LANES, LANES:]
    value = None
    for layer in range(NZ):
        inv = alias_inverse[layer]
        first = (layer // LAYERS) * half + layer % LAYERS
        row = source[pl.ds(first, PARTS, stride=LAYERS), :]
        row = jnp.concatenate([row] * 8, axis=0)
        scaled = row * inv
        value = scaled if value is None else scaled + (face[layer - 1] * inv) * value
        part[layer] = value
    value = None
    for layer in reversed(range(NZ)):
        value = part[layer] if value is None else part[layer] + (face[layer] * alias_inverse[layer]) * value
        first = (layer // LAYERS) * half + layer % LAYERS
        total = (value[0:8] + value[8:16]) + (value[16:24] + value[24:32])
        solved[pl.ds(first, PARTS, stride=LAYERS), :] = total[:PARTS] + total[PARTS:]
    planes = dot_full(backward[...], solved[...], ((1,), (1,)))
    own = []
    for chip in range(CHIPS):
        at = chip * half
        own.append(jnp.concatenate([planes[:SLABS, at : at + half], planes[SLABS:, at : at + half]], axis=1))
    change = dot_split(split_values(jnp.concatenate(own, axis=1)), response, ((1,), (1,)))
    ends = []
    for chip in range(CHIPS):
        end = change[:, chip * LANES : (chip + 1) * LANES]
        for other in range(CHIPS):
            end = end + corners[chip, other : other + 1, :] * sides[other]
        ends.append(end)
    nothing = jnp.zeros((SLABS, LANES), jnp.float32)
    ends.append(nothing)
    for chip in range(CHIPS):
        out[rows(chip, 0), :] = ends[chip]
        out[rows(chip, 1), :] = ends[chip + 1]
        out[rows(chip, 2), :] = own[chip]
        out[rows(chip, 3), :] = nothing


def second_solve_kernel(place, modes, arrived, shift_y, shift_col, weights, signs, table_high, table_low, slab_high, slab_low, coefficients, kept, sent, part, near, edge, inverse):
    core, base = place[0], place[1] * LAYERS
    cell, face, _ = columns_of(coefficients)
    chip_pivots(place, shift_y, shift_col, coefficients, inverse)
    below = unstack_parts(arrived[pl.ds(0, PEERS, stride=ROWS), :])
    above = unstack_parts(arrived[pl.ds(1, PEERS, stride=ROWS), :])
    turned = arrived[pl.ds(2, PEERS, stride=ROWS), :].T
    for which, target in enumerate((near, edge)):
        for step in range(PARTS):
            at = (which * PARTS + step) * LAYERS
            target[:, step * LANES : (step + 1) * LANES] = turned[at : at + LAYERS]
    weight = widen(weights)
    signed = widen(signs)
    keep = lax.broadcasted_iota(jnp.int32, (PLANES, HALF), 0) == 0
    value = None
    for layer in range(1, LAYERS):
        inv = inverse[layer]
        both = (near[layer : layer + 1, :] * weight + edge[layer : layer + 1, :] * signed) * cell[base + layer]
        right = modes[layer] + both
        if layer == 1:
            right = right + face[base] * below
        if layer == LAYERS - 1:
            right = right + face[base + layer] * above
        scaled = right * inv
        value = scaled if value is None else scaled + (face[base + layer - 1] * inv) * value
        part[layer] = value
    value = None
    for layer in reversed(range(1, LAYERS)):
        value = part[layer] if value is None else part[layer] + (face[base + layer] * inverse[layer]) * value
        part[layer] = jnp.where(keep, near[layer : layer + 1, :], value)
    part[0] = jnp.where(keep, near[0:1, :], below)
    kept[...] = part[pl.ds(core * 8, 8)]
    sent[...] = to_planes(part[pl.ds((1 - core) * 8, 8)], table_high, table_low, slab_high, slab_low)


def backward_kernel(place, modes, table_high, table_low, slab_high, slab_low, out):
    out[...] = to_planes(modes[...], table_high, table_low, slab_high, slab_low)


held = pl.BlockSpec(memory_space=pltpu.VMEM)
far = pl.BlockSpec(memory_space=pl.ANY)
scalars = pl.BlockSpec(memory_space=pltpu.SMEM)
in_hbm = functools.partial(pltpu.with_memory_space_constraint, memory_space=pltpu.HBM)


def call(kernel, place, inputs, in_specs, outs, out_specs, scratch=(), grid=(), cost=10_000_000):
    return pl.pallas_call(
        kernel,
        grid=grid,
        in_specs=[scalars, *in_specs],
        out_specs=out_specs,
        out_shape=outs,
        scratch_shapes=scratch,
        compiler_params=pltpu.CompilerParams(vmem_limit_bytes=VMEM_LIMIT),
        cost_estimate=pl.CostEstimate(flops=cost, bytes_accessed=4_000_000, transcendentals=0),
    )(place, *inputs)


def body(charge, cell, face, screening):
    gx, gz = lax.axis_index("gx"), lax.axis_index("gz")
    core, chip = lax.rem(gz, 2), lax.div(gz, 2)
    place = jnp.stack([core, chip, 1 - core, gx * CHIPS + chip]).astype(jnp.int32)
    forward_y, backward_y = y_tables()
    fy_high, fy_low = split_pair(forward_y)
    by_high, by_low = split_pair(backward_y)
    slab_high, slab_low = split_pair(np.kron(np.eye(8), slab_basis()))
    forward_slab, backward_slab, alias_shift = interface_tables()
    spread, mask = spread_tables()
    weights = np.broadcast_to(near_weights()[:, None], (PLANES, LANES)).copy()
    signs = weights * far_signs()[:, None]
    shift_y = y_shifts()
    mode_shift = np.tile(slab_shifts(), PARTS)[None, :]

    cube = (8, PLANES, HALF)
    field = (LAYERS, PLANES, HALF)
    message = (ROWS * PEERS, LANES)
    square = (CHIPS * LANES, CHIPS * LANES)
    table = pltpu.VMEM((HALF, HALF), jnp.bfloat16)
    far_table = pltpu.HBM((HALF, HALF), jnp.bfloat16)
    groups = [[x * 2 * CHIPS + 2 * c + r for x in range(SLABS) for c in range(CHIPS)] for r in range(2)]

    def vmem(*shape):
        return pltpu.VMEM(shape, jnp.float32)

    def exchange(values):
        blocks = values.reshape(PEERS, ROWS, LANES)
        return lax.all_to_all(blocks, ("gx", "gz"), 0, 0, axis_index_groups=groups, tiled=True).reshape(message)

    pair = [(s, s ^ 1) for s in range(2 * CHIPS)]
    lines = vmem(8, PLANES, NY)
    own, sent, table_high, table_low = call(
        split_kernel,
        place,
        (in_hbm(charge), in_hbm(fy_high), in_hbm(fy_low)),
        [far] * 3,
        [vmem(*cube), vmem(*cube), table, table],
        [held] * 4,
        [lines, pltpu.SemaphoreType.DMA((10,))],
    )
    other = lax.ppermute(sent, "gz", pair)
    shifts = (shift_y[:, None, :], np.broadcast_to(slab_shifts()[:, None], (PLANES, LANES)).copy())
    coefficients = jnp.concatenate([cell, face, screening])
    inverse, own_modes = call(
        early_kernel,
        place,
        (own, table_high, table_low, slab_high, slab_low, *shifts, coefficients),
        [held] * 7 + [scalars],
        [vmem(*field), vmem(*cube)],
        [held] * 2,
    )
    modes, ends = call(
        forward_kernel,
        place,
        (own_modes, other, table_high, table_low, slab_high, slab_low, inverse, weights, fold_table(), coefficients),
        [held] * 9 + [scalars],
        [pltpu.HBM(field, jnp.float32), pltpu.HBM(message, jnp.float32)],
        [far, held],
        [vmem(*field), vmem(*field), vmem(8 * LAYERS, HALF), pltpu.SemaphoreType.DMA((2,))],
    )
    alias_inverse, response_high, response_low, corners, table_high, table_low = call(
        prepare_kernel,
        place,
        (shift_y.reshape(-1), alias_shift, mode_shift, spread, mask, in_hbm(by_high), in_hbm(by_low), coefficients),
        [scalars] + [held] * 4 + [far] * 2 + [scalars],
        [vmem(NZ, 8 * PARTS, LANES), pltpu.VMEM(square, jnp.bfloat16), pltpu.VMEM(square, jnp.bfloat16), vmem(CHIPS, 8, LANES), far_table, far_table],
        [held] * 4 + [far] * 2,
        [vmem(NZ, 8, LANES), vmem(NZ, 8, LANES), vmem(8 * NZ, LANES), table, table, pltpu.SemaphoreType.DMA((4,))],
    )
    ends = exchange(ends)
    ends = call(
        interface_kernel,
        place,
        (ends, response_high, response_low, corners, alias_inverse, forward_slab, backward_slab, coefficients),
        [held] * 7 + [scalars],
        vmem(*message),
        held,
        [vmem(CHIPS * PARTS * LAYERS, LANES), vmem(NZ, 8 * PARTS, LANES), vmem(CHIPS * PARTS * LAYERS, LANES)],
    )
    ends = exchange(ends)
    kept, sent = call(
        second_solve_kernel,
        place,
        (modes, ends, *shifts, weights, signs, table_high, table_low, slab_high, slab_low, coefficients),
        [held] * 10 + [scalars],
        [vmem(*cube), vmem(*cube)],
        [held] * 2,
        [vmem(*field), vmem(LAYERS, HALF), vmem(LAYERS, HALF), vmem(*field)],
    )
    other = lax.ppermute(sent, "gz", pair)
    kept = call(backward_kernel, place, (kept, table_high, table_low, slab_high, slab_low), [held] * 5, vmem(*cube), held)
    sign = jnp.where(core == 0, 1.0, -1.0)
    return jnp.concatenate([kept + other, sign * (kept - other)], axis=2)


def solution(mesh):
    in_specs = (P("gz", "gx", None), P(), P(), P())
    out_specs = P("gz", "gx", None)
    return jax.shard_map(body, mesh=mesh, in_specs=in_specs, out_specs=out_specs, check_vma=False)
```

```python
import functools
import math

import jax
import jax.numpy as jnp
import ml_dtypes
import numpy as np
from jax import lax
from jax.experimental import pallas as pl
from jax.experimental.pallas import tpu as pltpu
from jax.sharding import PartitionSpec as P

NX, NY, NZ = 1024, 1024, 64
SLABS, PLANES = 32, 32
HALF = NY // 2
CHIPS = 4
LAYERS = NZ // CHIPS
PEERS = SLABS * CHIPS
PARTS = 4
ROWS = 4
LANES = 128
highest = lax.Precision.HIGHEST
VMEM_LIMIT = 48 * 1024 * 1024


def split_pair(table):
    high = table.astype(np.float32).astype(ml_dtypes.bfloat16)
    low = (table - high.astype(np.float64)).astype(np.float32).astype(ml_dtypes.bfloat16)
    return high, low


def y_frequencies():
    index = np.arange(HALF)
    even = np.where(index <= HALF // 2, 2 * index, 2 * (index - HALF // 2))
    odd = np.where(index < HALF // 2, 2 * index + 1, 2 * (index - HALF // 2) + 1)
    even_is_cos = index <= HALF // 2
    odd_is_cos = index < HALF // 2
    return np.stack([even, odd]), np.stack([even_is_cos, odd_is_cos])


def y_tables():
    freq, is_cos = y_frequencies()
    point = np.arange(HALF)
    angle = 2.0 * np.pi * (point[None, :, None] * freq[:, None, :] % NY) / NY
    forward = np.where(is_cos[:, None, :], np.cos(angle), np.sin(angle))
    weight = np.where((freq == 0) | (freq == NY // 2), 1.0 / NY, 2.0 / NY)
    backward = np.swapaxes(forward * weight[:, None, :], 1, 2)
    return forward, backward


def y_shifts():
    freq, _ = y_frequencies()
    return (4.0 * np.sin(np.pi * freq / NY) ** 2).astype(np.float32)


def slab_basis():
    index = np.arange(PLANES)
    basis = math.sqrt(2.0 / PLANES) * np.sin(np.pi * np.outer(index, index) / PLANES)
    basis[0, :] = 0.0
    basis[:, 0] = 0.0
    basis[0, 0] = 1.0
    return basis


def slab_shifts():
    return (4.0 * np.sin(np.pi * np.arange(PLANES) / (2 * PLANES)) ** 2).astype(np.float32)


def near_weights():
    weight = slab_basis()[1].copy()
    weight[0] = 0.0
    return weight.astype(np.float32)


def far_signs():
    return np.where(np.arange(PLANES) % 2 == 1, 1.0, -1.0).astype(np.float32)


def interface_tables():
    mode = np.arange(SLABS)
    freq = np.where(mode <= SLABS // 2, mode, mode - SLABS // 2)
    is_cos = mode <= SLABS // 2
    weight = np.where((freq == 0) | (freq == SLABS // 2), 1.0, 2.0) / SLABS / SLABS

    def basis(offset):
        angle = 2.0 * np.pi * ((np.arange(SLABS)[:, None] + offset) * freq[None, :] % SLABS) / SLABS
        return np.where(is_cos[None, :], np.cos(angle), np.sin(angle))

    forward = np.concatenate([np.tile(basis(0), (1, 4)), np.tile(basis(1), (1, 4))], axis=1)
    high, low = split_pair(forward)
    backward = np.concatenate([np.tile(basis(0) * weight, (1, 4)), np.tile(basis(1) * weight, (1, 4))], axis=0)
    alias = freq[None, None, :] + SLABS * (np.arange(8)[:, None, None] + 8 * np.arange(4)[None, :, None])
    alias = np.repeat(alias, PARTS, axis=0)
    alias_shift = 4.0 * np.sin(np.pi * alias / NX) ** 2
    return (
        np.concatenate([high, low, high], axis=0),
        backward.astype(np.float32),
        alias_shift.reshape(8 * PARTS, LANES).astype(np.float32),
    )


def fold_table():
    fold = np.zeros((2, LAYERS, LAYERS, 8), np.float32)
    for layer in range(LAYERS):
        fold[0, layer, layer, :] = 1.0
        fold[1, layer, layer, :] = far_signs()[:8]
    return fold.reshape(2 * LAYERS, 8 * LAYERS).astype(ml_dtypes.bfloat16)


def spread_tables():
    spread = np.zeros((CHIPS, LAYERS, CHIPS, 2, PARTS, LAYERS), np.float32)
    for chip in range(CHIPS):
        for layer in range(LAYERS):
            spread[chip, layer, chip, :, :, layer] = 1.0
    mask = np.zeros((PARTS, PLANES, 2, PARTS, LAYERS), np.float32)
    for part in range(PARTS):
        mask[part, :, 0, part, :] = near_weights()[:, None]
        mask[part, :, 1, part, :] = (near_weights() * far_signs())[:, None]
    return spread.reshape(NZ, CHIPS * LANES), mask.reshape(LANES, LANES)


def position():
    gz = lax.axis_index("gz")
    core, chip = lax.rem(gz, 2), lax.div(gz, 2)
    return core, chip, lax.axis_index("gx") * CHIPS + chip


class Column:
    def __init__(self, ref, which, repeat):
        self.ref, self.start, self.repeat = ref, which * NZ, repeat

    def __getitem__(self, layer):
        row = self.ref[pl.ds(self.start + layer, 1), :]
        return jnp.concatenate([row] * self.repeat, axis=1)


def columns_of(ref, repeat=1):
    return [Column(ref, which, repeat) for which in range(3)]


def split_values(values):
    high = values.astype(jnp.bfloat16)
    low = (values - high.astype(jnp.float32)).astype(jnp.bfloat16)
    return high, low


def dot_split(left, right, contract=((1,), (0,))):
    left_high, left_low = left
    right_high, right_low = right

    def dot(one, two):
        return lax.dot_general(one, two, (contract, ((), ())), preferred_element_type=jnp.float32)

    return dot(left_high, right_high) + (dot(left_high, right_low) + dot(left_low, right_high))


def dot_full(left, right, contract):
    return lax.dot_general(
        left, right, (contract, ((), ())), precision=highest, preferred_element_type=jnp.float32
    )


def split_kernel(charge, tables_high, tables_low, cell, face, screening, own, sent, table_high, table_low, coefficients, lines, rows, sems):
    core, _, _ = position()
    copies = [pltpu.make_async_copy(source, rows.at[step], sems.at[10 + step]) for step, source in enumerate((cell, face, screening))]
    copies += [pltpu.make_async_copy(charge.at[step], lines.at[step], sems.at[step]) for step in range(8)]
    copies.append(pltpu.make_async_copy(tables_high.at[core], table_high, sems.at[8]))
    copies.append(pltpu.make_async_copy(tables_low.at[core], table_low, sems.at[9]))
    for copy in copies:
        copy.start()
    for step, copy in enumerate(copies[:3]):
        copy.wait()
        coefficients[step * NZ : (step + 1) * NZ, :] = jnp.broadcast_to(rows[step], (LANES, NZ)).T
    sign = jnp.where(core == 0, 1.0, -1.0)
    for step, copy in enumerate(copies[3:11]):
        copy.wait()
        lower, upper = lines[step, :, :HALF], sign * lines[step, :, HALF:]
        own[step] = lower + upper
        sent[step] = lower - upper
    for copy in copies[11:]:
        copy.wait()


def widen(table):
    return jnp.concatenate([table] * PARTS, axis=1)


def chip_pivots(shifts, coefficients, inverse):
    cell, face, screening = columns_of(coefficients, PARTS)
    core, chip, _ = position()
    base = chip * LAYERS
    row = jnp.concatenate([shifts[pl.ds(core * PARTS + part, 1), :] for part in range(PARTS)], axis=1)
    shifts = widen(shifts[8:]) + row
    previous = None
    for layer in range(1, LAYERS):
        below, above = face[base + layer - 1], face[base + layer]
        pivot = (below + above + screening[base + layer]) + cell[base + layer] * shifts
        if previous is not None:
            pivot = pivot - (below * below) * previous
        previous = 1.0 / pivot
        inverse[layer] = previous


def early_kernel(own, table_high, table_low, slab_high, slab_low, shifts, coefficients, inverse, modes):
    chip_pivots(shifts, coefficients, inverse)
    modes[...] = to_modes(own, table_high, table_low, slab_high, slab_low)


def to_modes(planes, table_high, table_low, slab_high, slab_low):
    values = planes[...].reshape(8 * PLANES, HALF)
    spectrum = dot_split(split_values(values), (table_high[...], table_low[...]))
    return dot_split((slab_high[...], slab_low[...]), split_values(spectrum)).reshape(8, PLANES, HALF)


def to_planes(modes, table_high, table_low, slab_high, slab_low):
    values = dot_split((slab_high[...], slab_low[...]), split_values(modes.reshape(8 * PLANES, HALF)))
    return dot_split(split_values(values), (table_high[...], table_low[...])).reshape(8, PLANES, HALF)


def stack_parts(values):
    return jnp.concatenate([values[:, part * LANES : (part + 1) * LANES] for part in range(PARTS)], axis=0).T


def unstack_parts(values):
    turned = values.T
    return jnp.concatenate([turned[part * PLANES : (part + 1) * PLANES] for part in range(PARTS)], axis=1)


def forward_kernel(own_modes, other, table_high, table_low, slab_high, slab_low, inverse, weights, fold, coefficients, modes, out, part, folded):
    core, chip, _ = position()
    base = chip * LAYERS
    cell, face, _ = columns_of(coefficients, PARTS)
    modes[pl.ds(core * 8, 8)] = own_modes[...]
    modes[pl.ds((1 - core) * 8, 8)] = to_modes(other, table_high, table_low, slab_high, slab_low)
    value = None
    for layer in range(1, LAYERS):
        inv = inverse[layer]
        scaled = modes[layer] * inv
        value = scaled if value is None else scaled + (face[base + layer - 1] * inv) * value
        part[layer] = value
    weight = widen(weights[:PLANES])
    value = None
    folded[0:8] = jnp.zeros((8, HALF), jnp.float32)
    for layer in reversed(range(1, LAYERS)):
        value = part[layer] if value is None else part[layer] + (face[base + layer] * inverse[layer]) * value
        if layer == LAYERS - 1:
            out[pl.ds(1, PEERS, stride=ROWS), :] = stack_parts(face[base + layer] * value)
        weighted = weight * value
        total = (weighted[0:8] + weighted[8:16]) + (weighted[16:24] + weighted[24:32])
        folded[layer * 8 : (layer + 1) * 8] = total * cell[base + layer]
    out[pl.ds(0, PEERS, stride=ROWS), :] = stack_parts(modes[0] + face[base] * value)
    high, low = split_values(folded[...])
    sums = jnp.dot(fold[...], high, preferred_element_type=jnp.float32) + jnp.dot(fold[...], low, preferred_element_type=jnp.float32)
    planes = jnp.concatenate([modes[layer, 0:1] for layer in range(LAYERS)], axis=0)
    near = sums[:LAYERS] + planes
    far = sums[LAYERS:]
    blocks = [half[:, step * LANES : (step + 1) * LANES] for half in (near, far) for step in range(PARTS)]
    out[pl.ds(2, PEERS, stride=ROWS), :] = jnp.concatenate(blocks, axis=0).T
    out[pl.ds(3, PEERS, stride=ROWS), :] = jnp.zeros((PEERS, LANES), jnp.float32)


def keep_kernel(modes, kept, sem):
    copy = pltpu.make_async_copy(modes, kept, sem)
    copy.start()
    copy.wait()


def prepare_kernel(modes, shifts, alias_shift, mode_shift, spread, mask, tables_high, tables_low, coefficients, alias_inverse, response_high, response_low, corners, table_high, table_low, inverses, columns, scaled, held_high, held_low, sems):
    core, _, peer = position()
    copies = [
        pltpu.make_async_copy(tables_high.at[core], held_high, sems.at[0]),
        pltpu.make_async_copy(tables_low.at[core], held_low, sems.at[1]),
    ]
    for copy in copies:
        copy.start()
    cell, face, screening = columns_of(coefficients)
    lane = lax.broadcasted_iota(jnp.int32, (PARTS, LANES), 1)
    values = jnp.sum(jnp.where(lane == peer, shifts[pl.ds(core * PARTS, PARTS), :], 0.0), axis=1, keepdims=True)
    alias = alias_shift[...] + jnp.concatenate([values] * 8, axis=0)
    lane = lax.broadcasted_iota(jnp.int32, (8, LANES), 1)
    mode = jnp.broadcast_to(mode_shift[...], (8, LANES))
    for part in range(PARTS):
        mode = mode + jnp.where(lax.div(lane, PLANES) == part, values[part : part + 1], 0.0)
    shifts = jnp.concatenate([alias, mode], axis=0)
    row = lax.broadcasted_iota(jnp.int32, (8, LANES), 0)
    previous = None
    value = None
    for layer in range(NZ):
        below = face[layer - 1] if layer > 0 else face[NZ - 1]
        pivot = (below + face[layer] + screening[layer]) + cell[layer] * shifts
        if previous is not None:
            pivot = pivot - (below * below) * previous
        previous = 1.0 / pivot
        alias_inverse[layer] = previous[: 8 * PARTS]
        inv = previous[8 * PARTS :]
        inverses[layer] = inv
        fresh = jnp.where(row == layer // LAYERS, inv, 0.0) if layer % LAYERS == 0 else None
        if value is None:
            value = fresh
        else:
            value = (face[layer - 1] * inv) * value
            if fresh is not None:
                value = value + fresh
        columns[layer] = value
    value = None
    for layer in reversed(range(NZ)):
        value = columns[layer] if value is None else columns[layer] + (face[layer] * inverses[layer]) * value
        scaled[layer * 8 : (layer + 1) * 8] = cell[layer] * value
        if layer % LAYERS == 0:
            corners[layer // LAYERS] = value
    for copy in copies:
        copy.wait()
    copies = [pltpu.make_async_copy(held_high, table_high, sems.at[2]), pltpu.make_async_copy(held_low, table_low, sems.at[3])]
    for copy in copies:
        copy.start()
    weight = jnp.concatenate([mask[...]] * CHIPS, axis=1)
    for chip in range(CHIPS):
        column = scaled[pl.ds(chip, NZ, stride=8), :]
        response = dot_full(column, spread[...], ((0,), (0,))) * weight
        high, low = split_values(response)
        response_high[chip * LANES : (chip + 1) * LANES, :] = high
        response_low[chip * LANES : (chip + 1) * LANES, :] = low
    for copy in copies:
        copy.wait()


def interface_kernel(arrived, response_high, response_low, corners, alias_inverse, forward, backward, coefficients, out, source, part, solved):
    face = columns_of(coefficients)[1]

    def rows(chip, slot):
        return pl.ds(ROWS * chip + slot, SLABS, stride=ROWS * CHIPS)

    sides = []
    for chip in range(CHIPS):
        side = arrived[rows(chip, 0), :]
        sides.append(side + arrived[rows(chip - 1, 1), :] if chip > 0 else side)
    response = (response_high[...], response_low[...])
    sums = dot_split(split_values(jnp.concatenate(sides, axis=1)), response)
    sums = sums + jnp.concatenate([arrived[rows(chip, 2), :] for chip in range(CHIPS)], axis=1)
    high, low = split_values(sums)
    stacked = jnp.concatenate([high, high, low], axis=0)
    turned = lax.dot_general(stacked, forward[...], (((0,), (0,)), ((), ())), preferred_element_type=jnp.float32)
    half = PARTS * LAYERS
    for chip in range(CHIPS):
        at = chip * LANES
        source[chip * half : (chip + 1) * half, :] = turned[at : at + half, :LANES] + turned[at + half : at + LANES, LANES:]
    value = None
    for layer in range(NZ):
        inv = alias_inverse[layer]
        first = (layer // LAYERS) * half + layer % LAYERS
        row = source[pl.ds(first, PARTS, stride=LAYERS), :]
        row = jnp.concatenate([row] * 8, axis=0)
        scaled = row * inv
        value = scaled if value is None else scaled + (face[layer - 1] * inv) * value
        part[layer] = value
    value = None
    for layer in reversed(range(NZ)):
        value = part[layer] if value is None else part[layer] + (face[layer] * alias_inverse[layer]) * value
        first = (layer // LAYERS) * half + layer % LAYERS
        total = (value[0:8] + value[8:16]) + (value[16:24] + value[24:32])
        solved[pl.ds(first, PARTS, stride=LAYERS), :] = total[:PARTS] + total[PARTS:]
    planes = dot_full(backward[...], solved[...], ((1,), (1,)))
    own = []
    for chip in range(CHIPS):
        at = chip * half
        own.append(jnp.concatenate([planes[:SLABS, at : at + half], planes[SLABS:, at : at + half]], axis=1))
    change = dot_split(split_values(jnp.concatenate(own, axis=1)), response, ((1,), (1,)))
    ends = []
    for chip in range(CHIPS):
        end = change[:, chip * LANES : (chip + 1) * LANES]
        for other in range(CHIPS):
            end = end + corners[chip, other : other + 1, :] * sides[other]
        ends.append(end)
    nothing = jnp.zeros((SLABS, LANES), jnp.float32)
    ends.append(nothing)
    for chip in range(CHIPS):
        out[rows(chip, 0), :] = ends[chip]
        out[rows(chip, 1), :] = ends[chip + 1]
        out[rows(chip, 2), :] = own[chip]
        out[rows(chip, 3), :] = nothing


def second_solve_kernel(modes, arrived, shifts, weights, table_high, table_low, slab_high, slab_low, coefficients, kept, sent, part, near, edge, inverse):
    core, chip, _ = position()
    base = chip * LAYERS
    cell, face, _ = columns_of(coefficients, PARTS)
    chip_pivots(shifts, coefficients, inverse)
    below = unstack_parts(arrived[pl.ds(0, PEERS, stride=ROWS), :])
    above = unstack_parts(arrived[pl.ds(1, PEERS, stride=ROWS), :])
    turned = arrived[pl.ds(2, PEERS, stride=ROWS), :].T
    for which, target in enumerate((near, edge)):
        for step in range(PARTS):
            at = (which * PARTS + step) * LAYERS
            target[:, step * LANES : (step + 1) * LANES] = turned[at : at + LAYERS]
    weight = widen(weights[:PLANES])
    signed = widen(weights[PLANES:])
    keep = lax.broadcasted_iota(jnp.int32, (PLANES, HALF), 0) == 0
    value = None
    for layer in range(1, LAYERS):
        inv = inverse[layer]
        both = (near[layer : layer + 1, :] * weight + edge[layer : layer + 1, :] * signed) * cell[base + layer]
        right = modes[layer] + both
        if layer == 1:
            right = right + face[base] * below
        if layer == LAYERS - 1:
            right = right + face[base + layer] * above
        scaled = right * inv
        value = scaled if value is None else scaled + (face[base + layer - 1] * inv) * value
        part[layer] = value
    value = None
    for layer in reversed(range(1, LAYERS)):
        value = part[layer] if value is None else part[layer] + (face[base + layer] * inverse[layer]) * value
        part[layer] = jnp.where(keep, near[layer : layer + 1, :], value)
    part[0] = jnp.where(keep, near[0:1, :], below)
    kept[...] = part[pl.ds(core * 8, 8)]
    sent[...] = to_planes(part[pl.ds((1 - core) * 8, 8)], table_high, table_low, slab_high, slab_low)


def backward_kernel(modes, table_high, table_low, slab_high, slab_low, out):
    out[...] = to_planes(modes[...], table_high, table_low, slab_high, slab_low)


def join_kernel(kept, other, out, lines, sems):
    core, _, _ = position()
    sign = jnp.where(core == 0, 1.0, -1.0)
    copies = []
    for step in range(4):
        at = slice(2 * step, 2 * step + 2)
        one, two = kept[at], other[at]
        lines[at, :, :HALF] = one + two
        lines[at, :, HALF:] = sign * (one - two)
        copies.append(pltpu.make_async_copy(lines.at[pl.ds(2 * step, 2)], out.at[pl.ds(2 * step, 2)], sems.at[step]))
        copies[-1].start()
    for copy in copies:
        copy.wait()


held = pl.BlockSpec(memory_space=pltpu.VMEM)
far = pl.BlockSpec(memory_space=pl.ANY)
in_hbm = functools.partial(pltpu.with_memory_space_constraint, memory_space=pltpu.HBM)


def call(kernel, inputs, in_specs, outs, out_specs, scratch=(), cost=10_000_000):
    return pl.pallas_call(
        kernel,
        in_specs=in_specs,
        out_specs=out_specs,
        out_shape=outs,
        scratch_shapes=scratch,
        compiler_params=pltpu.CompilerParams(vmem_limit_bytes=VMEM_LIMIT),
        cost_estimate=pl.CostEstimate(flops=cost, bytes_accessed=4_000_000, transcendentals=0),
    )(*inputs)


def body(charge, cell, face, screening):
    forward_y, backward_y = y_tables()
    fy_high, fy_low = split_pair(forward_y)
    by_high, by_low = split_pair(backward_y)
    slab_high, slab_low = split_pair(np.kron(np.eye(8), slab_basis()))
    forward_slab, backward_slab, alias_shift = interface_tables()
    spread, mask = spread_tables()
    weights = np.concatenate([near_weights(), near_weights() * far_signs()])
    weights = np.broadcast_to(weights[:, None], (2 * PLANES, LANES)).copy()
    shift_y = y_shifts()
    mode_shift = np.tile(slab_shifts(), PARTS)[None, :]

    cube = (8, PLANES, HALF)
    field = (LAYERS, PLANES, HALF)
    message = (ROWS * PEERS, LANES)
    square = (CHIPS * LANES, CHIPS * LANES)
    table = pltpu.VMEM((HALF, HALF), jnp.bfloat16)
    far_table = pltpu.HBM((HALF, HALF), jnp.bfloat16)
    groups = [[x * 2 * CHIPS + 2 * c + r for x in range(SLABS) for c in range(CHIPS)] for r in range(2)]

    def vmem(*shape):
        return pltpu.VMEM(shape, jnp.float32)

    def exchange(values):
        blocks = values.reshape(PEERS, ROWS, LANES)
        return lax.all_to_all(blocks, ("gx", "gz"), 0, 0, axis_index_groups=groups, tiled=True).reshape(message)

    pair = [(s, s ^ 1) for s in range(2 * CHIPS)]
    lines = vmem(8, PLANES, NY)
    coefficient_rows = [in_hbm(array.reshape(1, NZ)) for array in (cell, face, screening)]
    own, sent, table_high, table_low, coefficients = call(
        split_kernel,
        (in_hbm(charge), in_hbm(fy_high), in_hbm(fy_low), *coefficient_rows),
        [far] * 6,
        [vmem(*cube), vmem(*cube), table, table, vmem(3 * NZ, LANES)],
        [held] * 5,
        [lines, vmem(3, 1, NZ), pltpu.SemaphoreType.DMA((13,))],
    )
    other = lax.ppermute(sent, "gz", pair)
    shifts = np.concatenate([shift_y.reshape(2 * PARTS, LANES), np.broadcast_to(slab_shifts()[:, None], (PLANES, LANES))])
    inverse, own_modes = call(
        early_kernel,
        (own, table_high, table_low, slab_high, slab_low, shifts, coefficients),
        [held] * 7,
        [vmem(*field), vmem(*cube)],
        [held] * 2,
    )
    modes, ends = call(
        forward_kernel,
        (own_modes, other, table_high, table_low, slab_high, slab_low, inverse, weights, fold_table(), coefficients),
        [held] * 10,
        [vmem(*field), pltpu.HBM(message, jnp.float32)],
        [held] * 2,
        [vmem(*field), vmem(8 * LAYERS, HALF)],
    )
    modes = call(keep_kernel, (modes,), [held], pltpu.HBM(field, jnp.float32), far, [pltpu.SemaphoreType.DMA])
    alias_inverse, response_high, response_low, corners, table_high, table_low = call(
        prepare_kernel,
        (in_hbm(modes), shifts, alias_shift, mode_shift, spread, mask, in_hbm(by_high), in_hbm(by_low), coefficients),
        [far] + [held] * 5 + [far] * 2 + [held],
        [vmem(NZ, 8 * PARTS, LANES), pltpu.VMEM(square, jnp.bfloat16), pltpu.VMEM(square, jnp.bfloat16), vmem(CHIPS, 8, LANES)]
        + [far_table, far_table],
        [held] * 4 + [far] * 2,
        [vmem(NZ, 8, LANES), vmem(NZ, 8, LANES), vmem(8 * NZ, LANES), table, table, pltpu.SemaphoreType.DMA((4,))],
    )
    ends = exchange(ends)
    ends = call(
        interface_kernel,
        (ends, response_high, response_low, corners, alias_inverse, forward_slab, backward_slab, coefficients),
        [held] * 8,
        vmem(*message),
        held,
        [vmem(CHIPS * PARTS * LAYERS, LANES), vmem(NZ, 8 * PARTS, LANES), vmem(CHIPS * PARTS * LAYERS, LANES)],
    )
    ends = exchange(ends)
    kept, sent = call(
        second_solve_kernel,
        (modes, ends, shifts, weights, table_high, table_low, slab_high, slab_low, coefficients),
        [held] * 9,
        [vmem(*cube), vmem(*cube)],
        [held] * 2,
        [vmem(*field), vmem(LAYERS, HALF), vmem(LAYERS, HALF), vmem(*field)],
    )
    other = lax.ppermute(sent, "gz", pair)
    kept = call(backward_kernel, (kept, table_high, table_low, slab_high, slab_low), [held] * 5, vmem(*cube), held)
    return call(
        join_kernel, (kept, other), [held] * 2, pltpu.HBM((8, PLANES, NY), jnp.float32), far, [lines, pltpu.SemaphoreType.DMA((4,))]
    )


def solution(mesh):
    in_specs = (P("gz", "gx", None), P(), P(), P())
    out_specs = P("gz", "gx", None)
    return jax.shard_map(body, mesh=mesh, in_specs=in_specs, out_specs=out_specs, check_vma=False)
```

```python
import functools
import math

import jax
import jax.numpy as jnp
import ml_dtypes
import numpy as np
from jax import lax
from jax.experimental import pallas as pl
from jax.experimental.pallas import tpu as pltpu
from jax.sharding import PartitionSpec as P

NX, NY, NZ = 1024, 1024, 64
SLABS, PLANES = 32, 32
HALF = NY // 2
CHIPS = 4
LAYERS = NZ // CHIPS
PEERS = SLABS * CHIPS
PARTS = 4
ROWS = 4
LANES = 128
highest = lax.Precision.HIGHEST
VMEM_LIMIT = 48 * 1024 * 1024


def split_pair(table):
    high = table.astype(np.float32).astype(ml_dtypes.bfloat16)
    low = (table - high.astype(np.float64)).astype(np.float32).astype(ml_dtypes.bfloat16)
    return high, low


def y_frequencies():
    index = np.arange(HALF)
    even = np.where(index <= HALF // 2, 2 * index, 2 * (index - HALF // 2))
    odd = np.where(index < HALF // 2, 2 * index + 1, 2 * (index - HALF // 2) + 1)
    even_is_cos = index <= HALF // 2
    odd_is_cos = index < HALF // 2
    return np.stack([even, odd]), np.stack([even_is_cos, odd_is_cos])


def y_tables():
    freq, is_cos = y_frequencies()
    point = np.arange(HALF)
    angle = 2.0 * np.pi * (point[None, :, None] * freq[:, None, :] % NY) / NY
    forward = np.where(is_cos[:, None, :], np.cos(angle), np.sin(angle))
    weight = np.where((freq == 0) | (freq == NY // 2), 1.0 / NY, 2.0 / NY)
    backward = np.swapaxes(forward * weight[:, None, :], 1, 2)
    return forward, backward


def y_shifts():
    freq, _ = y_frequencies()
    return (4.0 * np.sin(np.pi * freq / NY) ** 2).astype(np.float32)


def slab_basis():
    index = np.arange(PLANES)
    basis = math.sqrt(2.0 / PLANES) * np.sin(np.pi * np.outer(index, index) / PLANES)
    basis[0, :] = 0.0
    basis[:, 0] = 0.0
    basis[0, 0] = 1.0
    return basis


def slab_shifts():
    return (4.0 * np.sin(np.pi * np.arange(PLANES) / (2 * PLANES)) ** 2).astype(np.float32)


def near_weights():
    weight = slab_basis()[1].copy()
    weight[0] = 0.0
    return weight.astype(np.float32)


def far_signs():
    return np.where(np.arange(PLANES) % 2 == 1, 1.0, -1.0).astype(np.float32)


def interface_tables():
    mode = np.arange(SLABS)
    freq = np.where(mode <= SLABS // 2, mode, mode - SLABS // 2)
    is_cos = mode <= SLABS // 2
    weight = np.where((freq == 0) | (freq == SLABS // 2), 1.0, 2.0) / SLABS / SLABS

    def basis(offset):
        angle = 2.0 * np.pi * ((np.arange(SLABS)[:, None] + offset) * freq[None, :] % SLABS) / SLABS
        return np.where(is_cos[None, :], np.cos(angle), np.sin(angle))

    forward = np.concatenate([np.tile(basis(0), (1, 4)), np.tile(basis(1), (1, 4))], axis=1)
    high, low = split_pair(forward)
    backward = np.concatenate([np.tile(basis(0) * weight, (1, 4)), np.tile(basis(1) * weight, (1, 4))], axis=0)
    alias = freq[None, None, :] + SLABS * (np.arange(8)[:, None, None] + 8 * np.arange(4)[None, :, None])
    alias = np.repeat(alias, PARTS, axis=0)
    alias_shift = 4.0 * np.sin(np.pi * alias / NX) ** 2
    return (
        np.concatenate([high, low, high], axis=0),
        backward.astype(np.float32),
        alias_shift.reshape(8 * PARTS, LANES).astype(np.float32),
    )


def fold_table():
    fold = np.zeros((2, LAYERS, LAYERS, 8), np.float32)
    for layer in range(LAYERS):
        fold[0, layer, layer, :] = 1.0
        fold[1, layer, layer, :] = far_signs()[:8]
    return fold.reshape(2 * LAYERS, 8 * LAYERS).astype(ml_dtypes.bfloat16)


def spread_tables():
    spread = np.zeros((CHIPS, LAYERS, CHIPS, 2, PARTS, LAYERS), np.float32)
    for chip in range(CHIPS):
        for layer in range(LAYERS):
            spread[chip, layer, chip, :, :, layer] = 1.0
    mask = np.zeros((PARTS, PLANES, 2, PARTS, LAYERS), np.float32)
    for part in range(PARTS):
        mask[part, :, 0, part, :] = near_weights()[:, None]
        mask[part, :, 1, part, :] = (near_weights() * far_signs())[:, None]
    return spread.reshape(NZ, CHIPS * LANES), mask.reshape(LANES, LANES)


def position():
    gz = lax.axis_index("gz")
    core, chip = lax.rem(gz, 2), lax.div(gz, 2)
    return core, chip, lax.axis_index("gx") * CHIPS + chip


class Column:
    def __init__(self, ref, which, repeat):
        self.ref, self.start, self.repeat = ref, which * NZ, repeat

    def __getitem__(self, layer):
        row = self.ref[pl.ds(self.start + layer, 1), :]
        return jnp.concatenate([row] * self.repeat, axis=1)


def columns_of(ref, repeat=1):
    return [Column(ref, which, repeat) for which in range(3)]


def split_values(values):
    high = values.astype(jnp.bfloat16)
    low = (values - high.astype(jnp.float32)).astype(jnp.bfloat16)
    return high, low


def dot_split(left, right, contract=((1,), (0,))):
    left_high, left_low = left
    right_high, right_low = right

    def dot(one, two):
        return lax.dot_general(one, two, (contract, ((), ())), preferred_element_type=jnp.float32)

    return dot(left_high, right_high) + (dot(left_high, right_low) + dot(left_low, right_high))


def dot_full(left, right, contract):
    return lax.dot_general(
        left, right, (contract, ((), ())), precision=highest, preferred_element_type=jnp.float32
    )


def split_kernel(charge, tables_high, cell, face, screening, own, sent, table_high, coefficients, lines, rows, sems):
    core, _, _ = position()
    copies = [pltpu.make_async_copy(source, rows.at[step], sems.at[9 + step]) for step, source in enumerate((cell, face, screening))]
    copies += [pltpu.make_async_copy(charge.at[step], lines.at[step], sems.at[step]) for step in range(8)]
    copies.append(pltpu.make_async_copy(tables_high.at[core], table_high, sems.at[8]))
    for copy in copies:
        copy.start()
    for step, copy in enumerate(copies[:3]):
        copy.wait()
        coefficients[step * NZ : (step + 1) * NZ, :] = jnp.broadcast_to(rows[step], (LANES, NZ)).T
    sign = jnp.where(core == 0, 1.0, -1.0)
    for step, copy in enumerate(copies[3:11]):
        copy.wait()
        lower, upper = lines[step, :, :HALF], sign * lines[step, :, HALF:]
        own[step] = lower + upper
        sent[step] = lower - upper
    for copy in copies[11:]:
        copy.wait()


def widen(table):
    return jnp.concatenate([table] * PARTS, axis=1)


def chip_pivots(shifts, coefficients, inverse):
    cell, face, screening = columns_of(coefficients, PARTS)
    core, chip, _ = position()
    base = chip * LAYERS
    row = jnp.concatenate([shifts[pl.ds(core * PARTS + part, 1), :] for part in range(PARTS)], axis=1)
    shifts = widen(shifts[8:]) + row
    previous = None
    for layer in range(1, LAYERS):
        below, above = face[base + layer - 1], face[base + layer]
        pivot = (below + above + screening[base + layer]) + cell[base + layer] * shifts
        if previous is not None:
            pivot = pivot - (below * below) * previous
        previous = 1.0 / pivot
        inverse[layer] = previous


def early_kernel(own, table_high, tables_low, slab_high, slab_low, shifts, coefficients, inverse, modes, table_low, sem):
    core, _, _ = position()
    copy = pltpu.make_async_copy(tables_low.at[core], table_low, sem)
    copy.start()
    chip_pivots(shifts, coefficients, inverse)
    high, low = split_values(own[...].reshape(8 * PLANES, HALF))
    dot = functools.partial(jnp.dot, preferred_element_type=jnp.float32)
    spectrum = dot(high, table_high[...]) + dot(low, table_high[...])
    copy.wait()
    spectrum = spectrum + dot(high, table_low[...])
    modes[...] = dot_split((slab_high[...], slab_low[...]), split_values(spectrum)).reshape(8, PLANES, HALF)


def to_modes(planes, table_high, table_low, slab_high, slab_low):
    values = planes[...].reshape(8 * PLANES, HALF)
    spectrum = dot_split(split_values(values), (table_high[...], table_low[...]))
    return dot_split((slab_high[...], slab_low[...]), split_values(spectrum)).reshape(8, PLANES, HALF)


def to_planes(modes, table_high, table_low, slab_high, slab_low):
    values = dot_split((slab_high[...], slab_low[...]), split_values(modes.reshape(8 * PLANES, HALF)))
    return dot_split(split_values(values), (table_high[...], table_low[...])).reshape(8, PLANES, HALF)


def stack_parts(values):
    return jnp.concatenate([values[:, part * LANES : (part + 1) * LANES] for part in range(PARTS)], axis=0).T


def unstack_parts(values):
    turned = values.T
    return jnp.concatenate([turned[part * PLANES : (part + 1) * PLANES] for part in range(PARTS)], axis=1)


def forward_kernel(own_modes, other, table_high, table_low, slab_high, slab_low, inverse, weights, fold, coefficients, modes, out, part, folded):
    core, chip, _ = position()
    base = chip * LAYERS
    cell, face, _ = columns_of(coefficients, PARTS)
    modes[pl.ds(core * 8, 8)] = own_modes[...]
    modes[pl.ds((1 - core) * 8, 8)] = to_modes(other, table_high, table_low, slab_high, slab_low)
    value = None
    for layer in range(1, LAYERS):
        inv = inverse[layer]
        scaled = modes[layer] * inv
        value = scaled if value is None else scaled + (face[base + layer - 1] * inv) * value
        part[layer] = value
    weight = widen(weights[:PLANES])
    value = None
    folded[0:8] = jnp.zeros((8, HALF), jnp.float32)
    for layer in reversed(range(1, LAYERS)):
        value = part[layer] if value is None else part[layer] + (face[base + layer] * inverse[layer]) * value
        if layer == LAYERS - 1:
            out[pl.ds(1, PEERS, stride=ROWS), :] = stack_parts(face[base + layer] * value)
        weighted = weight * value
        total = (weighted[0:8] + weighted[8:16]) + (weighted[16:24] + weighted[24:32])
        folded[layer * 8 : (layer + 1) * 8] = total * cell[base + layer]
    out[pl.ds(0, PEERS, stride=ROWS), :] = stack_parts(modes[0] + face[base] * value)
    high, low = split_values(folded[...])
    sums = jnp.dot(fold[...], high, preferred_element_type=jnp.float32) + jnp.dot(fold[...], low, preferred_element_type=jnp.float32)
    planes = jnp.concatenate([modes[layer, 0:1] for layer in range(LAYERS)], axis=0)
    near = sums[:LAYERS] + planes
    far = sums[LAYERS:]
    blocks = [half[:, step * LANES : (step + 1) * LANES] for half in (near, far) for step in range(PARTS)]
    out[pl.ds(2, PEERS, stride=ROWS), :] = jnp.concatenate(blocks, axis=0).T
    out[pl.ds(3, PEERS, stride=ROWS), :] = jnp.zeros((PEERS, LANES), jnp.float32)


def keep_kernel(modes, kept, sem):
    copy = pltpu.make_async_copy(modes, kept, sem)
    copy.start()
    copy.wait()


def prepare_kernel(modes, shifts, alias_shift, mode_shift, spread, mask, tables_high, tables_low, coefficients, alias_inverse, response_high, response_low, corners, table_high, table_low, inverses, columns, scaled, held_high, held_low, sems):
    core, _, peer = position()
    copies = [
        pltpu.make_async_copy(tables_high.at[core], held_high, sems.at[0]),
        pltpu.make_async_copy(tables_low.at[core], held_low, sems.at[1]),
    ]
    for copy in copies:
        copy.start()
    cell, face, screening = columns_of(coefficients)
    lane = lax.broadcasted_iota(jnp.int32, (PARTS, LANES), 1)
    values = jnp.sum(jnp.where(lane == peer, shifts[pl.ds(core * PARTS, PARTS), :], 0.0), axis=1, keepdims=True)
    alias = alias_shift[...] + jnp.concatenate([values] * 8, axis=0)
    lane = lax.broadcasted_iota(jnp.int32, (8, LANES), 1)
    mode = jnp.broadcast_to(mode_shift[...], (8, LANES))
    for part in range(PARTS):
        mode = mode + jnp.where(lax.div(lane, PLANES) == part, values[part : part + 1], 0.0)
    shifts = jnp.concatenate([alias, mode], axis=0)
    row = lax.broadcasted_iota(jnp.int32, (8, LANES), 0)
    previous = None
    value = None
    for layer in range(NZ):
        below = face[layer - 1] if layer > 0 else face[NZ - 1]
        pivot = (below + face[layer] + screening[layer]) + cell[layer] * shifts
        if previous is not None:
            pivot = pivot - (below * below) * previous
        previous = 1.0 / pivot
        alias_inverse[layer] = previous[: 8 * PARTS]
        inv = previous[8 * PARTS :]
        inverses[layer] = inv
        fresh = jnp.where(row == layer // LAYERS, inv, 0.0) if layer % LAYERS == 0 else None
        if value is None:
            value = fresh
        else:
            value = (face[layer - 1] * inv) * value
            if fresh is not None:
                value = value + fresh
        columns[layer] = value
    value = None
    for layer in reversed(range(NZ)):
        value = columns[layer] if value is None else columns[layer] + (face[layer] * inverses[layer]) * value
        scaled[layer * 8 : (layer + 1) * 8] = cell[layer] * value
        if layer % LAYERS == 0:
            corners[layer // LAYERS] = value
    for copy in copies:
        copy.wait()
    copies = [pltpu.make_async_copy(held_high, table_high, sems.at[2]), pltpu.make_async_copy(held_low, table_low, sems.at[3])]
    for copy in copies:
        copy.start()
    weight = jnp.concatenate([mask[...]] * CHIPS, axis=1)
    for chip in range(CHIPS):
        column = scaled[pl.ds(chip, NZ, stride=8), :]
        response = dot_full(column, spread[...], ((0,), (0,))) * weight
        high, low = split_values(response)
        response_high[chip * LANES : (chip + 1) * LANES, :] = high
        response_low[chip * LANES : (chip + 1) * LANES, :] = low
    for copy in copies:
        copy.wait()


def interface_kernel(arrived, response_high, response_low, corners, alias_inverse, forward, backward, coefficients, out, source, part, solved):
    face = columns_of(coefficients)[1]

    def rows(chip, slot):
        return pl.ds(ROWS * chip + slot, SLABS, stride=ROWS * CHIPS)

    sides = []
    for chip in range(CHIPS):
        side = arrived[rows(chip, 0), :]
        sides.append(side + arrived[rows(chip - 1, 1), :] if chip > 0 else side)
    response = (response_high[...], response_low[...])
    sums = dot_split(split_values(jnp.concatenate(sides, axis=1)), response)
    sums = sums + jnp.concatenate([arrived[rows(chip, 2), :] for chip in range(CHIPS)], axis=1)
    high, low = split_values(sums)
    stacked = jnp.concatenate([high, high, low], axis=0)
    turned = lax.dot_general(stacked, forward[...], (((0,), (0,)), ((), ())), preferred_element_type=jnp.float32)
    half = PARTS * LAYERS
    for chip in range(CHIPS):
        at = chip * LANES
        source[chip * half : (chip + 1) * half, :] = turned[at : at + half, :LANES] + turned[at + half : at + LANES, LANES:]
    value = None
    for layer in range(NZ):
        inv = alias_inverse[layer]
        first = (layer // LAYERS) * half + layer % LAYERS
        row = source[pl.ds(first, PARTS, stride=LAYERS), :]
        row = jnp.concatenate([row] * 8, axis=0)
        scaled = row * inv
        value = scaled if value is None else scaled + (face[layer - 1] * inv) * value
        part[layer] = value
    value = None
    for layer in reversed(range(NZ)):
        value = part[layer] if value is None else part[layer] + (face[layer] * alias_inverse[layer]) * value
        first = (layer // LAYERS) * half + layer % LAYERS
        total = (value[0:8] + value[8:16]) + (value[16:24] + value[24:32])
        solved[pl.ds(first, PARTS, stride=LAYERS), :] = total[:PARTS] + total[PARTS:]
    planes = dot_full(backward[...], solved[...], ((1,), (1,)))
    own = []
    for chip in range(CHIPS):
        at = chip * half
        own.append(jnp.concatenate([planes[:SLABS, at : at + half], planes[SLABS:, at : at + half]], axis=1))
    change = dot_split(split_values(jnp.concatenate(own, axis=1)), response, ((1,), (1,)))
    ends = []
    for chip in range(CHIPS):
        end = change[:, chip * LANES : (chip + 1) * LANES]
        for other in range(CHIPS):
            end = end + corners[chip, other : other + 1, :] * sides[other]
        ends.append(end)
    nothing = jnp.zeros((SLABS, LANES), jnp.float32)
    ends.append(nothing)
    for chip in range(CHIPS):
        out[rows(chip, 0), :] = ends[chip]
        out[rows(chip, 1), :] = ends[chip + 1]
        out[rows(chip, 2), :] = own[chip]
        out[rows(chip, 3), :] = nothing


def second_solve_kernel(modes, arrived, shifts, weights, table_high, table_low, slab_high, slab_low, coefficients, kept, sent_first, sent_last, part, near, edge, inverse):
    core, chip, _ = position()
    base = chip * LAYERS
    cell, face, _ = columns_of(coefficients, PARTS)
    chip_pivots(shifts, coefficients, inverse)
    below = unstack_parts(arrived[pl.ds(0, PEERS, stride=ROWS), :])
    above = unstack_parts(arrived[pl.ds(1, PEERS, stride=ROWS), :])
    turned = arrived[pl.ds(2, PEERS, stride=ROWS), :].T
    for which, target in enumerate((near, edge)):
        for step in range(PARTS):
            at = (which * PARTS + step) * LAYERS
            target[:, step * LANES : (step + 1) * LANES] = turned[at : at + LAYERS]
    weight = widen(weights[:PLANES])
    signed = widen(weights[PLANES:])
    keep = lax.broadcasted_iota(jnp.int32, (PLANES, HALF), 0) == 0
    value = None
    for layer in range(1, LAYERS):
        inv = inverse[layer]
        both = (near[layer : layer + 1, :] * weight + edge[layer : layer + 1, :] * signed) * cell[base + layer]
        right = modes[layer] + both
        if layer == 1:
            right = right + face[base] * below
        if layer == LAYERS - 1:
            right = right + face[base + layer] * above
        scaled = right * inv
        value = scaled if value is None else scaled + (face[base + layer - 1] * inv) * value
        part[layer] = value
    value = None
    for layer in reversed(range(1, LAYERS)):
        value = part[layer] if value is None else part[layer] + (face[base + layer] * inverse[layer]) * value
        part[layer] = jnp.where(keep, near[layer : layer + 1, :], value)
    part[0] = jnp.where(keep, near[0:1, :], below)
    kept[...] = part[pl.ds(core * 8, 8)]
    planes = to_planes(part[pl.ds((1 - core) * 8, 8)], table_high, table_low, slab_high, slab_low)
    sent_first[...] = planes[:4]
    sent_last[...] = planes[4:]


def backward_kernel(modes, table_high, table_low, slab_high, slab_low, out):
    out[...] = to_planes(modes[...], table_high, table_low, slab_high, slab_low)


def join_layers(first, kept, other, out, lines, sems):
    core, _, _ = position()
    sign = jnp.where(core == 0, 1.0, -1.0)
    copies = []
    for step in range(4):
        one, two = kept[first + step], other[step]
        lines[step, :, :HALF] = one + two
        lines[step, :, HALF:] = sign * (one - two)
        copies.append(pltpu.make_async_copy(lines.at[step], out.at[first + step], sems.at[step]))
        copies[-1].start()
    for copy in copies:
        copy.wait()


def join_first_kernel(kept, other, out, lines, sems):
    join_layers(0, kept, other, out, lines, sems)


def join_last_kernel(kept, other, begun, out, lines, sems):
    join_layers(4, kept, other, out, lines, sems)


held = pl.BlockSpec(memory_space=pltpu.VMEM)
far = pl.BlockSpec(memory_space=pl.ANY)
in_hbm = functools.partial(pltpu.with_memory_space_constraint, memory_space=pltpu.HBM)


def call(kernel, inputs, in_specs, outs, out_specs, scratch=(), cost=10_000_000, aliases={}):
    return pl.pallas_call(
        kernel,
        in_specs=in_specs,
        out_specs=out_specs,
        out_shape=outs,
        scratch_shapes=scratch,
        input_output_aliases=aliases,
        compiler_params=pltpu.CompilerParams(vmem_limit_bytes=VMEM_LIMIT),
        cost_estimate=pl.CostEstimate(flops=cost, bytes_accessed=4_000_000, transcendentals=0),
    )(*inputs)


def body(charge, cell, face, screening):
    forward_y, backward_y = y_tables()
    fy_high, fy_low = split_pair(forward_y)
    by_high, by_low = split_pair(backward_y)
    slab_high, slab_low = split_pair(np.kron(np.eye(8), slab_basis()))
    forward_slab, backward_slab, alias_shift = interface_tables()
    spread, mask = spread_tables()
    weights = np.concatenate([near_weights(), near_weights() * far_signs()])
    weights = np.broadcast_to(weights[:, None], (2 * PLANES, LANES)).copy()
    shift_y = y_shifts()
    mode_shift = np.tile(slab_shifts(), PARTS)[None, :]

    cube = (8, PLANES, HALF)
    field = (LAYERS, PLANES, HALF)
    message = (ROWS * PEERS, LANES)
    square = (CHIPS * LANES, CHIPS * LANES)
    table = pltpu.VMEM((HALF, HALF), jnp.bfloat16)
    far_table = pltpu.HBM((HALF, HALF), jnp.bfloat16)
    groups = [[x * 2 * CHIPS + 2 * c + r for x in range(SLABS) for c in range(CHIPS)] for r in range(2)]

    def vmem(*shape):
        return pltpu.VMEM(shape, jnp.float32)

    def exchange(values):
        blocks = values.reshape(PEERS, ROWS, LANES)
        return lax.all_to_all(blocks, ("gx", "gz"), 0, 0, axis_index_groups=groups, tiled=True).reshape(message)

    pair = [(s, s ^ 1) for s in range(2 * CHIPS)]
    lines = vmem(8, PLANES, NY)
    coefficient_rows = [in_hbm(array.reshape(1, NZ)) for array in (cell, face, screening)]
    own, sent, table_high, coefficients = call(
        split_kernel,
        (in_hbm(charge), in_hbm(fy_high), *coefficient_rows),
        [far] * 5,
        [vmem(*cube), vmem(*cube), table, vmem(3 * NZ, LANES)],
        [held] * 4,
        [lines, vmem(3, 1, NZ), pltpu.SemaphoreType.DMA((12,))],
    )
    other = lax.ppermute(sent, "gz", pair)
    shifts = np.concatenate([shift_y.reshape(2 * PARTS, LANES), np.broadcast_to(slab_shifts()[:, None], (PLANES, LANES))])
    inverse, own_modes, table_low = call(
        early_kernel,
        (own, table_high, in_hbm(fy_low), slab_high, slab_low, shifts, coefficients),
        [held] * 2 + [far] + [held] * 4,
        [vmem(*field), vmem(*cube), table],
        [held] * 3,
        [pltpu.SemaphoreType.DMA],
    )
    modes, ends = call(
        forward_kernel,
        (own_modes, other, table_high, table_low, slab_high, slab_low, inverse, weights, fold_table(), coefficients),
        [held] * 10,
        [vmem(*field), pltpu.HBM(message, jnp.float32)],
        [held] * 2,
        [vmem(*field), vmem(8 * LAYERS, HALF)],
    )
    modes = call(keep_kernel, (modes,), [held], pltpu.HBM(field, jnp.float32), far, [pltpu.SemaphoreType.DMA])
    alias_inverse, response_high, response_low, corners, table_high, table_low = call(
        prepare_kernel,
        (in_hbm(modes), shifts, alias_shift, mode_shift, spread, mask, in_hbm(by_high), in_hbm(by_low), coefficients),
        [far] + [held] * 5 + [far] * 2 + [held],
        [vmem(NZ, 8 * PARTS, LANES), pltpu.VMEM(square, jnp.bfloat16), pltpu.VMEM(square, jnp.bfloat16), vmem(CHIPS, 8, LANES)]
        + [far_table, far_table],
        [held] * 4 + [far] * 2,
        [vmem(NZ, 8, LANES), vmem(NZ, 8, LANES), vmem(8 * NZ, LANES), table, table, pltpu.SemaphoreType.DMA((4,))],
    )
    ends = exchange(ends)
    ends = call(
        interface_kernel,
        (ends, response_high, response_low, corners, alias_inverse, forward_slab, backward_slab, coefficients),
        [held] * 8,
        vmem(*message),
        held,
        [vmem(CHIPS * PARTS * LAYERS, LANES), vmem(NZ, 8 * PARTS, LANES), vmem(CHIPS * PARTS * LAYERS, LANES)],
    )
    ends = exchange(ends)
    kept, sent_first, sent_last = call(
        second_solve_kernel,
        (modes, ends, shifts, weights, table_high, table_low, slab_high, slab_low, coefficients),
        [held] * 9,
        [vmem(*cube), vmem(4, PLANES, HALF), vmem(4, PLANES, HALF)],
        [held] * 3,
        [vmem(*field), vmem(LAYERS, HALF), vmem(LAYERS, HALF), vmem(*field)],
    )
    other_first = lax.ppermute(sent_first, "gz", pair)
    other_last = lax.ppermute(sent_last, "gz", pair)
    kept = call(backward_kernel, (kept, table_high, table_low, slab_high, slab_low), [held] * 5, vmem(*cube), held)
    scratch = [vmem(4, PLANES, NY), pltpu.SemaphoreType.DMA((4,))]
    out = pltpu.HBM((8, PLANES, NY), jnp.float32)
    begun = call(join_first_kernel, (kept, other_first), [held] * 2, out, far, scratch)
    return call(join_last_kernel, (kept, other_last, in_hbm(begun)), [held] * 2 + [far], out, far, scratch, aliases={2: 0})


def solution(mesh):
    in_specs = (P("gz", "gx", None), P(), P(), P())
    out_specs = P("gz", "gx", None)
    return jax.shard_map(body, mesh=mesh, in_specs=in_specs, out_specs=out_specs, check_vma=False)
```

```python
import functools
import math

import jax
import jax.numpy as jnp
import ml_dtypes
import numpy as np
from jax import lax
from jax.experimental import pallas as pl
from jax.experimental.pallas import tpu as pltpu
from jax.sharding import PartitionSpec as P

NX, NY, NZ = 1024, 1024, 64
SLABS, PLANES = 32, 32
HALF = NY // 2
CHIPS = 4
LAYERS = NZ // CHIPS
MIDDLE = NZ // 2
PEERS = SLABS * CHIPS
PARTS = 4
ROWS = 4
LANES = 128
highest = lax.Precision.HIGHEST
VMEM_LIMIT = 48 * 1024 * 1024


def split_pair(table):
    high = table.astype(np.float32).astype(ml_dtypes.bfloat16)
    low = (table - high.astype(np.float64)).astype(np.float32).astype(ml_dtypes.bfloat16)
    return high, low


def y_frequencies():
    index = np.arange(HALF)
    even = np.where(index <= HALF // 2, 2 * index, 2 * (index - HALF // 2))
    odd = np.where(index < HALF // 2, 2 * index + 1, 2 * (index - HALF // 2) + 1)
    even_is_cos = index <= HALF // 2
    odd_is_cos = index < HALF // 2
    return np.stack([even, odd]), np.stack([even_is_cos, odd_is_cos])


def y_tables():
    freq, is_cos = y_frequencies()
    point = np.arange(HALF)
    angle = 2.0 * np.pi * (point[None, :, None] * freq[:, None, :] % NY) / NY
    forward = np.where(is_cos[:, None, :], np.cos(angle), np.sin(angle))
    weight = np.where((freq == 0) | (freq == NY // 2), 1.0 / NY, 2.0 / NY)
    backward = np.swapaxes(forward * weight[:, None, :], 1, 2)
    return forward, backward


def y_shifts():
    freq, _ = y_frequencies()
    return (4.0 * np.sin(np.pi * freq / NY) ** 2).astype(np.float32)


def slab_basis():
    index = np.arange(PLANES)
    basis = math.sqrt(2.0 / PLANES) * np.sin(np.pi * np.outer(index, index) / PLANES)
    basis[0, :] = 0.0
    basis[:, 0] = 0.0
    basis[0, 0] = 1.0
    return basis


def slab_shifts():
    return (4.0 * np.sin(np.pi * np.arange(PLANES) / (2 * PLANES)) ** 2).astype(np.float32)


def near_weights():
    weight = slab_basis()[1].copy()
    weight[0] = 0.0
    return weight.astype(np.float32)


def far_signs():
    return np.where(np.arange(PLANES) % 2 == 1, 1.0, -1.0).astype(np.float32)


def interface_tables():
    mode = np.arange(SLABS)
    freq = np.where(mode <= SLABS // 2, mode, mode - SLABS // 2)
    is_cos = mode <= SLABS // 2
    weight = np.where((freq == 0) | (freq == SLABS // 2), 1.0, 2.0) / SLABS / SLABS

    def basis(offset):
        angle = 2.0 * np.pi * ((np.arange(SLABS)[:, None] + offset) * freq[None, :] % SLABS) / SLABS
        return np.where(is_cos[None, :], np.cos(angle), np.sin(angle))

    forward = np.concatenate([np.tile(basis(0), (1, 4)), np.tile(basis(1), (1, 4))], axis=1)
    high, low = split_pair(forward)
    backward = np.concatenate([np.tile(basis(0) * weight, (1, 4)), np.tile(basis(1) * weight, (1, 4))], axis=0)
    alias = freq[None, None, :] + SLABS * (np.arange(8)[:, None, None] + 8 * np.arange(4)[None, :, None])
    alias = np.repeat(alias, PARTS, axis=0)
    alias_shift = 4.0 * np.sin(np.pi * alias / NX) ** 2
    return (
        np.concatenate([high, low, high], axis=0),
        backward.astype(np.float32),
        alias_shift.reshape(8 * PARTS, LANES).astype(np.float32),
    )


def fold_table():
    fold = np.zeros((2, LAYERS, LAYERS, 8), np.float32)
    for layer in range(LAYERS):
        fold[0, layer, layer, :] = 1.0
        fold[1, layer, layer, :] = far_signs()[:8]
    return fold.reshape(2 * LAYERS, 8 * LAYERS).astype(ml_dtypes.bfloat16)


def spread_tables():
    spread = np.zeros((CHIPS, LAYERS, CHIPS, 2, PARTS, LAYERS), np.float32)
    for chip in range(CHIPS):
        for layer in range(LAYERS):
            spread[chip, layer, chip, :, :, layer] = 1.0
    mask = np.zeros((PARTS, PLANES, 2, PARTS, LAYERS), np.float32)
    for part in range(PARTS):
        mask[part, :, 0, part, :] = near_weights()[:, None]
        mask[part, :, 1, part, :] = (near_weights() * far_signs())[:, None]
    return spread.reshape(NZ, CHIPS * LANES), mask.reshape(LANES, LANES)


def position():
    gz = lax.axis_index("gz")
    core, chip = lax.rem(gz, 2), lax.div(gz, 2)
    return core, chip, lax.axis_index("gx") * CHIPS + chip


class Column:
    def __init__(self, ref, which, repeat):
        self.ref, self.start, self.repeat = ref, which * NZ, repeat

    def __getitem__(self, layer):
        row = self.ref[pl.ds(self.start + layer, 1), :]
        return jnp.concatenate([row] * self.repeat, axis=1)


def columns_of(ref, repeat=1):
    return [Column(ref, which, repeat) for which in range(3)]


def split_values(values):
    high = values.astype(jnp.bfloat16)
    low = (values - high.astype(jnp.float32)).astype(jnp.bfloat16)
    return high, low


def dot_split(left, right, contract=((1,), (0,))):
    left_high, left_low = left
    right_high, right_low = right

    def dot(one, two):
        return lax.dot_general(one, two, (contract, ((), ())), preferred_element_type=jnp.float32)

    return dot(left_high, right_high) + (dot(left_high, right_low) + dot(left_low, right_high))


def dot_stacked(left, right, contract):
    high, low = split_values(left)
    rows = left.shape[0]

    def dot(one, two):
        return lax.dot_general(one, two, (contract, ((), ())), preferred_element_type=jnp.float32)

    both = dot(jnp.concatenate([high, low], axis=0), right[0])
    return both[:rows] + (both[rows:] + dot(high, right[1]))


def dot_full(left, right, contract):
    return lax.dot_general(
        left, right, (contract, ((), ())), precision=highest, preferred_element_type=jnp.float32
    )


def split_kernel(charge, tables_high, cell, face, screening, own, sent, table_high, coefficients, lines, rows, sems):
    core, _, _ = position()
    copies = [pltpu.make_async_copy(source, rows.at[step], sems.at[9 + step]) for step, source in enumerate((cell, face, screening))]
    copies += [pltpu.make_async_copy(charge.at[step], lines.at[step], sems.at[step]) for step in range(8)]
    copies.append(pltpu.make_async_copy(tables_high.at[core], table_high, sems.at[8]))
    for copy in copies:
        copy.start()
    for step, copy in enumerate(copies[:3]):
        copy.wait()
        coefficients[step * NZ : (step + 1) * NZ, :] = jnp.broadcast_to(rows[step], (LANES, NZ)).T
    sign = jnp.where(core == 0, 1.0, -1.0)
    for step, copy in enumerate(copies[3:11]):
        copy.wait()
        lower, upper = lines[step, :, :HALF], sign * lines[step, :, HALF:]
        own[step] = lower + upper
        sent[step] = lower - upper
    for copy in copies[11:]:
        copy.wait()


def widen(table):
    return jnp.concatenate([table] * PARTS, axis=1)


def chip_pivots(shifts, coefficients, inverse):
    cell, face, screening = columns_of(coefficients, PARTS)
    core, chip, _ = position()
    base = chip * LAYERS
    row = jnp.concatenate([shifts[pl.ds(core * PARTS + part, 1), :] for part in range(PARTS)], axis=1)
    shifts = widen(shifts[8:]) + row
    previous = None
    for layer in range(1, LAYERS):
        below, above = face[base + layer - 1], face[base + layer]
        pivot = (below + above + screening[base + layer]) + cell[base + layer] * shifts
        if previous is not None:
            pivot = pivot - (below * below) * previous
        previous = 1.0 / pivot
        inverse[layer] = previous


def early_kernel(own, table_high, tables_low, slab_high, slab_low, shifts, coefficients, inverse, modes, table_low, sem):
    core, _, _ = position()
    copy = pltpu.make_async_copy(tables_low.at[core], table_low, sem)
    copy.start()
    chip_pivots(shifts, coefficients, inverse)
    high, low = split_values(own[...].reshape(8 * PLANES, HALF))
    dot = functools.partial(jnp.dot, preferred_element_type=jnp.float32)
    spectrum = dot(high, table_high[...]) + dot(low, table_high[...])
    copy.wait()
    spectrum = spectrum + dot(high, table_low[...])
    modes[...] = dot_split((slab_high[...], slab_low[...]), split_values(spectrum)).reshape(8, PLANES, HALF)


def to_modes(planes, table_high, table_low, slab_high, slab_low):
    values = planes[...].reshape(8 * PLANES, HALF)
    spectrum = dot_split(split_values(values), (table_high[...], table_low[...]))
    return dot_split((slab_high[...], slab_low[...]), split_values(spectrum)).reshape(8, PLANES, HALF)


def to_planes(modes, table_high, table_low, slab_high, slab_low):
    values = dot_split((slab_high[...], slab_low[...]), split_values(modes.reshape(8 * PLANES, HALF)))
    return dot_split(split_values(values), (table_high[...], table_low[...])).reshape(8, PLANES, HALF)


def stack_parts(values):
    return jnp.concatenate([values[:, part * LANES : (part + 1) * LANES] for part in range(PARTS)], axis=0).T


def unstack_parts(values):
    turned = values.T
    return jnp.concatenate([turned[part * PLANES : (part + 1) * PLANES] for part in range(PARTS)], axis=1)


def forward_kernel(own_modes, other, table_high, table_low, slab_high, slab_low, inverse, weights, fold, coefficients, modes, out, part, folded):
    core, chip, _ = position()
    base = chip * LAYERS
    cell, face, _ = columns_of(coefficients, PARTS)
    modes[pl.ds(core * 8, 8)] = own_modes[...]
    modes[pl.ds((1 - core) * 8, 8)] = to_modes(other, table_high, table_low, slab_high, slab_low)
    value = None
    for layer in range(1, LAYERS):
        inv = inverse[layer]
        scaled = modes[layer] * inv
        value = scaled if value is None else scaled + (face[base + layer - 1] * inv) * value
        part[layer] = value
    weight = widen(weights[:PLANES])
    value = None
    folded[0:8] = jnp.zeros((8, HALF), jnp.float32)
    for layer in reversed(range(1, LAYERS)):
        value = part[layer] if value is None else part[layer] + (face[base + layer] * inverse[layer]) * value
        if layer == LAYERS - 1:
            out[pl.ds(1, PEERS, stride=ROWS), :] = stack_parts(face[base + layer] * value)
        weighted = weight * value
        total = (weighted[0:8] + weighted[8:16]) + (weighted[16:24] + weighted[24:32])
        folded[layer * 8 : (layer + 1) * 8] = total * cell[base + layer]
    out[pl.ds(0, PEERS, stride=ROWS), :] = stack_parts(modes[0] + face[base] * value)
    high, low = split_values(folded[...])
    sums = jnp.dot(fold[...], high, preferred_element_type=jnp.float32) + jnp.dot(fold[...], low, preferred_element_type=jnp.float32)
    planes = jnp.concatenate([modes[layer, 0:1] for layer in range(LAYERS)], axis=0)
    near = sums[:LAYERS] + planes
    far = sums[LAYERS:]
    blocks = [half[:, step * LANES : (step + 1) * LANES] for half in (near, far) for step in range(PARTS)]
    out[pl.ds(2, PEERS, stride=ROWS), :] = jnp.concatenate(blocks, axis=0).T
    out[pl.ds(3, PEERS, stride=ROWS), :] = jnp.zeros((PEERS, LANES), jnp.float32)


def solve_layers(right, inverse, face, part, use):
    upper = lower = None
    for step in range(MIDDLE):
        inv = inverse[step]
        value = right(step) * inv
        upper = value if upper is None else value + (face[step - 1] * inv) * upper
        part[step] = upper
        layer = NZ - 1 - step
        if layer > MIDDLE:
            inv = inverse[layer]
            value = right(layer) * inv
            lower = value if lower is None else value + (face[layer] * inv) * lower
            part[layer] = lower
    inv = inverse[MIDDLE]
    value = right(MIDDLE) * inv + (face[MIDDLE - 1] * inv) * upper + (face[MIDDLE] * inv) * lower
    use(MIDDLE, value)
    upper = lower = value
    for step in range(1, MIDDLE + 1):
        layer = MIDDLE - step
        upper = part[layer] + (face[layer] * inverse[layer]) * upper
        use(layer, upper)
        layer = MIDDLE + step
        if layer < NZ:
            lower = part[layer] + (face[layer - 1] * inverse[layer]) * lower
            use(layer, lower)


def keep_kernel(modes, kept, sem):
    copy = pltpu.make_async_copy(modes, kept, sem)
    copy.start()
    copy.wait()


def prepare_kernel(modes, shifts, alias_shift, mode_shift, spread, mask, tables_high, tables_low, coefficients, alias_inverse, response_high, response_low, corners, table_high, table_low, inverses, columns, scaled, held_high, held_low, sems):
    core, _, peer = position()
    copies = [
        pltpu.make_async_copy(tables_high.at[core], held_high, sems.at[0]),
        pltpu.make_async_copy(tables_low.at[core], held_low, sems.at[1]),
    ]
    for copy in copies:
        copy.start()
    cell, face, screening = columns_of(coefficients)
    lane = lax.broadcasted_iota(jnp.int32, (PARTS, LANES), 1)
    values = jnp.sum(jnp.where(lane == peer, shifts[pl.ds(core * PARTS, PARTS), :], 0.0), axis=1, keepdims=True)
    alias = alias_shift[...] + jnp.concatenate([values] * 8, axis=0)
    lane = lax.broadcasted_iota(jnp.int32, (8, LANES), 1)
    mode = jnp.broadcast_to(mode_shift[...], (8, LANES))
    for part in range(PARTS):
        mode = mode + jnp.where(lax.div(lane, PLANES) == part, values[part : part + 1], 0.0)
    shifts = jnp.concatenate([alias, mode], axis=0)
    row = lax.broadcasted_iota(jnp.int32, (8, LANES), 0)

    def diagonal(layer):
        below = face[layer - 1] if layer > 0 else face[NZ - 1]
        return (below + face[layer] + screening[layer]) + cell[layer] * shifts

    def keep_pivot(layer, inverse):
        alias_inverse[layer] = inverse[: 8 * PARTS]
        inverses[layer] = inverse[8 * PARTS :]

    upper = lower = None
    for step in range(MIDDLE):
        pivot = diagonal(step)
        if upper is not None:
            pivot = pivot - (face[step - 1] * face[step - 1]) * upper
        upper = 1.0 / pivot
        keep_pivot(step, upper)
        layer = NZ - 1 - step
        if layer > MIDDLE:
            pivot = diagonal(layer)
            if lower is not None:
                pivot = pivot - (face[layer] * face[layer]) * lower
            lower = 1.0 / pivot
            keep_pivot(layer, lower)
    pivot = diagonal(MIDDLE) - (face[MIDDLE - 1] * face[MIDDLE - 1]) * upper
    keep_pivot(MIDDLE, 1.0 / (pivot - (face[MIDDLE] * face[MIDDLE]) * lower))

    def unit(layer):
        return jnp.where(row == layer // LAYERS, 1.0, 0.0) if layer % LAYERS == 0 else jnp.zeros((8, LANES), jnp.float32)

    def keep_column(layer, value):
        scaled[layer * 8 : (layer + 1) * 8] = cell[layer] * value
        if layer % LAYERS == 0:
            corners[layer // LAYERS] = value

    solve_layers(unit, inverses, face, columns, keep_column)
    for copy in copies:
        copy.wait()
    copies = [pltpu.make_async_copy(held_high, table_high, sems.at[2]), pltpu.make_async_copy(held_low, table_low, sems.at[3])]
    for copy in copies:
        copy.start()
    weight = jnp.concatenate([mask[...]] * CHIPS, axis=1)
    for chip in range(CHIPS):
        column = scaled[pl.ds(chip, NZ, stride=8), :]
        response = dot_full(column, spread[...], ((0,), (0,))) * weight
        high, low = split_values(response)
        response_high[chip * LANES : (chip + 1) * LANES, :] = high
        response_low[chip * LANES : (chip + 1) * LANES, :] = low
    for copy in copies:
        copy.wait()


def interface_kernel(arrived, response_high, response_low, corners, alias_inverse, forward, backward, coefficients, out, source, part, solved):
    face = columns_of(coefficients)[1]

    def rows(chip, slot):
        return pl.ds(ROWS * chip + slot, SLABS, stride=ROWS * CHIPS)

    sides = []
    for chip in range(CHIPS):
        side = arrived[rows(chip, 0), :]
        sides.append(side + arrived[rows(chip - 1, 1), :] if chip > 0 else side)
    response = (response_high[...], response_low[...])
    sums = dot_stacked(jnp.concatenate(sides, axis=1), response, ((1,), (0,)))
    sums = sums + jnp.concatenate([arrived[rows(chip, 2), :] for chip in range(CHIPS)], axis=1)
    high, low = split_values(sums)
    stacked = jnp.concatenate([high, high, low], axis=0)
    turned = lax.dot_general(stacked, forward[...], (((0,), (0,)), ((), ())), preferred_element_type=jnp.float32)
    half = PARTS * LAYERS
    for chip in range(CHIPS):
        at = chip * LANES
        source[chip * half : (chip + 1) * half, :] = turned[at : at + half, :LANES] + turned[at + half : at + LANES, LANES:]

    def first_row(layer):
        return (layer // LAYERS) * half + layer % LAYERS

    def right(layer):
        row = source[pl.ds(first_row(layer), PARTS, stride=LAYERS), :]
        return jnp.concatenate([row] * 8, axis=0)

    def keep_sum(layer, value):
        total = (value[0:8] + value[8:16]) + (value[16:24] + value[24:32])
        solved[pl.ds(first_row(layer), PARTS, stride=LAYERS), :] = total[:PARTS] + total[PARTS:]

    solve_layers(right, alias_inverse, face, part, keep_sum)
    planes = dot_full(backward[...], solved[...], ((1,), (1,)))
    own = []
    for chip in range(CHIPS):
        at = chip * half
        own.append(jnp.concatenate([planes[:SLABS, at : at + half], planes[SLABS:, at : at + half]], axis=1))
    change = dot_stacked(jnp.concatenate(own, axis=1), response, ((1,), (1,)))
    ends = []
    for chip in range(CHIPS):
        end = change[:, chip * LANES : (chip + 1) * LANES]
        for other in range(CHIPS):
            end = end + corners[chip, other : other + 1, :] * sides[other]
        ends.append(end)
    nothing = jnp.zeros((SLABS, LANES), jnp.float32)
    ends.append(nothing)
    for chip in range(CHIPS):
        out[rows(chip, 0), :] = ends[chip]
        out[rows(chip, 1), :] = ends[chip + 1]
        out[rows(chip, 2), :] = own[chip]
        out[rows(chip, 3), :] = nothing


def second_solve_kernel(modes, arrived, shifts, weights, table_high, table_low, slab_high, slab_low, coefficients, kept, sent, part, near, edge, inverse):
    core, chip, _ = position()
    base = chip * LAYERS
    cell, face, _ = columns_of(coefficients, PARTS)
    chip_pivots(shifts, coefficients, inverse)
    below = unstack_parts(arrived[pl.ds(0, PEERS, stride=ROWS), :])
    above = unstack_parts(arrived[pl.ds(1, PEERS, stride=ROWS), :])
    turned = arrived[pl.ds(2, PEERS, stride=ROWS), :].T
    for which, target in enumerate((near, edge)):
        for step in range(PARTS):
            at = (which * PARTS + step) * LAYERS
            target[:, step * LANES : (step + 1) * LANES] = turned[at : at + LAYERS]
    weight = widen(weights[:PLANES])
    signed = widen(weights[PLANES:])
    keep = lax.broadcasted_iota(jnp.int32, (PLANES, HALF), 0) == 0
    value = None
    for layer in range(1, LAYERS):
        inv = inverse[layer]
        both = (near[layer : layer + 1, :] * weight + edge[layer : layer + 1, :] * signed) * cell[base + layer]
        right = modes[layer] + both
        if layer == 1:
            right = right + face[base] * below
        if layer == LAYERS - 1:
            right = right + face[base + layer] * above
        scaled = right * inv
        value = scaled if value is None else scaled + (face[base + layer - 1] * inv) * value
        part[layer] = value
    value = None
    for layer in reversed(range(1, LAYERS)):
        value = part[layer] if value is None else part[layer] + (face[base + layer] * inverse[layer]) * value
        part[layer] = jnp.where(keep, near[layer : layer + 1, :], value)
    part[0] = jnp.where(keep, near[0:1, :], below)
    kept[...] = part[pl.ds(core * 8, 8)]
    sent[...] = to_planes(part[pl.ds((1 - core) * 8, 8)], table_high, table_low, slab_high, slab_low)


def backward_kernel(modes, table_high, table_low, slab_high, slab_low, out):
    out[...] = to_planes(modes[...], table_high, table_low, slab_high, slab_low)


def join_kernel(kept, other, out, lines, sems):
    core, _, _ = position()
    sign = jnp.where(core == 0, 1.0, -1.0)
    copies = []
    for step in range(4):
        at = slice(2 * step, 2 * step + 2)
        one, two = kept[at], other[at]
        lines[at, :, :HALF] = one + two
        lines[at, :, HALF:] = sign * (one - two)
        copies.append(pltpu.make_async_copy(lines.at[pl.ds(2 * step, 2)], out.at[pl.ds(2 * step, 2)], sems.at[step]))
        copies[-1].start()
    for copy in copies:
        copy.wait()


held = pl.BlockSpec(memory_space=pltpu.VMEM)
far = pl.BlockSpec(memory_space=pl.ANY)
in_hbm = functools.partial(pltpu.with_memory_space_constraint, memory_space=pltpu.HBM)


def call(kernel, inputs, in_specs, outs, out_specs, scratch=(), cost=10_000_000):
    return pl.pallas_call(
        kernel,
        in_specs=in_specs,
        out_specs=out_specs,
        out_shape=outs,
        scratch_shapes=scratch,
        compiler_params=pltpu.CompilerParams(vmem_limit_bytes=VMEM_LIMIT),
        cost_estimate=pl.CostEstimate(flops=cost, bytes_accessed=4_000_000, transcendentals=0),
    )(*inputs)


def body(charge, cell, face, screening):
    forward_y, backward_y = y_tables()
    fy_high, fy_low = split_pair(forward_y)
    by_high, by_low = split_pair(backward_y)
    slab_high, slab_low = split_pair(np.kron(np.eye(8), slab_basis()))
    forward_slab, backward_slab, alias_shift = interface_tables()
    spread, mask = spread_tables()
    weights = np.concatenate([near_weights(), near_weights() * far_signs()])
    weights = np.broadcast_to(weights[:, None], (2 * PLANES, LANES)).copy()
    shift_y = y_shifts()
    mode_shift = np.tile(slab_shifts(), PARTS)[None, :]

    cube = (8, PLANES, HALF)
    field = (LAYERS, PLANES, HALF)
    message = (ROWS * PEERS, LANES)
    square = (CHIPS * LANES, CHIPS * LANES)
    table = pltpu.VMEM((HALF, HALF), jnp.bfloat16)
    far_table = pltpu.HBM((HALF, HALF), jnp.bfloat16)
    groups = [[x * 2 * CHIPS + 2 * c + r for x in range(SLABS) for c in range(CHIPS)] for r in range(2)]

    def vmem(*shape):
        return pltpu.VMEM(shape, jnp.float32)

    def exchange(values):
        blocks = values.reshape(PEERS, ROWS, LANES)
        return lax.all_to_all(blocks, ("gx", "gz"), 0, 0, axis_index_groups=groups, tiled=True).reshape(message)

    pair = [(s, s ^ 1) for s in range(2 * CHIPS)]
    lines = vmem(8, PLANES, NY)
    coefficient_rows = [in_hbm(array.reshape(1, NZ)) for array in (cell, face, screening)]
    own, sent, table_high, coefficients = call(
        split_kernel,
        (in_hbm(charge), in_hbm(fy_high), *coefficient_rows),
        [far] * 5,
        [vmem(*cube), vmem(*cube), table, vmem(3 * NZ, LANES)],
        [held] * 4,
        [lines, vmem(3, 1, NZ), pltpu.SemaphoreType.DMA((12,))],
    )
    other = lax.ppermute(sent, "gz", pair)
    shifts = np.concatenate([shift_y.reshape(2 * PARTS, LANES), np.broadcast_to(slab_shifts()[:, None], (PLANES, LANES))])
    inverse, own_modes, table_low = call(
        early_kernel,
        (own, table_high, in_hbm(fy_low), slab_high, slab_low, shifts, coefficients),
        [held] * 2 + [far] + [held] * 4,
        [vmem(*field), vmem(*cube), table],
        [held] * 3,
        [pltpu.SemaphoreType.DMA],
    )
    modes, ends = call(
        forward_kernel,
        (own_modes, other, table_high, table_low, slab_high, slab_low, inverse, weights, fold_table(), coefficients),
        [held] * 10,
        [vmem(*field), pltpu.HBM(message, jnp.float32)],
        [held] * 2,
        [vmem(*field), vmem(8 * LAYERS, HALF)],
    )
    modes = call(keep_kernel, (modes,), [held], pltpu.HBM(field, jnp.float32), far, [pltpu.SemaphoreType.DMA])
    alias_inverse, response_high, response_low, corners, table_high, table_low = call(
        prepare_kernel,
        (in_hbm(modes), shifts, alias_shift, mode_shift, spread, mask, in_hbm(by_high), in_hbm(by_low), coefficients),
        [far] + [held] * 5 + [far] * 2 + [held],
        [vmem(NZ, 8 * PARTS, LANES), pltpu.VMEM(square, jnp.bfloat16), pltpu.VMEM(square, jnp.bfloat16), vmem(CHIPS, 8, LANES)]
        + [far_table, far_table],
        [held] * 4 + [far] * 2,
        [vmem(NZ, 8, LANES), vmem(NZ, 8, LANES), vmem(8 * NZ, LANES), table, table, pltpu.SemaphoreType.DMA((4,))],
    )
    ends = exchange(ends)
    ends = call(
        interface_kernel,
        (ends, response_high, response_low, corners, alias_inverse, forward_slab, backward_slab, coefficients),
        [held] * 8,
        vmem(*message),
        held,
        [vmem(CHIPS * PARTS * LAYERS, LANES), vmem(NZ, 8 * PARTS, LANES), vmem(CHIPS * PARTS * LAYERS, LANES)],
    )
    ends = exchange(ends)
    kept, sent = call(
        second_solve_kernel,
        (modes, ends, shifts, weights, table_high, table_low, slab_high, slab_low, coefficients),
        [held] * 9,
        [vmem(*cube), vmem(*cube)],
        [held] * 2,
        [vmem(*field), vmem(LAYERS, HALF), vmem(LAYERS, HALF), vmem(*field)],
    )
    other = lax.ppermute(sent, "gz", pair)
    kept = call(backward_kernel, (kept, table_high, table_low, slab_high, slab_low), [held] * 5, vmem(*cube), held)
    return call(
        join_kernel, (kept, other), [held] * 2, pltpu.HBM((8, PLANES, NY), jnp.float32), far, [lines, pltpu.SemaphoreType.DMA((4,))]
    )


def solution(mesh):
    in_specs = (P("gz", "gx", None), P(), P(), P())
    out_specs = P("gz", "gx", None)
    return jax.shard_map(body, mesh=mesh, in_specs=in_specs, out_specs=out_specs, check_vma=False)
```

```python
import functools
import math

import jax
import jax.numpy as jnp
import ml_dtypes
import numpy as np
from jax import lax
from jax.experimental import pallas as pl
from jax.experimental.pallas import tpu as pltpu
from jax.sharding import PartitionSpec as P

NX, NY, NZ = 1024, 1024, 64
SLABS, PLANES = 32, 32
HALF = NY // 2
CHIPS = 4
LAYERS = NZ // CHIPS
MIDDLE = NZ // 2
PEERS = SLABS * CHIPS
PARTS = 4
ROWS = 4
LANES = 128
highest = lax.Precision.HIGHEST
VMEM_LIMIT = 48 * 1024 * 1024


def split_pair(table):
    high = table.astype(np.float32).astype(ml_dtypes.bfloat16)
    low = (table - high.astype(np.float64)).astype(np.float32).astype(ml_dtypes.bfloat16)
    return high, low


def y_frequencies():
    index = np.arange(HALF // 2)
    quarter = HALF // 4
    even = np.concatenate([4 * np.where(index <= quarter, index, index - quarter), 4 * (index % quarter) + 2])
    even_is_cos = np.concatenate([index <= quarter, index < quarter])
    index = np.arange(HALF)
    odd = 2 * (index % (HALF // 2)) + 1
    return np.stack([even, odd]), np.stack([even_is_cos, index < HALF // 2])


def y_tables():
    freq, is_cos = y_frequencies()
    point = np.arange(HALF)
    angle = 2.0 * np.pi * (point[None, :, None] * freq[:, None, :] % NY) / NY
    forward = np.where(is_cos[:, None, :], np.cos(angle), np.sin(angle))
    weight = np.where((freq == 0) | (freq == NY // 2), 1.0 / NY, 2.0 / NY)
    backward = np.swapaxes(forward * weight[:, None, :], 1, 2)
    return forward, backward


def y_shifts():
    freq, _ = y_frequencies()
    return (4.0 * np.sin(np.pi * freq / NY) ** 2).astype(np.float32)


def slab_basis():
    index = np.arange(PLANES)
    basis = math.sqrt(2.0 / PLANES) * np.sin(np.pi * np.outer(index, index) / PLANES)
    basis[0, :] = 0.0
    basis[:, 0] = 0.0
    basis[0, 0] = 1.0
    return basis


def slab_shifts():
    return (4.0 * np.sin(np.pi * np.arange(PLANES) / (2 * PLANES)) ** 2).astype(np.float32)


def near_weights():
    weight = slab_basis()[1].copy()
    weight[0] = 0.0
    return weight.astype(np.float32)


def far_signs():
    return np.where(np.arange(PLANES) % 2 == 1, 1.0, -1.0).astype(np.float32)


def interface_tables():
    mode = np.arange(SLABS)
    freq = np.where(mode <= SLABS // 2, mode, mode - SLABS // 2)
    is_cos = mode <= SLABS // 2
    weight = np.where((freq == 0) | (freq == SLABS // 2), 1.0, 2.0) / SLABS / SLABS

    def basis(offset):
        angle = 2.0 * np.pi * ((np.arange(SLABS)[:, None] + offset) * freq[None, :] % SLABS) / SLABS
        return np.where(is_cos[None, :], np.cos(angle), np.sin(angle))

    forward = np.concatenate([np.tile(basis(0), (1, 4)), np.tile(basis(1), (1, 4))], axis=1)
    high, low = split_pair(forward)
    backward = np.concatenate([np.tile(basis(0) * weight, (1, 4)), np.tile(basis(1) * weight, (1, 4))], axis=0)
    alias = freq[None, None, :] + SLABS * (np.arange(8)[:, None, None] + 8 * np.arange(4)[None, :, None])
    alias = np.repeat(alias, PARTS, axis=0)
    alias_shift = 4.0 * np.sin(np.pi * alias / NX) ** 2
    return (
        np.concatenate([high, low, high], axis=0),
        backward.astype(np.float32),
        alias_shift.reshape(8 * PARTS, LANES).astype(np.float32),
    )


def fold_table():
    fold = np.zeros((2, LAYERS, LAYERS, 8), np.float32)
    for layer in range(LAYERS):
        fold[0, layer, layer, :] = 1.0
        fold[1, layer, layer, :] = far_signs()[:8]
    return fold.reshape(2 * LAYERS, 8 * LAYERS).astype(ml_dtypes.bfloat16)


def spread_tables():
    spread = np.zeros((CHIPS, LAYERS, CHIPS, 2, PARTS, LAYERS), np.float32)
    for chip in range(CHIPS):
        for layer in range(LAYERS):
            spread[chip, layer, chip, :, :, layer] = 1.0
    mask = np.zeros((PARTS, PLANES, 2, PARTS, LAYERS), np.float32)
    for part in range(PARTS):
        mask[part, :, 0, part, :] = near_weights()[:, None]
        mask[part, :, 1, part, :] = (near_weights() * far_signs())[:, None]
    return spread.reshape(NZ, CHIPS * LANES), mask.reshape(LANES, LANES)


def position():
    gz = lax.axis_index("gz")
    core, chip = lax.rem(gz, 2), lax.div(gz, 2)
    return core, chip, lax.axis_index("gx") * CHIPS + chip


class Column:
    def __init__(self, ref, which, repeat):
        self.ref, self.start, self.repeat = ref, which * NZ, repeat

    def __getitem__(self, layer):
        row = self.ref[pl.ds(self.start + layer, 1), :]
        return jnp.concatenate([row] * self.repeat, axis=1)


def columns_of(ref, repeat=1):
    return [Column(ref, which, repeat) for which in range(3)]


def split_values(values):
    high = values.astype(jnp.bfloat16)
    low = (values - high.astype(jnp.float32)).astype(jnp.bfloat16)
    return high, low


def dot_split(left, right, contract=((1,), (0,))):
    left_high, left_low = left
    right_high, right_low = right

    def dot(one, two):
        return lax.dot_general(one, two, (contract, ((), ())), preferred_element_type=jnp.float32)

    return dot(left_high, right_high) + (dot(left_high, right_low) + dot(left_low, right_high))


def dot_stacked(left, right, contract):
    high, low = split_values(left)
    rows = left.shape[0]

    def dot(one, two):
        return lax.dot_general(one, two, (contract, ((), ())), preferred_element_type=jnp.float32)

    both = dot(jnp.concatenate([high, low], axis=0), right[0])
    return both[:rows] + (both[rows:] + dot(high, right[1]))


def dot_full(left, right, contract):
    return lax.dot_general(
        left, right, (contract, ((), ())), precision=highest, preferred_element_type=jnp.float32
    )


def split_kernel(charge, tables_high, cell, face, screening, own, sent, table_high, coefficients, lines, rows, sems):
    core, _, _ = position()
    copies = [pltpu.make_async_copy(source, rows.at[step], sems.at[9 + step]) for step, source in enumerate((cell, face, screening))]
    copies += [pltpu.make_async_copy(charge.at[step], lines.at[step], sems.at[step]) for step in range(8)]
    copies.append(pltpu.make_async_copy(tables_high.at[core], table_high, sems.at[8]))
    for copy in copies:
        copy.start()
    for step, copy in enumerate(copies[:3]):
        copy.wait()
        coefficients[step * NZ : (step + 1) * NZ, :] = jnp.broadcast_to(rows[step], (LANES, NZ)).T
    sign = jnp.where(core == 0, 1.0, -1.0)
    for step, copy in enumerate(copies[3:11]):
        copy.wait()
        lower, upper = lines[step, :, :HALF], sign * lines[step, :, HALF:]
        own[step] = lower + upper
        sent[step] = lower - upper
    for copy in copies[11:]:
        copy.wait()


def widen(table):
    return jnp.concatenate([table] * PARTS, axis=1)


def chip_pivots(shifts, coefficients, inverse):
    cell, face, screening = columns_of(coefficients, PARTS)
    core, chip, _ = position()
    base = chip * LAYERS
    row = jnp.concatenate([shifts[pl.ds(core * PARTS + part, 1), :] for part in range(PARTS)], axis=1)
    shifts = widen(shifts[8:]) + row
    previous = None
    for layer in range(1, LAYERS):
        below, above = face[base + layer - 1], face[base + layer]
        pivot = (below + above + screening[base + layer]) + cell[base + layer] * shifts
        if previous is not None:
            pivot = pivot - (below * below) * previous
        previous = 1.0 / pivot
        inverse[layer] = previous


def early_kernel(own, table_high, tables_low, slab_high, slab_low, shifts, coefficients, inverse, modes, table_low, sem):
    core, _, _ = position()
    copy = pltpu.make_async_copy(tables_low.at[core], table_low, sem)
    copy.start()
    chip_pivots(shifts, coefficients, inverse)
    high, low = split_values(own[...].reshape(8 * PLANES, HALF))
    dot = functools.partial(jnp.dot, preferred_element_type=jnp.float32)
    spectrum = dot(high, table_high[...]) + dot(low, table_high[...])
    copy.wait()
    spectrum = spectrum + dot(high, table_low[...])
    modes[...] = dot_split((slab_high[...], slab_low[...]), split_values(spectrum)).reshape(8, PLANES, HALF)


def spectrum_into(out, planes, table_high, table_low):
    core, _, _ = position()
    values = planes[...].reshape(8 * PLANES, HALF)
    half = HALF // 2

    @pl.when(core == 0)
    def _():
        for at, sign in ((0, 1.0), (half, -1.0)):
            mixed = values[:, :half] + sign * values[:, half:]
            table = (table_high[:half, at : at + half], table_low[:half, at : at + half])
            out[:, :, at : at + half] = dot_split(split_values(mixed), table).reshape(8, PLANES, half)

    @pl.when(core != 0)
    def _():
        out[...] = dot_split(split_values(values), (table_high[...], table_low[...])).reshape(8, PLANES, HALF)


def planes_into(out, modes, table_high, table_low, slab_high, slab_low):
    core, _, _ = position()
    values = dot_split((slab_high[...], slab_low[...]), split_values(modes.reshape(8 * PLANES, HALF)))
    half = HALF // 2

    @pl.when(core == 0)
    def _():
        one, two = [
            dot_split(split_values(values[:, at : at + half]), (table_high[at : at + half, :half], table_low[at : at + half, :half]))
            for at in (0, half)
        ]
        out[:, :, :half] = (one + two).reshape(8, PLANES, half)
        out[:, :, half:] = (one - two).reshape(8, PLANES, half)

    @pl.when(core != 0)
    def _():
        out[...] = dot_split(split_values(values), (table_high[...], table_low[...])).reshape(8, PLANES, HALF)


def stack_parts(values):
    return jnp.concatenate([values[:, part * LANES : (part + 1) * LANES] for part in range(PARTS)], axis=0).T


def unstack_parts(values):
    turned = values.T
    return jnp.concatenate([turned[part * PLANES : (part + 1) * PLANES] for part in range(PARTS)], axis=1)


def forward_kernel(own_modes, other, table_high, table_low, slab_high, slab_low, inverse, weights, fold, coefficients, modes, out, part, folded):
    core, chip, _ = position()
    base = chip * LAYERS
    cell, face, _ = columns_of(coefficients, PARTS)
    modes[pl.ds(core * 8, 8)] = own_modes[...]
    spectrum_into(part.at[pl.ds(0, 8)], other, table_high, table_low)
    spectrum = split_values(part[0:8].reshape(8 * PLANES, HALF))
    modes[pl.ds((1 - core) * 8, 8)] = dot_split((slab_high[...], slab_low[...]), spectrum).reshape(8, PLANES, HALF)
    value = None
    for layer in range(1, LAYERS):
        inv = inverse[layer]
        scaled = modes[layer] * inv
        value = scaled if value is None else scaled + (face[base + layer - 1] * inv) * value
        part[layer] = value
    weight = widen(weights[:PLANES])
    value = None
    folded[0:8] = jnp.zeros((8, HALF), jnp.float32)
    for layer in reversed(range(1, LAYERS)):
        value = part[layer] if value is None else part[layer] + (face[base + layer] * inverse[layer]) * value
        if layer == LAYERS - 1:
            out[pl.ds(1, PEERS, stride=ROWS), :] = stack_parts(face[base + layer] * value)
        weighted = weight * value
        total = (weighted[0:8] + weighted[8:16]) + (weighted[16:24] + weighted[24:32])
        folded[layer * 8 : (layer + 1) * 8] = total * cell[base + layer]
    out[pl.ds(0, PEERS, stride=ROWS), :] = stack_parts(modes[0] + face[base] * value)
    high, low = split_values(folded[...])
    sums = jnp.dot(fold[...], high, preferred_element_type=jnp.float32) + jnp.dot(fold[...], low, preferred_element_type=jnp.float32)
    planes = jnp.concatenate([modes[layer, 0:1] for layer in range(LAYERS)], axis=0)
    near = sums[:LAYERS] + planes
    far = sums[LAYERS:]
    blocks = [half[:, step * LANES : (step + 1) * LANES] for half in (near, far) for step in range(PARTS)]
    out[pl.ds(2, PEERS, stride=ROWS), :] = jnp.concatenate(blocks, axis=0).T
    out[pl.ds(3, PEERS, stride=ROWS), :] = jnp.zeros((PEERS, LANES), jnp.float32)


def solve_layers(right, inverse, face, part, use):
    upper = lower = None
    for step in range(MIDDLE):
        inv = inverse[step]
        value = right(step) * inv
        upper = value if upper is None else value + (face[step - 1] * inv) * upper
        part[step] = upper
        layer = NZ - 1 - step
        if layer > MIDDLE:
            inv = inverse[layer]
            value = right(layer) * inv
            lower = value if lower is None else value + (face[layer] * inv) * lower
            part[layer] = lower
    inv = inverse[MIDDLE]
    value = right(MIDDLE) * inv + (face[MIDDLE - 1] * inv) * upper + (face[MIDDLE] * inv) * lower
    use(MIDDLE, value)
    upper = lower = value
    for step in range(1, MIDDLE + 1):
        layer = MIDDLE - step
        upper = part[layer] + (face[layer] * inverse[layer]) * upper
        use(layer, upper)
        layer = MIDDLE + step
        if layer < NZ:
            lower = part[layer] + (face[layer - 1] * inverse[layer]) * lower
            use(layer, lower)


def keep_kernel(modes, kept, sem):
    copy = pltpu.make_async_copy(modes, kept, sem)
    copy.start()
    copy.wait()


def prepare_kernel(modes, shifts, alias_shift, mode_shift, spread, mask, tables_high, tables_low, coefficients, alias_inverse, response_high, response_low, corners, table_high, table_low, inverses, columns, scaled, held_high, held_low, sems):
    core, _, peer = position()
    copies = [
        pltpu.make_async_copy(tables_high.at[core], held_high, sems.at[0]),
        pltpu.make_async_copy(tables_low.at[core], held_low, sems.at[1]),
    ]
    for copy in copies:
        copy.start()
    cell, face, screening = columns_of(coefficients)
    lane = lax.broadcasted_iota(jnp.int32, (PARTS, LANES), 1)
    values = jnp.sum(jnp.where(lane == peer, shifts[pl.ds(core * PARTS, PARTS), :], 0.0), axis=1, keepdims=True)
    alias = alias_shift[...] + jnp.concatenate([values] * 8, axis=0)
    lane = lax.broadcasted_iota(jnp.int32, (8, LANES), 1)
    mode = jnp.broadcast_to(mode_shift[...], (8, LANES))
    for part in range(PARTS):
        mode = mode + jnp.where(lax.div(lane, PLANES) == part, values[part : part + 1], 0.0)
    shifts = jnp.concatenate([alias, mode], axis=0)
    row = lax.broadcasted_iota(jnp.int32, (8, LANES), 0)

    def diagonal(layer):
        below = face[layer - 1] if layer > 0 else face[NZ - 1]
        return (below + face[layer] + screening[layer]) + cell[layer] * shifts

    def keep_pivot(layer, inverse):
        alias_inverse[layer] = inverse[: 8 * PARTS]
        inverses[layer] = inverse[8 * PARTS :]

    upper = lower = None
    for step in range(MIDDLE):
        pivot = diagonal(step)
        if upper is not None:
            pivot = pivot - (face[step - 1] * face[step - 1]) * upper
        upper = 1.0 / pivot
        keep_pivot(step, upper)
        layer = NZ - 1 - step
        if layer > MIDDLE:
            pivot = diagonal(layer)
            if lower is not None:
                pivot = pivot - (face[layer] * face[layer]) * lower
            lower = 1.0 / pivot
            keep_pivot(layer, lower)
    pivot = diagonal(MIDDLE) - (face[MIDDLE - 1] * face[MIDDLE - 1]) * upper
    keep_pivot(MIDDLE, 1.0 / (pivot - (face[MIDDLE] * face[MIDDLE]) * lower))

    def unit(layer):
        return jnp.where(row == layer // LAYERS, 1.0, 0.0) if layer % LAYERS == 0 else jnp.zeros((8, LANES), jnp.float32)

    def keep_column(layer, value):
        scaled[layer * 8 : (layer + 1) * 8] = cell[layer] * value
        if layer % LAYERS == 0:
            corners[layer // LAYERS] = value

    solve_layers(unit, inverses, face, columns, keep_column)
    for copy in copies:
        copy.wait()
    copies = [pltpu.make_async_copy(held_high, table_high, sems.at[2]), pltpu.make_async_copy(held_low, table_low, sems.at[3])]
    for copy in copies:
        copy.start()
    weight = jnp.concatenate([mask[...]] * CHIPS, axis=1)
    for chip in range(CHIPS):
        column = scaled[pl.ds(chip, NZ, stride=8), :]
        response = dot_full(column, spread[...], ((0,), (0,))) * weight
        high, low = split_values(response)
        response_high[chip * LANES : (chip + 1) * LANES, :] = high
        response_low[chip * LANES : (chip + 1) * LANES, :] = low
    for copy in copies:
        copy.wait()


def interface_kernel(arrived, response_high, response_low, corners, alias_inverse, forward, backward, coefficients, out, source, part, solved):
    face = columns_of(coefficients)[1]

    def rows(chip, slot):
        return pl.ds(ROWS * chip + slot, SLABS, stride=ROWS * CHIPS)

    sides = []
    for chip in range(CHIPS):
        side = arrived[rows(chip, 0), :]
        sides.append(side + arrived[rows(chip - 1, 1), :] if chip > 0 else side)
    response = (response_high[...], response_low[...])
    sums = dot_stacked(jnp.concatenate(sides, axis=1), response, ((1,), (0,)))
    sums = sums + jnp.concatenate([arrived[rows(chip, 2), :] for chip in range(CHIPS)], axis=1)
    high, low = split_values(sums)
    stacked = jnp.concatenate([high, high, low], axis=0)
    turned = lax.dot_general(stacked, forward[...], (((0,), (0,)), ((), ())), preferred_element_type=jnp.float32)
    half = PARTS * LAYERS
    for chip in range(CHIPS):
        at = chip * LANES
        source[chip * half : (chip + 1) * half, :] = turned[at : at + half, :LANES] + turned[at + half : at + LANES, LANES:]

    def first_row(layer):
        return (layer // LAYERS) * half + layer % LAYERS

    def right(layer):
        row = source[pl.ds(first_row(layer), PARTS, stride=LAYERS), :]
        return jnp.concatenate([row] * 8, axis=0)

    def keep_sum(layer, value):
        total = (value[0:8] + value[8:16]) + (value[16:24] + value[24:32])
        solved[pl.ds(first_row(layer), PARTS, stride=LAYERS), :] = total[:PARTS] + total[PARTS:]

    solve_layers(right, alias_inverse, face, part, keep_sum)
    planes = dot_full(backward[...], solved[...], ((1,), (1,)))
    own = []
    for chip in range(CHIPS):
        at = chip * half
        own.append(jnp.concatenate([planes[:SLABS, at : at + half], planes[SLABS:, at : at + half]], axis=1))
    change = dot_stacked(jnp.concatenate(own, axis=1), response, ((1,), (1,)))
    ends = []
    for chip in range(CHIPS):
        end = change[:, chip * LANES : (chip + 1) * LANES]
        for other in range(CHIPS):
            end = end + corners[chip, other : other + 1, :] * sides[other]
        ends.append(end)
    nothing = jnp.zeros((SLABS, LANES), jnp.float32)
    ends.append(nothing)
    for chip in range(CHIPS):
        out[rows(chip, 0), :] = ends[chip]
        out[rows(chip, 1), :] = ends[chip + 1]
        out[rows(chip, 2), :] = own[chip]
        out[rows(chip, 3), :] = nothing


def second_solve_kernel(modes, arrived, shifts, weights, table_high, table_low, slab_high, slab_low, coefficients, kept, sent, part, near, edge, inverse):
    core, chip, _ = position()
    base = chip * LAYERS
    cell, face, _ = columns_of(coefficients, PARTS)
    chip_pivots(shifts, coefficients, inverse)
    below = unstack_parts(arrived[pl.ds(0, PEERS, stride=ROWS), :])
    above = unstack_parts(arrived[pl.ds(1, PEERS, stride=ROWS), :])
    turned = arrived[pl.ds(2, PEERS, stride=ROWS), :].T
    for which, target in enumerate((near, edge)):
        for step in range(PARTS):
            at = (which * PARTS + step) * LAYERS
            target[:, step * LANES : (step + 1) * LANES] = turned[at : at + LAYERS]
    weight = widen(weights[:PLANES])
    signed = widen(weights[PLANES:])
    keep = lax.broadcasted_iota(jnp.int32, (PLANES, HALF), 0) == 0
    value = None
    for layer in range(1, LAYERS):
        inv = inverse[layer]
        both = (near[layer : layer + 1, :] * weight + edge[layer : layer + 1, :] * signed) * cell[base + layer]
        right = modes[layer] + both
        if layer == 1:
            right = right + face[base] * below
        if layer == LAYERS - 1:
            right = right + face[base + layer] * above
        scaled = right * inv
        value = scaled if value is None else scaled + (face[base + layer - 1] * inv) * value
        part[layer] = value
    value = None
    for layer in reversed(range(1, LAYERS)):
        value = part[layer] if value is None else part[layer] + (face[base + layer] * inverse[layer]) * value
        part[layer] = jnp.where(keep, near[layer : layer + 1, :], value)
    part[0] = jnp.where(keep, near[0:1, :], below)
    kept[...] = part[pl.ds(core * 8, 8)]
    planes_into(sent, part[pl.ds((1 - core) * 8, 8)], table_high, table_low, slab_high, slab_low)


def backward_kernel(modes, table_high, table_low, slab_high, slab_low, out):
    planes_into(out, modes[...], table_high, table_low, slab_high, slab_low)


def join_kernel(kept, other, out, lines, sems):
    core, _, _ = position()
    sign = jnp.where(core == 0, 1.0, -1.0)
    copies = []
    for step in range(4):
        at = slice(2 * step, 2 * step + 2)
        one, two = kept[at], other[at]
        lines[at, :, :HALF] = one + two
        lines[at, :, HALF:] = sign * (one - two)
        copies.append(pltpu.make_async_copy(lines.at[pl.ds(2 * step, 2)], out.at[pl.ds(2 * step, 2)], sems.at[step]))
        copies[-1].start()
    for copy in copies:
        copy.wait()


held = pl.BlockSpec(memory_space=pltpu.VMEM)
far = pl.BlockSpec(memory_space=pl.ANY)
in_hbm = functools.partial(pltpu.with_memory_space_constraint, memory_space=pltpu.HBM)


def call(kernel, inputs, in_specs, outs, out_specs, scratch=(), cost=10_000_000):
    return pl.pallas_call(
        kernel,
        in_specs=in_specs,
        out_specs=out_specs,
        out_shape=outs,
        scratch_shapes=scratch,
        compiler_params=pltpu.CompilerParams(vmem_limit_bytes=VMEM_LIMIT),
        cost_estimate=pl.CostEstimate(flops=cost, bytes_accessed=4_000_000, transcendentals=0),
    )(*inputs)


def body(charge, cell, face, screening):
    forward_y, backward_y = y_tables()
    fy_high, fy_low = split_pair(forward_y)
    by_high, by_low = split_pair(backward_y)
    slab_high, slab_low = split_pair(np.kron(np.eye(8), slab_basis()))
    forward_slab, backward_slab, alias_shift = interface_tables()
    spread, mask = spread_tables()
    weights = np.concatenate([near_weights(), near_weights() * far_signs()])
    weights = np.broadcast_to(weights[:, None], (2 * PLANES, LANES)).copy()
    shift_y = y_shifts()
    mode_shift = np.tile(slab_shifts(), PARTS)[None, :]

    cube = (8, PLANES, HALF)
    field = (LAYERS, PLANES, HALF)
    message = (ROWS * PEERS, LANES)
    square = (CHIPS * LANES, CHIPS * LANES)
    table = pltpu.VMEM((HALF, HALF), jnp.bfloat16)
    far_table = pltpu.HBM((HALF, HALF), jnp.bfloat16)
    groups = [[x * 2 * CHIPS + 2 * c + r for x in range(SLABS) for c in range(CHIPS)] for r in range(2)]

    def vmem(*shape):
        return pltpu.VMEM(shape, jnp.float32)

    def exchange(values):
        blocks = values.reshape(PEERS, ROWS, LANES)
        return lax.all_to_all(blocks, ("gx", "gz"), 0, 0, axis_index_groups=groups, tiled=True).reshape(message)

    pair = [(s, s ^ 1) for s in range(2 * CHIPS)]
    lines = vmem(8, PLANES, NY)
    coefficient_rows = [in_hbm(array.reshape(1, NZ)) for array in (cell, face, screening)]
    own, sent, table_high, coefficients = call(
        split_kernel,
        (in_hbm(charge), in_hbm(fy_high), *coefficient_rows),
        [far] * 5,
        [vmem(*cube), vmem(*cube), table, vmem(3 * NZ, LANES)],
        [held] * 4,
        [lines, vmem(3, 1, NZ), pltpu.SemaphoreType.DMA((12,))],
    )
    other = lax.ppermute(sent, "gz", pair)
    shifts = np.concatenate([shift_y.reshape(2 * PARTS, LANES), np.broadcast_to(slab_shifts()[:, None], (PLANES, LANES))])
    inverse, own_modes, table_low = call(
        early_kernel,
        (own, table_high, in_hbm(fy_low), slab_high, slab_low, shifts, coefficients),
        [held] * 2 + [far] + [held] * 4,
        [vmem(*field), vmem(*cube), table],
        [held] * 3,
        [pltpu.SemaphoreType.DMA],
    )
    modes, ends = call(
        forward_kernel,
        (own_modes, other, table_high, table_low, slab_high, slab_low, inverse, weights, fold_table(), coefficients),
        [held] * 10,
        [vmem(*field), pltpu.HBM(message, jnp.float32)],
        [held] * 2,
        [vmem(*field), vmem(8 * LAYERS, HALF)],
    )
    modes = call(keep_kernel, (modes,), [held], pltpu.HBM(field, jnp.float32), far, [pltpu.SemaphoreType.DMA])
    alias_inverse, response_high, response_low, corners, table_high, table_low = call(
        prepare_kernel,
        (in_hbm(modes), shifts, alias_shift, mode_shift, spread, mask, in_hbm(by_high), in_hbm(by_low), coefficients),
        [far] + [held] * 5 + [far] * 2 + [held],
        [vmem(NZ, 8 * PARTS, LANES), pltpu.VMEM(square, jnp.bfloat16), pltpu.VMEM(square, jnp.bfloat16), vmem(CHIPS, 8, LANES)]
        + [far_table, far_table],
        [held] * 4 + [far] * 2,
        [vmem(NZ, 8, LANES), vmem(NZ, 8, LANES), vmem(8 * NZ, LANES), table, table, pltpu.SemaphoreType.DMA((4,))],
    )
    ends = exchange(ends)
    ends = call(
        interface_kernel,
        (ends, response_high, response_low, corners, alias_inverse, forward_slab, backward_slab, coefficients),
        [held] * 8,
        vmem(*message),
        held,
        [vmem(CHIPS * PARTS * LAYERS, LANES), vmem(NZ, 8 * PARTS, LANES), vmem(CHIPS * PARTS * LAYERS, LANES)],
    )
    ends = exchange(ends)
    kept, sent = call(
        second_solve_kernel,
        (modes, ends, shifts, weights, table_high, table_low, slab_high, slab_low, coefficients),
        [held] * 9,
        [vmem(*cube), vmem(*cube)],
        [held] * 2,
        [vmem(*field), vmem(LAYERS, HALF), vmem(LAYERS, HALF), vmem(*field)],
    )
    other = lax.ppermute(sent, "gz", pair)
    kept = call(backward_kernel, (kept, table_high, table_low, slab_high, slab_low), [held] * 5, vmem(*cube), held)
    return call(
        join_kernel, (kept, other), [held] * 2, pltpu.HBM((8, PLANES, NY), jnp.float32), far, [lines, pltpu.SemaphoreType.DMA((4,))]
    )


def solution(mesh):
    in_specs = (P("gz", "gx", None), P(), P(), P())
    out_specs = P("gz", "gx", None)
    return jax.shard_map(body, mesh=mesh, in_specs=in_specs, out_specs=out_specs, check_vma=False)
```

```python
import functools
import math

import jax
import jax.numpy as jnp
import ml_dtypes
import numpy as np
from jax import lax
from jax.experimental import pallas as pl
from jax.experimental.pallas import tpu as pltpu
from jax.sharding import PartitionSpec as P

NX, NY, NZ = 1024, 1024, 64
SLABS, PLANES = 32, 32
HALF = NY // 2
CHIPS = 4
LAYERS = NZ // CHIPS
MIDDLE = NZ // 2
PEERS = SLABS * CHIPS
PARTS = 4
ROWS = 4
LANES = 128
highest = lax.Precision.HIGHEST
VMEM_LIMIT = 48 * 1024 * 1024


def split_pair(table):
    high = table.astype(np.float32).astype(ml_dtypes.bfloat16)
    low = (table - high.astype(np.float64)).astype(np.float32).astype(ml_dtypes.bfloat16)
    return high, low


def y_frequencies():
    index = np.arange(HALF // 2)
    quarter = HALF // 4
    even = np.concatenate([4 * np.where(index <= quarter, index, index - quarter), 4 * (index % quarter) + 2])
    even_is_cos = np.concatenate([index <= quarter, index < quarter])
    index = np.arange(HALF)
    odd = 2 * (index % (HALF // 2)) + 1
    return np.stack([even, odd]), np.stack([even_is_cos, index < HALF // 2])


def y_tables():
    freq, is_cos = y_frequencies()
    point = np.arange(HALF)
    angle = 2.0 * np.pi * (point[None, :, None] * freq[:, None, :] % NY) / NY
    forward = np.where(is_cos[:, None, :], np.cos(angle), np.sin(angle))
    weight = np.where((freq == 0) | (freq == NY // 2), 1.0 / NY, 2.0 / NY)
    backward = np.swapaxes(forward * weight[:, None, :], 1, 2)
    return forward, backward


def y_shifts():
    freq, _ = y_frequencies()
    return (4.0 * np.sin(np.pi * freq / NY) ** 2).astype(np.float32)


def slab_basis():
    index = np.arange(PLANES)
    basis = math.sqrt(2.0 / PLANES) * np.sin(np.pi * np.outer(index, index) / PLANES)
    basis[0, :] = 0.0
    basis[:, 0] = 0.0
    basis[0, 0] = 1.0
    return basis


def slab_shifts():
    return (4.0 * np.sin(np.pi * np.arange(PLANES) / (2 * PLANES)) ** 2).astype(np.float32)


def near_weights():
    weight = slab_basis()[1].copy()
    weight[0] = 0.0
    return weight.astype(np.float32)


def far_signs():
    return np.where(np.arange(PLANES) % 2 == 1, 1.0, -1.0).astype(np.float32)


def interface_tables():
    mode = np.arange(SLABS)
    freq = np.where(mode <= SLABS // 2, mode, mode - SLABS // 2)
    is_cos = mode <= SLABS // 2
    weight = np.where((freq == 0) | (freq == SLABS // 2), 1.0, 2.0) / SLABS / SLABS

    def basis(offset):
        angle = 2.0 * np.pi * ((np.arange(SLABS)[:, None] + offset) * freq[None, :] % SLABS) / SLABS
        return np.where(is_cos[None, :], np.cos(angle), np.sin(angle))

    forward = np.concatenate([np.tile(basis(0), (1, 4)), np.tile(basis(1), (1, 4))], axis=1)
    high, low = split_pair(forward)
    backward = np.concatenate([np.tile(basis(0) * weight, (1, 4)), np.tile(basis(1) * weight, (1, 4))], axis=0)
    alias = freq[None, None, :] + SLABS * (np.arange(8)[:, None, None] + 8 * np.arange(4)[None, :, None])
    alias = np.repeat(alias, PARTS, axis=0)
    alias_shift = 4.0 * np.sin(np.pi * alias / NX) ** 2
    return (
        np.concatenate([high, low, high], axis=0),
        backward.astype(np.float32),
        alias_shift.reshape(8 * PARTS, LANES).astype(np.float32),
    )


def fold_table():
    fold = np.zeros((2, LAYERS, LAYERS, 8), np.float32)
    for layer in range(LAYERS):
        fold[0, layer, layer, :] = 1.0
        fold[1, layer, layer, :] = far_signs()[:8]
    return fold.reshape(2 * LAYERS, 8 * LAYERS).astype(ml_dtypes.bfloat16)


def spread_tables():
    spread = np.zeros((CHIPS, LAYERS, CHIPS, 2, PARTS, LAYERS), np.float32)
    for chip in range(CHIPS):
        for layer in range(LAYERS):
            spread[chip, layer, chip, :, :, layer] = 1.0
    mask = np.zeros((PARTS, PLANES, 2, PARTS, LAYERS), np.float32)
    for part in range(PARTS):
        mask[part, :, 0, part, :] = near_weights()[:, None]
        mask[part, :, 1, part, :] = (near_weights() * far_signs())[:, None]
    return spread.reshape(NZ, CHIPS * LANES), mask.reshape(LANES, LANES)


def position():
    gz = lax.axis_index("gz")
    core, chip = lax.rem(gz, 2), lax.div(gz, 2)
    return core, chip, lax.axis_index("gx") * CHIPS + chip


class Column:
    def __init__(self, ref, which, repeat):
        self.ref, self.start, self.repeat = ref, which * NZ, repeat

    def __getitem__(self, layer):
        row = self.ref[pl.ds(self.start + layer, 1), :]
        return jnp.concatenate([row] * self.repeat, axis=1)


def columns_of(ref, repeat=1):
    return [Column(ref, which, repeat) for which in range(3)]


def split_values(values):
    high = values.astype(jnp.bfloat16)
    low = (values - high.astype(jnp.float32)).astype(jnp.bfloat16)
    return high, low


def dot_split(left, right, contract=((1,), (0,))):
    left_high, left_low = left
    right_high, right_low = right

    def dot(one, two):
        return lax.dot_general(one, two, (contract, ((), ())), preferred_element_type=jnp.float32)

    return dot(left_high, right_high) + (dot(left_high, right_low) + dot(left_low, right_high))


def dot_stacked(left, right, contract):
    high, low = split_values(left)
    rows = left.shape[0]

    def dot(one, two):
        return lax.dot_general(one, two, (contract, ((), ())), preferred_element_type=jnp.float32)

    both = dot(jnp.concatenate([high, low], axis=0), right[0])
    return both[:rows] + (both[rows:] + dot(high, right[1]))


def dot_full(left, right, contract):
    return lax.dot_general(
        left, right, (contract, ((), ())), precision=highest, preferred_element_type=jnp.float32
    )


def split_kernel(charge, tables_high, tables_low, cell, face, screening, own, sent, table_high, table_low, coefficients, lines, rows, sems):
    core, _, _ = position()
    copies = [pltpu.make_async_copy(source, rows.at[step], sems.at[10 + step]) for step, source in enumerate((cell, face, screening))]
    copies += [pltpu.make_async_copy(charge.at[step], lines.at[step], sems.at[step]) for step in range(8)]
    copies.append(pltpu.make_async_copy(tables_high.at[core], table_high, sems.at[8]))
    copies.append(pltpu.make_async_copy(tables_low.at[core], table_low, sems.at[9]))
    for copy in copies:
        copy.start()
    for step, copy in enumerate(copies[:3]):
        copy.wait()
        coefficients[step * NZ : (step + 1) * NZ, :] = jnp.broadcast_to(rows[step], (LANES, NZ)).T
    sign = jnp.where(core == 0, 1.0, -1.0)
    for step, copy in enumerate(copies[3:11]):
        copy.wait()
        lower, upper = lines[step, :, :HALF], sign * lines[step, :, HALF:]
        own[step] = lower + upper
        sent[step] = lower - upper
    for copy in copies[11:]:
        copy.wait()


def widen(table):
    return jnp.concatenate([table] * PARTS, axis=1)


def chip_pivots(shifts, coefficients, inverse):
    cell, face, screening = columns_of(coefficients, PARTS)
    core, chip, _ = position()
    base = chip * LAYERS
    row = jnp.concatenate([shifts[pl.ds(core * PARTS + part, 1), :] for part in range(PARTS)], axis=1)
    shifts = widen(shifts[8:]) + row
    previous = None
    for layer in range(1, LAYERS):
        below, above = face[base + layer - 1], face[base + layer]
        pivot = (below + above + screening[base + layer]) + cell[base + layer] * shifts
        if previous is not None:
            pivot = pivot - (below * below) * previous
        previous = 1.0 / pivot
        inverse[layer] = previous


def early_kernel(own, table_high, table_low, slab_high, slab_low, shifts, coefficients, inverse, modes):
    chip_pivots(shifts, coefficients, inverse)
    modes[...] = to_modes(own, table_high, table_low, slab_high, slab_low)


def to_modes(planes, table_high, table_low, slab_high, slab_low):
    values = planes[...].reshape(8 * PLANES, HALF)
    spectrum = dot_split(split_values(values), (table_high[...], table_low[...]))
    return dot_split((slab_high[...], slab_low[...]), split_values(spectrum)).reshape(8, PLANES, HALF)


def spectrum_into(out, planes, table_high, table_low):
    core, _, _ = position()
    values = planes[...].reshape(8 * PLANES, HALF)
    half = HALF // 2

    @pl.when(core == 0)
    def _():
        for at, sign in ((0, 1.0), (half, -1.0)):
            mixed = values[:, :half] + sign * values[:, half:]
            table = (table_high[:half, at : at + half], table_low[:half, at : at + half])
            out[:, :, at : at + half] = dot_split(split_values(mixed), table).reshape(8, PLANES, half)

    @pl.when(core != 0)
    def _():
        out[...] = dot_split(split_values(values), (table_high[...], table_low[...])).reshape(8, PLANES, HALF)


def planes_into(out, modes, table_high, table_low, slab_high, slab_low):
    core, _, _ = position()
    values = dot_split((slab_high[...], slab_low[...]), split_values(modes.reshape(8 * PLANES, HALF)))
    half = HALF // 2

    @pl.when(core == 0)
    def _():
        one, two = [
            dot_split(split_values(values[:, at : at + half]), (table_high[at : at + half, :half], table_low[at : at + half, :half]))
            for at in (0, half)
        ]
        out[:, :, :half] = (one + two).reshape(8, PLANES, half)
        out[:, :, half:] = (one - two).reshape(8, PLANES, half)

    @pl.when(core != 0)
    def _():
        out[...] = dot_split(split_values(values), (table_high[...], table_low[...])).reshape(8, PLANES, HALF)


def stack_parts(values):
    return jnp.concatenate([values[:, part * LANES : (part + 1) * LANES] for part in range(PARTS)], axis=0).T


def unstack_parts(values):
    turned = values.T
    return jnp.concatenate([turned[part * PLANES : (part + 1) * PLANES] for part in range(PARTS)], axis=1)


def forward_kernel(own_modes, other, table_high, table_low, slab_high, slab_low, inverse, weights, fold, coefficients, modes, out, part, folded):
    core, chip, _ = position()
    base = chip * LAYERS
    cell, face, _ = columns_of(coefficients, PARTS)
    modes[pl.ds(core * 8, 8)] = own_modes[...]
    spectrum_into(part.at[pl.ds(0, 8)], other, table_high, table_low)
    spectrum = split_values(part[0:8].reshape(8 * PLANES, HALF))
    modes[pl.ds((1 - core) * 8, 8)] = dot_split((slab_high[...], slab_low[...]), spectrum).reshape(8, PLANES, HALF)
    value = None
    for layer in range(1, LAYERS):
        inv = inverse[layer]
        scaled = modes[layer] * inv
        value = scaled if value is None else scaled + (face[base + layer - 1] * inv) * value
        part[layer] = value
    weight = widen(weights[:PLANES])
    value = None
    folded[0:8] = jnp.zeros((8, HALF), jnp.float32)
    for layer in reversed(range(1, LAYERS)):
        value = part[layer] if value is None else part[layer] + (face[base + layer] * inverse[layer]) * value
        if layer == LAYERS - 1:
            out[pl.ds(1, PEERS, stride=ROWS), :] = stack_parts(face[base + layer] * value)
        weighted = weight * value
        total = (weighted[0:8] + weighted[8:16]) + (weighted[16:24] + weighted[24:32])
        folded[layer * 8 : (layer + 1) * 8] = total * cell[base + layer]
    out[pl.ds(0, PEERS, stride=ROWS), :] = stack_parts(modes[0] + face[base] * value)
    high, low = split_values(folded[...])
    sums = jnp.dot(fold[...], high, preferred_element_type=jnp.float32) + jnp.dot(fold[...], low, preferred_element_type=jnp.float32)
    planes = jnp.concatenate([modes[layer, 0:1] for layer in range(LAYERS)], axis=0)
    near = sums[:LAYERS] + planes
    far = sums[LAYERS:]
    blocks = [half[:, step * LANES : (step + 1) * LANES] for half in (near, far) for step in range(PARTS)]
    out[pl.ds(2, PEERS, stride=ROWS), :] = jnp.concatenate(blocks, axis=0).T
    out[pl.ds(3, PEERS, stride=ROWS), :] = jnp.zeros((PEERS, LANES), jnp.float32)


def solve_layers(right, inverse, face, part, use):
    upper = lower = None
    for step in range(MIDDLE):
        inv = inverse[step]
        value = right(step) * inv
        upper = value if upper is None else value + (face[step - 1] * inv) * upper
        part[step] = upper
        layer = NZ - 1 - step
        if layer > MIDDLE:
            inv = inverse[layer]
            value = right(layer) * inv
            lower = value if lower is None else value + (face[layer] * inv) * lower
            part[layer] = lower
    inv = inverse[MIDDLE]
    value = right(MIDDLE) * inv + (face[MIDDLE - 1] * inv) * upper + (face[MIDDLE] * inv) * lower
    use(MIDDLE, value)
    upper = lower = value
    for step in range(1, MIDDLE + 1):
        layer = MIDDLE - step
        upper = part[layer] + (face[layer] * inverse[layer]) * upper
        use(layer, upper)
        layer = MIDDLE + step
        if layer < NZ:
            lower = part[layer] + (face[layer - 1] * inverse[layer]) * lower
            use(layer, lower)


def keep_kernel(modes, kept, sem):
    copy = pltpu.make_async_copy(modes, kept, sem)
    copy.start()
    copy.wait()


def prepare_kernel(modes, shifts, alias_shift, mode_shift, spread, mask, tables_high, tables_low, coefficients, alias_inverse, response_high, response_low, corners, table_high, table_low, inverses, columns, scaled, held_high, held_low, sems):
    core, _, peer = position()
    copies = [
        pltpu.make_async_copy(tables_high.at[core], held_high, sems.at[0]),
        pltpu.make_async_copy(tables_low.at[core], held_low, sems.at[1]),
    ]
    for copy in copies:
        copy.start()
    cell, face, screening = columns_of(coefficients)
    lane = lax.broadcasted_iota(jnp.int32, (PARTS, LANES), 1)
    values = jnp.sum(jnp.where(lane == peer, shifts[pl.ds(core * PARTS, PARTS), :], 0.0), axis=1, keepdims=True)
    alias = alias_shift[...] + jnp.concatenate([values] * 8, axis=0)
    lane = lax.broadcasted_iota(jnp.int32, (8, LANES), 1)
    mode = jnp.broadcast_to(mode_shift[...], (8, LANES))
    for part in range(PARTS):
        mode = mode + jnp.where(lax.div(lane, PLANES) == part, values[part : part + 1], 0.0)
    shifts = jnp.concatenate([alias, mode], axis=0)
    row = lax.broadcasted_iota(jnp.int32, (8, LANES), 0)

    def diagonal(layer):
        below = face[layer - 1] if layer > 0 else face[NZ - 1]
        return (below + face[layer] + screening[layer]) + cell[layer] * shifts

    def keep_pivot(layer, inverse):
        alias_inverse[layer] = inverse[: 8 * PARTS]
        inverses[layer] = inverse[8 * PARTS :]

    upper = lower = None
    for step in range(MIDDLE):
        pivot = diagonal(step)
        if upper is not None:
            pivot = pivot - (face[step - 1] * face[step - 1]) * upper
        upper = 1.0 / pivot
        keep_pivot(step, upper)
        layer = NZ - 1 - step
        if layer > MIDDLE:
            pivot = diagonal(layer)
            if lower is not None:
                pivot = pivot - (face[layer] * face[layer]) * lower
            lower = 1.0 / pivot
            keep_pivot(layer, lower)
    pivot = diagonal(MIDDLE) - (face[MIDDLE - 1] * face[MIDDLE - 1]) * upper
    keep_pivot(MIDDLE, 1.0 / (pivot - (face[MIDDLE] * face[MIDDLE]) * lower))

    def unit(layer):
        return jnp.where(row == layer // LAYERS, 1.0, 0.0) if layer % LAYERS == 0 else jnp.zeros((8, LANES), jnp.float32)

    def keep_column(layer, value):
        scaled[layer * 8 : (layer + 1) * 8] = cell[layer] * value
        if layer % LAYERS == 0:
            corners[layer // LAYERS] = value

    solve_layers(unit, inverses, face, columns, keep_column)
    for copy in copies:
        copy.wait()
    copies = [pltpu.make_async_copy(held_high, table_high, sems.at[2]), pltpu.make_async_copy(held_low, table_low, sems.at[3])]
    for copy in copies:
        copy.start()
    weight = jnp.concatenate([mask[...]] * CHIPS, axis=1)
    for chip in range(CHIPS):
        column = scaled[pl.ds(chip, NZ, stride=8), :]
        response = dot_full(column, spread[...], ((0,), (0,))) * weight
        high, low = split_values(response)
        response_high[chip * LANES : (chip + 1) * LANES, :] = high
        response_low[chip * LANES : (chip + 1) * LANES, :] = low
    for copy in copies:
        copy.wait()


def interface_kernel(arrived, response_high, response_low, corners, alias_inverse, forward, backward, coefficients, out, source, part, solved):
    face = columns_of(coefficients)[1]

    def rows(chip, slot):
        return pl.ds(ROWS * chip + slot, SLABS, stride=ROWS * CHIPS)

    sides = []
    for chip in range(CHIPS):
        side = arrived[rows(chip, 0), :]
        sides.append(side + arrived[rows(chip - 1, 1), :] if chip > 0 else side)
    response = (response_high[...], response_low[...])
    sums = dot_stacked(jnp.concatenate(sides, axis=1), response, ((1,), (0,)))
    sums = sums + jnp.concatenate([arrived[rows(chip, 2), :] for chip in range(CHIPS)], axis=1)
    high, low = split_values(sums)
    stacked = jnp.concatenate([high, high, low], axis=0)
    turned = lax.dot_general(stacked, forward[...], (((0,), (0,)), ((), ())), preferred_element_type=jnp.float32)
    half = PARTS * LAYERS
    for chip in range(CHIPS):
        at = chip * LANES
        source[chip * half : (chip + 1) * half, :] = turned[at : at + half, :LANES] + turned[at + half : at + LANES, LANES:]

    def first_row(layer):
        return (layer // LAYERS) * half + layer % LAYERS

    def right(layer):
        row = source[pl.ds(first_row(layer), PARTS, stride=LAYERS), :]
        return jnp.concatenate([row] * 8, axis=0)

    def keep_sum(layer, value):
        total = (value[0:8] + value[8:16]) + (value[16:24] + value[24:32])
        solved[pl.ds(first_row(layer), PARTS, stride=LAYERS), :] = total[:PARTS] + total[PARTS:]

    solve_layers(right, alias_inverse, face, part, keep_sum)
    planes = dot_full(backward[...], solved[...], ((1,), (1,)))
    own = []
    for chip in range(CHIPS):
        at = chip * half
        own.append(jnp.concatenate([planes[:SLABS, at : at + half], planes[SLABS:, at : at + half]], axis=1))
    change = dot_stacked(jnp.concatenate(own, axis=1), response, ((1,), (1,)))
    ends = []
    for chip in range(CHIPS):
        end = change[:, chip * LANES : (chip + 1) * LANES]
        for other in range(CHIPS):
            end = end + corners[chip, other : other + 1, :] * sides[other]
        ends.append(end)
    nothing = jnp.zeros((SLABS, LANES), jnp.float32)
    ends.append(nothing)
    for chip in range(CHIPS):
        out[rows(chip, 0), :] = ends[chip]
        out[rows(chip, 1), :] = ends[chip + 1]
        out[rows(chip, 2), :] = own[chip]
        out[rows(chip, 3), :] = nothing


def second_solve_kernel(modes, arrived, shifts, weights, table_high, table_low, slab_high, slab_low, coefficients, kept, sent, part, near, edge, inverse):
    core, chip, _ = position()
    base = chip * LAYERS
    cell, face, _ = columns_of(coefficients, PARTS)
    chip_pivots(shifts, coefficients, inverse)
    below = unstack_parts(arrived[pl.ds(0, PEERS, stride=ROWS), :])
    above = unstack_parts(arrived[pl.ds(1, PEERS, stride=ROWS), :])
    turned = arrived[pl.ds(2, PEERS, stride=ROWS), :].T
    for which, target in enumerate((near, edge)):
        for step in range(PARTS):
            at = (which * PARTS + step) * LAYERS
            target[:, step * LANES : (step + 1) * LANES] = turned[at : at + LAYERS]
    weight = widen(weights[:PLANES])
    signed = widen(weights[PLANES:])
    keep = lax.broadcasted_iota(jnp.int32, (PLANES, HALF), 0) == 0
    value = None
    for layer in range(1, LAYERS):
        inv = inverse[layer]
        both = (near[layer : layer + 1, :] * weight + edge[layer : layer + 1, :] * signed) * cell[base + layer]
        right = modes[layer] + both
        if layer == 1:
            right = right + face[base] * below
        if layer == LAYERS - 1:
            right = right + face[base + layer] * above
        scaled = right * inv
        value = scaled if value is None else scaled + (face[base + layer - 1] * inv) * value
        part[layer] = value
    value = None
    for layer in reversed(range(1, LAYERS)):
        value = part[layer] if value is None else part[layer] + (face[base + layer] * inverse[layer]) * value
        part[layer] = jnp.where(keep, near[layer : layer + 1, :], value)
    part[0] = jnp.where(keep, near[0:1, :], below)
    kept[...] = part[pl.ds(core * 8, 8)]
    planes_into(sent, part[pl.ds((1 - core) * 8, 8)], table_high, table_low, slab_high, slab_low)


def backward_kernel(modes, table_high, table_low, slab_high, slab_low, out):
    planes_into(out, modes[...], table_high, table_low, slab_high, slab_low)


def join_kernel(kept, other, out, lines, sems):
    core, _, _ = position()
    sign = jnp.where(core == 0, 1.0, -1.0)
    copies = []
    for step in range(4):
        at = slice(2 * step, 2 * step + 2)
        one, two = kept[at], other[at]
        lines[at, :, :HALF] = one + two
        lines[at, :, HALF:] = sign * (one - two)
        copies.append(pltpu.make_async_copy(lines.at[pl.ds(2 * step, 2)], out.at[pl.ds(2 * step, 2)], sems.at[step]))
        copies[-1].start()
    for copy in copies:
        copy.wait()


held = pl.BlockSpec(memory_space=pltpu.VMEM)
far = pl.BlockSpec(memory_space=pl.ANY)
in_hbm = functools.partial(pltpu.with_memory_space_constraint, memory_space=pltpu.HBM)


def call(kernel, inputs, in_specs, outs, out_specs, scratch=(), cost=10_000_000):
    return pl.pallas_call(
        kernel,
        in_specs=in_specs,
        out_specs=out_specs,
        out_shape=outs,
        scratch_shapes=scratch,
        compiler_params=pltpu.CompilerParams(vmem_limit_bytes=VMEM_LIMIT),
        cost_estimate=pl.CostEstimate(flops=cost, bytes_accessed=4_000_000, transcendentals=0),
    )(*inputs)


def body(charge, cell, face, screening):
    forward_y, backward_y = y_tables()
    fy_high, fy_low = split_pair(forward_y)
    by_high, by_low = split_pair(backward_y)
    slab_high, slab_low = split_pair(np.kron(np.eye(8), slab_basis()))
    forward_slab, backward_slab, alias_shift = interface_tables()
    spread, mask = spread_tables()
    weights = np.concatenate([near_weights(), near_weights() * far_signs()])
    weights = np.broadcast_to(weights[:, None], (2 * PLANES, LANES)).copy()
    shift_y = y_shifts()
    mode_shift = np.tile(slab_shifts(), PARTS)[None, :]

    cube = (8, PLANES, HALF)
    field = (LAYERS, PLANES, HALF)
    message = (ROWS * PEERS, LANES)
    square = (CHIPS * LANES, CHIPS * LANES)
    table = pltpu.VMEM((HALF, HALF), jnp.bfloat16)
    far_table = pltpu.HBM((HALF, HALF), jnp.bfloat16)
    groups = [[x * 2 * CHIPS + 2 * c + r for x in range(SLABS) for c in range(CHIPS)] for r in range(2)]

    def vmem(*shape):
        return pltpu.VMEM(shape, jnp.float32)

    def exchange(values):
        blocks = values.reshape(PEERS, ROWS, LANES)
        return lax.all_to_all(blocks, ("gx", "gz"), 0, 0, axis_index_groups=groups, tiled=True).reshape(message)

    pair = [(s, s ^ 1) for s in range(2 * CHIPS)]
    lines = vmem(8, PLANES, NY)
    coefficient_rows = [in_hbm(array.reshape(1, NZ)) for array in (cell, face, screening)]
    own, sent, table_high, table_low, coefficients = call(
        split_kernel,
        (in_hbm(charge), in_hbm(fy_high), in_hbm(fy_low), *coefficient_rows),
        [far] * 6,
        [vmem(*cube), vmem(*cube), table, table, vmem(3 * NZ, LANES)],
        [held] * 5,
        [lines, vmem(3, 1, NZ), pltpu.SemaphoreType.DMA((13,))],
    )
    other = lax.ppermute(sent, "gz", pair)
    shifts = np.concatenate([shift_y.reshape(2 * PARTS, LANES), np.broadcast_to(slab_shifts()[:, None], (PLANES, LANES))])
    inverse, own_modes = call(
        early_kernel,
        (own, table_high, table_low, slab_high, slab_low, shifts, coefficients),
        [held] * 7,
        [vmem(*field), vmem(*cube)],
        [held] * 2,
    )
    modes, ends = call(
        forward_kernel,
        (own_modes, other, table_high, table_low, slab_high, slab_low, inverse, weights, fold_table(), coefficients),
        [held] * 10,
        [vmem(*field), pltpu.HBM(message, jnp.float32)],
        [held] * 2,
        [vmem(*field), vmem(8 * LAYERS, HALF)],
    )
    modes = call(keep_kernel, (modes,), [held], pltpu.HBM(field, jnp.float32), far, [pltpu.SemaphoreType.DMA])
    alias_inverse, response_high, response_low, corners, table_high, table_low = call(
        prepare_kernel,
        (in_hbm(modes), shifts, alias_shift, mode_shift, spread, mask, in_hbm(by_high), in_hbm(by_low), coefficients),
        [far] + [held] * 5 + [far] * 2 + [held],
        [vmem(NZ, 8 * PARTS, LANES), pltpu.VMEM(square, jnp.bfloat16), pltpu.VMEM(square, jnp.bfloat16), vmem(CHIPS, 8, LANES)]
        + [far_table, far_table],
        [held] * 4 + [far] * 2,
        [vmem(NZ, 8, LANES), vmem(NZ, 8, LANES), vmem(8 * NZ, LANES), table, table, pltpu.SemaphoreType.DMA((4,))],
    )
    ends = exchange(ends)
    ends = call(
        interface_kernel,
        (ends, response_high, response_low, corners, alias_inverse, forward_slab, backward_slab, coefficients),
        [held] * 8,
        vmem(*message),
        held,
        [vmem(CHIPS * PARTS * LAYERS, LANES), vmem(NZ, 8 * PARTS, LANES), vmem(CHIPS * PARTS * LAYERS, LANES)],
    )
    ends = exchange(ends)
    kept, sent = call(
        second_solve_kernel,
        (modes, ends, shifts, weights, table_high, table_low, slab_high, slab_low, coefficients),
        [held] * 9,
        [vmem(*cube), vmem(*cube)],
        [held] * 2,
        [vmem(*field), vmem(LAYERS, HALF), vmem(LAYERS, HALF), vmem(*field)],
    )
    other = lax.ppermute(sent, "gz", pair)
    kept = call(backward_kernel, (kept, table_high, table_low, slab_high, slab_low), [held] * 5, vmem(*cube), held)
    return call(
        join_kernel, (kept, other), [held] * 2, pltpu.HBM((8, PLANES, NY), jnp.float32), far, [lines, pltpu.SemaphoreType.DMA((4,))]
    )


def solution(mesh):
    in_specs = (P("gz", "gx", None), P(), P(), P())
    out_specs = P("gz", "gx", None)
    return jax.shard_map(body, mesh=mesh, in_specs=in_specs, out_specs=out_specs, check_vma=False)
```
